32 devices in a mesh: groups: 1, samp: 4 (over x, core), var: 8 (over z, y).
Axes of the slice: x: 2, y: 2, z: 4, core: 2. Of those that a mesh axis runs over, the one named last changes fastest.
Arguments:
- expression: bfloat16 [4096, 5120], P(('groups', 'samp'), 'var'), may hold values from -6 to 6
- genotypes: bfloat16 [4096, 1536], P(('groups', 'samp'), 'var'), may hold values from 0 to 2
- covariates: bfloat16 [4096, 64], P(('groups', 'samp')), may hold values from -6 to 6
- distance_bins: int32 [24, 5120], P('groups', ('var', 'samp')), may hold values from 0 to 15
- gene_folds: int32 [5120], P(('groups', 'var', 'samp')), may hold values from 0 to 4
- fold_weights: float32 [5, 16], replicated, may hold values from 0.25 to 4
Outputs:
- weighted_stats: float32 [5120, 1536], P(('groups', 'var', 'samp'))
The draws below stay inside these ranges and needn't reach their ends.
Inputs may be any that keep to these rules, and one draw needn't show every extreme that they name: `distance_bins`: bins index rows of fold_weights' second dimension. `gene_folds`: folds index rows of fold_weights.
All inputs are finite; a program needn't handle non-finite values.
Results may differ from the reference program's by a relative error of at most 0.0047.
Values may be sent and summed in bfloat16 or wider, within the bound.
No kernel may reach another device: no remote copies, remote signals or barrier semaphores. Data moves between devices by JAX's collectives and lax.ppermute only.
A program may use at most 64 MiB of HBM per device.

```python
import math
import jax
import jax.numpy as jnp
from jax import lax

COVS = 64
VARS = 1536
VTILE = 64
NBINS = 16
FOLDS = 5
SAMPLES = 4096
GENES = 5120
VTILES = 24


def set_ends(values, rng, low, largest):
    dims = values.shape
    spot = [jax.random.randint(jax.random.fold_in(rng, axis), (), 0, dims[axis]) for axis in range(len(dims))]
    values = values.at[tuple(spot)].set(low)
    longest = dims.index(max(dims))
    spot[longest] = (spot[longest] + 1) % dims[longest]
    return values.at[tuple(spot)].set(largest)


def block_scale(own_key, extent, split, low, top_value):
    def one(position, blocks):
        steps = jax.random.uniform(jax.random.fold_in(jax.random.fold_in(own_key, 6), position), (blocks,), jnp.float32, low / len(split), top_value / len(split))
        return jnp.repeat(jnp.exp(steps), extent[position] // blocks).reshape((-1,) + (1,) * (len(extent) - position - 1))

    level = one(*split[0])
    for cut in split[1:]:
        level = level * one(*cut)
    return level


def bell_draw(rng, dims, spread, limit, pieces=(), dtype=jnp.bfloat16):
    drawn = spread * jax.random.normal(rng, dims, jnp.float32)
    if pieces:
        drawn = drawn * block_scale(rng, dims, pieces, -0.22, 0.18)
    return jnp.clip(drawn, -limit, limit).astype(dtype)


def setup_inputs(seed: int = 0, part: int = 0) -> dict:
    streams_of = jax.random.split(jax.random.key(seed), 7)
    part_splits = jax.random.split(jax.random.fold_in(streams_of[6], part), 7)
    expression = bell_draw(part_splits[0], (SAMPLES, GENES), 1.0, 6.0, ((0, 4), (1, 8)))
    genotypes = jnp.clip(2.0 * jax.random.uniform(part_splits[1], (SAMPLES, VARS), jnp.float32) ** block_scale(part_splits[1], (SAMPLES, VARS), ((0, 4), (1, 8)), -0.2, 0.2), 0.0, 2.0).astype(jnp.bfloat16)
    covariates = bell_draw(part_splits[2], (SAMPLES, COVS), 1.0, 6.0, ((0, 4),))
    distance_bins = set_ends(jax.random.randint(part_splits[3], (VTILES, GENES), 0, NBINS), jax.random.fold_in(part_splits[3], 1), 0, NBINS - 1).astype(jnp.int32)
    gene_folds = set_ends(jax.random.randint(part_splits[4], (GENES,), 0, FOLDS), jax.random.fold_in(part_splits[4], 1), 0, FOLDS - 1).astype(jnp.int32)
    fold_weights = jnp.clip(jnp.exp(jax.random.uniform(streams_of[5], (FOLDS, NBINS), jnp.float32, math.log(0.25), math.log(4.0))), 0.25, 4.0)
    return dict(expression=expression, genotypes=genotypes, covariates=covariates, distance_bins=distance_bins, gene_folds=gene_folds, fold_weights=fold_weights)


def standardize(data, design, gram):
    cross = jnp.dot(design.T.astype(jnp.float32), data.astype(jnp.float32), preferred_element_type=jnp.float32)
    beta = jnp.linalg.solve(gram, cross)
    fitted = jnp.dot(design.astype(jnp.float32), beta, precision=lax.Precision.HIGHEST)
    residual = data.astype(jnp.float32) - fitted
    norm = lax.optimization_barrier(jnp.sum(residual * residual, axis=0))
    return (residual * lax.rsqrt(norm + 1e-06)).astype(jnp.bfloat16)

def reference(expression, genotypes, covariates, distance_bins, gene_folds, fold_weights):
    samples = expression.shape[0]
    design = jnp.concatenate([jnp.ones((samples, 1), jnp.bfloat16), covariates], axis=1)
    gram = jnp.dot(design.T.astype(jnp.float32), design.astype(jnp.float32), preferred_element_type=jnp.float32)
    expr_unit = standardize(expression, design, gram)
    geno_unit = standardize(genotypes, design, gram)
    corr = jnp.dot(expr_unit.T.astype(jnp.float32), geno_unit.astype(jnp.float32), preferred_element_type=jnp.float32)
    row_weights = fold_weights[gene_folds]
    tile_weight = jnp.take_along_axis(row_weights, distance_bins.T, axis=1)
    dof = jnp.float32(samples - COVS - 2)
    stats = dof * corr * corr
    genes = corr.shape[0]
    weighted = stats.reshape(genes, VTILES, VTILE) * tile_weight[:, :, None]
    return weighted.reshape(genes, VARS)
```

```python
import functools
import math

import jax
import jax.numpy as jnp
from jax import lax
from jax.experimental import pallas as pl
from jax.experimental.pallas import tpu as pltpu
from jax.sharding import PartitionSpec as P

LANES = 128
EPS = 1e-06
VMEM_LIMIT = 48 * 1024 * 1024

NT = (((1,), (1,)), ((), ()))
HIGHEST = lax.Precision.HIGHEST


def ring_order(mesh):
    members = list(mesh.devices[0, 0])
    places = [getattr(device, "coords", None) for device in members]
    if len(members) < 2 or any(place is None for place in places):
        return list(range(len(members)))
    axis = [i for i in range(len(places[0])) if places[0][i] != places[1][i]][0]
    columns = {}
    for index, place in enumerate(places):
        columns.setdefault(place[axis], []).append(index)
    order = []
    for step, key in enumerate(sorted(columns)):
        order += columns[key] if step % 2 == 0 else columns[key][::-1]
    if len(columns) == len(members):
        order = list(range(len(members)))
    return order


def params(**kw):
    return pltpu.CompilerParams(vmem_limit_bytes=VMEM_LIMIT, **kw)


def full_specs(count):
    return [pl.BlockSpec(memory_space=pltpu.VMEM)] * count


SCALARS = pl.BlockSpec(memory_space=pltpu.SMEM)


def local_sums_kernel(parts, covs, sid_ref, e_ref, gt_ref, dt_ref, et_ref, *rest):
    out_refs, design = rest[:parts], rest[parts]
    rows = e_ref.shape[0]
    genes = et_ref.shape[0] // parts
    variants = gt_ref.shape[0]
    share = (out_refs[0].shape[0] - genes - (covs + 8)) if parts > 1 else variants
    sid = sid_ref[0]
    design[...] = jnp.zeros_like(design)
    design[:covs] = dt_ref[...]
    first = lax.broadcasted_iota(jnp.int32, (16, rows), 0) == 0
    design[covs : covs + 16] = first.astype(jnp.float32).astype(jnp.bfloat16)
    et_ref[...] = e_ref[...].T
    right = design[...]

    def sums(block):
        prod = lax.dot_general(block, right, NT, preferred_element_type=jnp.float32)
        wide = block.astype(jnp.float32)
        squares = jnp.sum(wide * wide, axis=1, keepdims=True)
        lane = lax.broadcasted_iota(jnp.int32, prod.shape, 1)
        return jnp.where(lane == covs + 1, squares, prod)

    gram = lax.dot_general(design[: covs + 16], right, NT, preferred_element_type=jnp.float32)[: covs + 8]
    for d in range(parts):
        other = sid ^ d
        start = pl.multiple_of(other * genes, 16)
        out_refs[d][:genes] = sums(et_ref[pl.ds(start, genes), :])
        if share == variants:
            out_refs[d][genes : genes + share] = sums(gt_ref[...])
        else:
            start = pl.multiple_of(other * share, 16)
            out_refs[d][genes : genes + share] = sums(gt_ref[pl.ds(start, share), :])
        out_refs[d][genes + share :] = gram


def local_sums(sid, e, gt, dt, parts, share):
    rows, width = e.shape
    covs = dt.shape[0]
    genes = width // parts
    height = genes + share + covs + 8
    outs = [jax.ShapeDtypeStruct((width, rows), jnp.bfloat16)]
    outs += [jax.ShapeDtypeStruct((height, LANES), jnp.float32)] * parts
    return pl.pallas_call(
        functools.partial(local_sums_kernel, parts, covs),
        out_shape=outs,
        in_specs=[SCALARS] + full_specs(3),
        out_specs=full_specs(parts + 1),
        scratch_shapes=[pltpu.VMEM((LANES, rows), jnp.bfloat16)],
        compiler_params=params(),
        cost_estimate=pl.CostEstimate(flops=2 * rows * LANES * (width + 300), bytes_accessed=4 * rows * width, transcendentals=0),
        name="local_sums",
    )(sid, e, gt, dt)


def products_kernel(parts, blocks, sid_ref, own_ref, partner_ref, *rest):
    near, far, outs = rest[:blocks], rest[blocks : 2 * blocks], rest[2 * blocks :]
    genes = own_ref.shape[0] // parts
    sid = sid_ref[0]
    x_own = jnp.concatenate([ref[...] for ref in near], axis=0)
    x_far = jnp.concatenate([ref[...] for ref in far], axis=0)
    for d in range(parts):
        start = pl.multiple_of((sid ^ d) * genes, 16)
        part = lax.dot_general(own_ref[pl.ds(start, genes), :], x_own, NT, preferred_element_type=jnp.float32)
        part += lax.dot_general(partner_ref[pl.ds(start, genes), :], x_far, NT, preferred_element_type=jnp.float32)
        outs[d][...] = part


def products(sid, et_own, et_partner, near, far, parts):
    width, rows = et_own.shape
    columns = sum(x.shape[0] for x in near)
    return pl.pallas_call(
        functools.partial(products_kernel, parts, len(near)),
        out_shape=[jax.ShapeDtypeStruct((width // parts, columns), jnp.float32)] * parts,
        in_specs=[SCALARS] + full_specs(2 + 2 * len(near)),
        out_specs=full_specs(parts),
        compiler_params=params(),
        cost_estimate=pl.CostEstimate(flops=4 * rows * width * columns, bytes_accessed=4 * rows * width, transcendentals=0),
        name="products",
    )(sid, et_own, et_partner, *near, *far)


def finish_kernel(parts, ring, half, place_ref, fit_ref, scale_ref, *rest):
    chunks, out_ref, held = rest[:-2], rest[-2], rest[-1]
    middle = ring // 2
    genes = out_ref.shape[0]
    core = place_ref[0]
    for k in range(middle + 1):
        own = chunks[k * parts : (k + 1) * parts]
        sums = [own[0][...], own[1][...]]
        for d in range(2, parts):
            sums[d % 2] = sums[d % 2] + own[d][...]
        for side in range(2):
            if k in (0, middle):
                held[side * ring + k] = sums[side]
            else:
                held[side * ring + ring - k] = sums[side][:, :half]
                held[side * ring + k] = sums[side][:, half:]
    variants = 2 * half
    group = LANES // math.gcd(variants, LANES)
    for j in range(0, ring, group):
        pieces = []
        for block in range(j, j + group):
            slot = place_ref[1 + block]
            for side in range(2):
                pieces.append(held[(core ^ side) * ring + slot])
        span = slice(j * variants, (j + group) * variants)
        corr = jnp.concatenate(pieces, axis=1) - fit_ref[:, span]
        out_ref[:, span] = corr * corr * scale_ref[:, span]


def finish(place, fit, scale, chunks, parts, ring, half):
    genes = fit.shape[0]
    return pl.pallas_call(
        functools.partial(finish_kernel, parts, ring, half),
        out_shape=jax.ShapeDtypeStruct(fit.shape, jnp.float32),
        in_specs=[SCALARS] + full_specs(2 + len(chunks)),
        out_specs=pl.BlockSpec(memory_space=pltpu.VMEM),
        scratch_shapes=[pltpu.VMEM((2 * ring, genes, half), jnp.float32)],
        compiler_params=params(),
        name="finish",
    )(place, fit, scale, *chunks)


def shards(order, expression, genotypes, covariates, distance_bins, gene_folds, fold_weights):
    parts, ring = lax.axis_size("samp"), lax.axis_size("var")
    rows, width = expression.shape
    covs = covariates.shape[1]
    samples = rows * parts
    genes = width // parts
    gt = genotypes.T
    variants = gt.shape[0]
    half = variants // 2
    quarter = half // 2
    middle = ring // 2
    sid = lax.axis_index("samp").astype(jnp.int32)
    core = sid & 1
    here = lax.axis_index("var")

    def exchange(x, d):
        return lax.ppermute(x, "samp", [(s, s ^ d) for s in range(parts)])

    forward = [(order[i], order[(i + 1) % ring]) for i in range(ring)]
    backward = [(b, a) for a, b in forward]

    low, high = gt[:half], gt[half:]
    mine = jnp.where(core == 0, low, high)
    yours = jnp.where(core == 0, high, low)
    own = [(mine,)]
    far = [(exchange(yours, 1),)]
    for held in (own, far):
        right, left = held[0][0], held[0][0]
        for k in range(1, middle):
            right = lax.ppermute(right, "var", forward)
            left = lax.ppermute(left, "var", backward)
            held.append((right, left))
        held.append((lax.ppermute(right[:quarter], "var", forward), lax.ppermute(left[quarter:], "var", backward)))

    share = variants // parts if variants % (16 * parts) == 0 else variants
    et, *sums = local_sums(sid[None], expression, gt, covariates.T, parts, share)
    et_far = exchange(et, 1)
    total = sums[0]
    for d in range(1, parts):
        total = total + exchange(sums[d], d)
    expr_sums, geno_sums, gram = total[:genes], total[genes : genes + share], total[genes + share :]
    if share == variants:
        geno_all = lax.all_gather(geno_sums, "var", axis=0, tiled=True)
    else:
        geno_all = lax.all_gather(geno_sums, ("var", "samp"), axis=0, tiled=True)

    chunks = []
    for k in range(middle + 1):
        out = products(sid[None], et, et_far, own[k], far[k], parts)
        chunks += [out[0]] + [exchange(out[d], d) for d in range(1, parts)]

    design_rank = covs + 1
    factor = jnp.linalg.cholesky(gram[:design_rank, :design_rank])
    inverse = lax.linalg.triangular_solve(factor, jnp.eye(design_rank, dtype=jnp.float32), left_side=True, lower=True)

    def whiten(x):
        fit = lax.dot_general(x[:, :design_rank], inverse, NT, precision=HIGHEST)
        squares = x[:, design_rank]
        norm = jnp.maximum(squares - jnp.sum(fit * fit, axis=1), 1e-06 * squares)
        return fit, 1.0 / (norm + EPS)

    expr_fit, expr_inv = whiten(expr_sums)
    geno_fit, geno_inv = whiten(geno_all)
    fit = lax.dot_general(expr_fit, geno_fit, NT, precision=HIGHEST)

    folds, bins = fold_weights.shape
    tiles = distance_bins.shape[0]
    total_variants = ring * variants
    fold_onehot = (gene_folds[:, None] == jnp.arange(folds)[None, :]).astype(jnp.float32)
    row_weights = jnp.dot(fold_onehot, fold_weights, precision=HIGHEST)
    bin_match = distance_bins.T[:, :, None] == jnp.arange(bins)[None, None, :]
    tile_weight = jnp.sum(jnp.where(bin_match, row_weights[:, None, :], 0.0), axis=2)
    dof = jnp.float32(samples - covs - 2)
    tile_scale = dof * tile_weight * expr_inv[:, None]
    scale = jnp.repeat(tile_scale, total_variants // tiles, axis=1) * geno_inv[None, :]

    position = [0] * ring
    for i, index in enumerate(order):
        position[index] = i
    position = jnp.asarray(position, jnp.int32)
    slots = jnp.mod(position - position[here], ring)
    place = jnp.concatenate([core[None], slots]).astype(jnp.int32)
    return finish(place, fit, scale, chunks, parts, ring, half)


def solution(mesh):
    return jax.shard_map(
        functools.partial(shards, ring_order(mesh)),
        mesh=mesh,
        in_specs=(
            P(("groups", "samp"), "var"),
            P(("groups", "samp"), "var"),
            P(("groups", "samp"), None),
            P("groups", ("var", "samp")),
            P(("groups", "var", "samp")),
            P(),
        ),
        out_specs=P(("groups", "var", "samp"), None),
        check_vma=False,
    )
```

```python
import functools
import math

import jax
import jax.numpy as jnp
from jax import lax
from jax.experimental import pallas as pl
from jax.experimental.pallas import tpu as pltpu
from jax.sharding import PartitionSpec as P

LANES = 128
EPS = 1e-06
VMEM_LIMIT = 48 * 1024 * 1024

NT = (((1,), (1,)), ((), ()))
NN = (((1,), (0,)), ((), ()))
HIGHEST = lax.Precision.HIGHEST


def ring_order(mesh):
    members = list(mesh.devices[0, 0])
    places = [getattr(device, "coords", None) for device in members]
    if len(members) < 2 or any(place is None for place in places):
        return list(range(len(members)))
    axis = [i for i in range(len(places[0])) if places[0][i] != places[1][i]][0]
    columns = {}
    for index, place in enumerate(places):
        columns.setdefault(place[axis], []).append(index)
    order = []
    for step, key in enumerate(sorted(columns)):
        order += columns[key] if step % 2 == 0 else columns[key][::-1]
    return order


def call(kernel, out_shape, name, flops, operands, scratch=(), scalars=1, tokens=0):
    vmem = pl.BlockSpec(memory_space=pltpu.VMEM)
    smem = pl.BlockSpec(memory_space=pltpu.SMEM)
    rest = len(operands) - scalars - tokens
    moved = sum(math.prod(x.shape) * x.dtype.itemsize for x in operands[: scalars + rest])
    return pl.pallas_call(
        kernel,
        out_shape=out_shape,
        in_specs=[smem] * scalars + [vmem] * rest + [pl.BlockSpec(memory_space=pl.ANY)] * tokens,
        out_specs=jax.tree.map(lambda _: vmem, out_shape),
        scratch_shapes=list(scratch),
        compiler_params=pltpu.CompilerParams(vmem_limit_bytes=VMEM_LIMIT),
        cost_estimate=pl.CostEstimate(flops=flops, bytes_accessed=moved, transcendentals=0),
        name=name,
    )(*operands)


def first_kernel(parts, covs, sid_ref, e_ref, gt_ref, dt_ref, left_ref, send_ref, other_ref, mine_ref, wide):
    width = e_ref.shape[1]
    genes = width // parts
    sid = sid_ref[0]
    wide[...] = e_ref[...].T
    owners = [sid ^ 1 ^ d for d in range(2, parts, 2)] + [sid ^ 1]
    owners += [sid ^ d for d in range(2, parts, 2)] + [sid]
    for i, owner in enumerate(owners):
        start = pl.multiple_of(owner * genes, 16)
        left_ref[i * genes : (i + 1) * genes] = wide[pl.ds(start, genes), :]
    rows = dt_ref.shape[1]
    left_ref[width : width + covs] = dt_ref[...]
    first = lax.broadcasted_iota(jnp.int32, (16, rows), 0) == 0
    left_ref[width + covs :] = first.astype(jnp.float32).astype(jnp.bfloat16)
    design = left_ref[width:]
    right = jnp.concatenate([design, jnp.zeros((LANES - design.shape[0], rows), jnp.bfloat16)], axis=0)
    right = jnp.concatenate([right, gt_ref[...]], axis=0)
    split(parts, covs, genes, left_ref, right, send_ref, other_ref, mine_ref, True)


def next_kernel(parts, covs, blocks, left_ref, *rest):
    right = jnp.concatenate([ref[...] for ref in rest[:blocks]], axis=0)
    send_ref, other_ref, mine_ref = rest[-3:]
    genes = mine_ref.shape[0]
    split(parts, covs, genes, left_ref, right, send_ref, other_ref, mine_ref, False)


def split(parts, covs, genes, left_ref, right, send_ref, other_ref, mine_ref, squares):
    width = genes * parts
    span = genes * (parts // 2 - 1)
    deep = covs + 8

    def dot(a):
        return lax.dot_general(a, right, NT, preferred_element_type=jnp.float32)

    def genes_of(start, count):
        a = left_ref[start : start + count]
        prod = dot(a)
        if not squares:
            return prod
        a = a.astype(jnp.float32)
        lane = lax.broadcasted_iota(jnp.int32, prod.shape, 1)
        return jnp.where(lane == covs + 1, jnp.sum(a * a, axis=1, keepdims=True), prod)

    send_ref[:span] = genes_of(0, span)
    send_ref[span + deep :] = genes_of(span, genes)
    other_ref[:span] = genes_of(span + genes, span)
    mine_ref[...] = genes_of(2 * span + genes, genes)
    square = right.astype(jnp.float32)
    square = square * square
    high = square.astype(jnp.bfloat16)
    low = (square - high.astype(jnp.float32)).astype(jnp.bfloat16)
    ones = jnp.ones((16, right.shape[1]), jnp.bfloat16)
    total = lax.dot_general(ones, high, NT, preferred_element_type=jnp.float32)
    total += lax.dot_general(ones, low, NT, preferred_element_type=jnp.float32)
    fits = dot(left_ref[width:])[:deep]
    row = lax.broadcasted_iota(jnp.int32, fits.shape, 0)
    fits = jnp.where(row == covs + 1, total[:1], fits)
    send_ref[span : span + deep] = fits
    other_ref[span:] = fits


def product_shapes(parts, covs, genes, columns):
    span = genes * (parts // 2 - 1)
    rows = (span + covs + 8 + genes, span + covs + 8, genes)
    return [jax.ShapeDtypeStruct((r, columns), jnp.float32) for r in rows]


def first_products(sid, e, gt, dt, parts):
    rows, width = e.shape
    covs = dt.shape[0]
    columns = LANES + gt.shape[0]
    left = jax.ShapeDtypeStruct((width + covs + 16, rows), jnp.bfloat16)
    return call(
        functools.partial(first_kernel, parts, covs),
        [left] + product_shapes(parts, covs, width // parts, columns),
        "first_products",
        2 * rows * width * columns,
        (sid, e, gt, dt),
        scratch=[pltpu.VMEM((width, rows), jnp.bfloat16)],
    )


def next_products(left, blocks, parts, covs, tokens):
    rows = left.shape[1]
    width = left.shape[0] - covs - 16
    columns = sum(b.shape[0] for b in blocks)
    return call(
        functools.partial(next_kernel, parts, covs, len(blocks)),
        product_shapes(parts, covs, width // parts, columns),
        "next_products",
        2 * rows * width * columns,
        (left, *blocks, *tokens),
        scalars=0,
        tokens=len(tokens),
    )


def add_kernel(genes, deep, other_ref, came_ref, *out_refs):
    span = genes * len(out_refs)
    for i, out_ref in enumerate(out_refs):
        rows = slice(i * genes, (i + 1) * genes)
        out_ref[:genes] = other_ref[rows] + came_ref[rows]
        out_ref[genes:] = other_ref[span:] + came_ref[span : span + deep]


def add_cores(other, came, genes, deep):
    chips = (other.shape[0] - deep) // genes
    shape = jax.ShapeDtypeStruct((genes + deep, other.shape[1]), jnp.float32)
    return call(
        functools.partial(add_kernel, genes, deep),
        [shape] * chips,
        "add_cores",
        other.size,
        (other, came),
        scalars=0,
    )


def chunk_sums(genes, deep, mine_ref, came_ref, sent_ref, got_refs):
    corr = mine_ref[...] + came_ref[came_ref.shape[0] - genes :]
    fits = sent_ref[genes:]
    for got_ref in got_refs:
        corr = corr + got_ref[:genes]
        fits = fits + got_ref[genes:]
    return corr, fits


def solve_kernel(chips, covs, dof, weight_ref, mine_ref, came_ref, sent_ref, *rest):
    got_refs, (bins_ref, folds_ref, solved_ref, tile_ref) = rest[:chips], rest[chips : chips + 4]
    genes = mine_ref.shape[0]
    rank, deep = covs + 1, covs + 8
    corr, fits = chunk_sums(genes, deep, mine_ref, came_ref, sent_ref, got_refs)
    cross, gram = corr[:, :LANES], fits[:, :LANES]
    row = lax.broadcasted_iota(jnp.int32, gram.shape, 0)
    lane = lax.broadcasted_iota(jnp.int32, gram.shape, 1)
    inside = jnp.logical_and(row < rank, lane < rank)
    a = jnp.where(inside, gram, 0.0)
    for k in range(rank):
        across = a[k : k + 1, :]
        down = a[:, k : k + 1]
        inv = 1.0 / across[:, k : k + 1]
        scaled = across * inv
        swept = a - down * scaled
        swept = jnp.where(row == k, scaled, swept)
        swept = jnp.where(lane == k, down * inv, swept)
        a = jnp.where(jnp.logical_and(row == k, lane == k), -inv, swept)
    inverse = jnp.where(inside, -a, 0.0)
    lane = lax.broadcasted_iota(jnp.int32, cross.shape, 1)
    squares = jnp.sum(jnp.where(lane == rank, cross, 0.0), axis=1, keepdims=True)
    cross = jnp.where(lane < rank, cross, 0.0)
    beta = lax.dot_general(cross, inverse, NT, precision=HIGHEST, preferred_element_type=jnp.float32)
    norm = squares - jnp.sum(beta * cross[:, :deep], axis=1, keepdims=True)
    norm = jnp.maximum(norm, 1e-06 * squares) + EPS
    solved_ref[:genes] = beta
    solved_ref[genes:] = inverse[:, :deep]

    bins, folds = bins_ref[...], folds_ref[...]
    tile = jnp.zeros(bins.shape, jnp.float32)
    for b in range(weight_ref.shape[1]):
        of_bin = jnp.zeros(folds.shape, jnp.float32)
        for f in range(weight_ref.shape[0]):
            of_bin = jnp.where(folds == f, weight_ref[f, b], of_bin)
        tile = jnp.where(bins == b, of_bin, tile)
    tile_ref[...] = tile.T * (dof / norm)


def solve(weights, mine, came, sent, got, bins, folds, covs, dof):
    genes = mine.shape[0]
    outs = [
        jax.ShapeDtypeStruct((genes + covs + 8, covs + 8), jnp.float32),
        jax.ShapeDtypeStruct((genes, bins.shape[0]), jnp.float32),
    ]
    return call(
        functools.partial(solve_kernel, len(got), covs, dof),
        outs,
        "solve",
        10**8,
        (weights, mine, came, sent, *got, bins, folds),
    )


def finish_kernel(chips, covs, ring, order, here_ref, solved_ref, tile_ref, *rest):
    chunks, out_ref, held = rest[:-2], rest[-2], rest[-1]
    middle = ring // 2
    genes = out_ref.shape[0]
    deep = covs + 8
    variants = held.shape[2]
    step = 3 + chips
    solved = solved_ref[...]
    for k in range(middle + 1):
        mine, came, sent, *got = chunks[k * step : (k + 1) * step]
        corr, fits = chunk_sums(genes, deep, mine, came, sent, got)
        if k == 0:
            corr, fits = corr[:, LANES:], fits[:, LANES:]
        row = lax.broadcasted_iota(jnp.int32, fits.shape, 0)
        squares = fits[covs + 1 : covs + 2]
        fits = jnp.where(row <= covs, fits, 0.0)
        both = lax.dot_general(solved, fits, NN, precision=HIGHEST, preferred_element_type=jnp.float32)
        norm = squares - jnp.sum(both[genes:] * fits, axis=0, keepdims=True)
        norm = jnp.maximum(norm, 1e-06 * squares) + EPS
        corr = corr - both[:genes]
        stat = corr * corr * (1.0 / norm)
        if k in (0, middle):
            held[k] = stat
        else:
            held[ring - k] = stat[:, :variants]
            held[k] = stat[:, variants:]
    here = here_ref[0]
    position = {index: i for i, index in enumerate(order)}
    mine = jnp.int32(0)
    for index in range(ring):
        mine = jnp.where(here == index, position[index], mine)
    group = LANES // math.gcd(variants, LANES)
    tile_width = ring * variants // tile_ref.shape[1]
    tile = tile_ref[...]
    for j in range(0, ring, group):
        pieces = [held[lax.rem(position[j + b] - mine + ring, ring)] for b in range(group)]
        span = slice(j * variants, (j + group) * variants)
        weight = [
            jnp.broadcast_to(tile[:, t : t + 1], (genes, tile_width))
            for t in range(span.start // tile_width, span.stop // tile_width)
        ]
        out_ref[:, span] = jnp.concatenate(pieces, axis=1) * jnp.concatenate(weight, axis=1)


def finish(here, solved, tile, chunks, covs, ring, order, chips):
    genes = tile.shape[0]
    variants = chunks[-1].shape[1]
    flat = [x for x in chunks]
    return call(
        functools.partial(finish_kernel, chips, covs, ring, order),
        jax.ShapeDtypeStruct((genes, ring * variants), jnp.float32),
        "finish",
        10**8,
        (here, solved, tile, *flat),
        scratch=[pltpu.VMEM((ring, genes, variants), jnp.float32)],
    )


def shards(order, expression, genotypes, covariates, distance_bins, gene_folds, fold_weights):
    parts, ring = lax.axis_size("samp"), lax.axis_size("var")
    rows, width = expression.shape
    covs = covariates.shape[1]
    genes = width // parts
    deep = covs + 8
    dof = float(rows * parts - covs - 2)
    gt = genotypes.T
    variants = gt.shape[0]
    middle = ring // 2
    sid = lax.axis_index("samp").astype(jnp.int32)[None]
    here = lax.axis_index("var").astype(jnp.int32)[None]

    def exchange(x, d):
        return lax.ppermute(x, "samp", [(s, s ^ d) for s in range(parts)])

    forward = [(order[i], order[(i + 1) % ring]) for i in range(ring)]
    backward = [(b, a) for a, b in forward]

    def right(x):
        return lax.ppermute(x, "var", forward)

    def left(x):
        return lax.ppermute(x, "var", backward)

    blocks = [(gt, gt)]
    for k in range(1, middle):
        blocks.append((right(blocks[-1][0]), left(blocks[-1][1])))
    blocks.append((right(blocks[-1][0][: variants // 2]), left(blocks[-1][1][variants // 2 :])))

    chunks, tokens = [], []
    lhs = None
    for k in range(middle + 1):
        if k == 0:
            lhs, send, other, mine = first_products(sid, expression, gt, covariates.T, parts)
        else:
            send, other, mine = next_products(lhs, blocks[k], parts, covs, tokens)
        came = exchange(send, 1)
        sent = add_cores(other, came, genes, deep)
        got = [exchange(sent[i], 2 * (i + 1)) for i in range(len(sent))]
        if k == 0:
            solved, tile = solve(
                fold_weights, mine, came, sent[0], got, distance_bins, gene_folds[None], covs, dof
            )
        chunks += [mine, came, sent[0], *got]
        tokens = [sent[0]] + (chunks[-2 * (3 + len(got)) :][3 : 3 + len(got)] if k > 0 else [])
    return finish(here, solved, tile, chunks, covs, ring, tuple(order), len(got))


def solution(mesh):
    return jax.shard_map(
        functools.partial(shards, ring_order(mesh)),
        mesh=mesh,
        in_specs=(
            P(("groups", "samp"), "var"),
            P(("groups", "samp"), "var"),
            P(("groups", "samp"), None),
            P("groups", ("var", "samp")),
            P(("groups", "var", "samp")),
            P(),
        ),
        out_specs=P(("groups", "var", "samp"), None),
        check_vma=False,
    )
```

```python
import functools
import math

import jax
import jax.numpy as jnp
from jax import lax
from jax.experimental import pallas as pl
from jax.experimental.pallas import tpu as pltpu
from jax.sharding import PartitionSpec as P

LANES = 128
EPS = 1e-06
VMEM_LIMIT = 16 * 1024 * 1024

NT = (((1,), (1,)), ((), ()))
NN = (((1,), (0,)), ((), ()))
HIGHEST = lax.Precision.HIGHEST


def ring_order(mesh):
    members = list(mesh.devices[0, 0])
    places = [getattr(device, "coords", None) for device in members]
    if len(members) < 2 or any(place is None for place in places):
        return list(range(len(members)))
    axis = [i for i in range(len(places[0])) if places[0][i] != places[1][i]][0]
    columns = {}
    for index, place in enumerate(places):
        columns.setdefault(place[axis], []).append(index)
    order = []
    for step, key in enumerate(sorted(columns)):
        order += columns[key] if step % 2 == 0 else columns[key][::-1]
    return order


def call(kernel, out_shape, name, flops, operands, scratch=(), scalars=1, tokens=0):
    vmem = pl.BlockSpec(memory_space=pltpu.VMEM)
    smem = pl.BlockSpec(memory_space=pltpu.SMEM)
    rest = len(operands) - scalars - tokens
    moved = sum(math.prod(x.shape) * x.dtype.itemsize for x in operands[: scalars + rest])
    return pl.pallas_call(
        kernel,
        out_shape=out_shape,
        in_specs=[smem] * scalars + [vmem] * rest + [pl.BlockSpec(memory_space=pl.ANY)] * tokens,
        out_specs=jax.tree.map(lambda _: vmem, out_shape),
        scratch_shapes=list(scratch),
        compiler_params=pltpu.CompilerParams(vmem_limit_bytes=VMEM_LIMIT),
        cost_estimate=pl.CostEstimate(flops=flops, bytes_accessed=moved, transcendentals=0),
        name=name,
    )(*operands)


def first_kernel(parts, covs, sid_ref, e_ref, gt_ref, dt_ref, left_ref, send_ref, other_ref, mine_ref, wide):
    width = e_ref.shape[1]
    genes = width // parts
    sid = sid_ref[0]
    wide[...] = e_ref[...].T
    owners = [sid ^ 1 ^ d for d in range(2, parts, 2)] + [sid ^ 1]
    owners += [sid ^ d for d in range(2, parts, 2)] + [sid]
    for i, owner in enumerate(owners):
        start = pl.multiple_of(owner * genes, 16)
        left_ref[i * genes : (i + 1) * genes] = wide[pl.ds(start, genes), :]
    rows = dt_ref.shape[1]
    left_ref[width : width + covs] = dt_ref[...]
    first = lax.broadcasted_iota(jnp.int32, (16, rows), 0) == 0
    left_ref[width + covs :] = first.astype(jnp.float32).astype(jnp.bfloat16)
    design = left_ref[width:]
    right = jnp.concatenate([design, jnp.zeros((LANES - design.shape[0], rows), jnp.bfloat16)], axis=0)
    right = jnp.concatenate([right, gt_ref[...]], axis=0)
    split(parts, covs, genes, left_ref, right, send_ref, other_ref, mine_ref, True)


def next_kernel(parts, covs, blocks, left_ref, *rest):
    right = jnp.concatenate([ref[...] for ref in rest[:blocks]], axis=0)
    send_ref, other_ref, mine_ref = rest[-3:]
    genes = mine_ref.shape[0]
    split(parts, covs, genes, left_ref, right, send_ref, other_ref, mine_ref, False)


def split(parts, covs, genes, left_ref, right, send_ref, other_ref, mine_ref, squares):
    width = genes * parts
    span = genes * (parts // 2 - 1)
    deep = covs + 8

    prod = lax.dot_general(left_ref[...], right, NT, preferred_element_type=jnp.float32)
    outs = prod[:width]
    if squares:
        a = left_ref[:width].astype(jnp.float32)
        lane = lax.broadcasted_iota(jnp.int32, outs.shape, 1)
        outs = jnp.where(lane == covs + 1, jnp.sum(a * a, axis=1, keepdims=True), outs)
    send_ref[:span] = outs[:span]
    send_ref[span + deep :] = outs[span : span + genes]
    other_ref[:span] = outs[span + genes : 2 * span + genes]
    mine_ref[...] = outs[2 * span + genes :]
    square = right.astype(jnp.float32)
    square = square * square
    high = square.astype(jnp.bfloat16)
    low = (square - high.astype(jnp.float32)).astype(jnp.bfloat16)
    ones = jnp.ones((16, right.shape[1]), jnp.bfloat16)
    total = lax.dot_general(ones, high, NT, preferred_element_type=jnp.float32)
    total += lax.dot_general(ones, low, NT, preferred_element_type=jnp.float32)
    fits = prod[width : width + deep]
    row = lax.broadcasted_iota(jnp.int32, fits.shape, 0)
    fits = jnp.where(row == covs + 1, total[:1], fits)
    send_ref[span : span + deep] = fits
    other_ref[span:] = fits


def product_shapes(parts, covs, genes, columns):
    span = genes * (parts // 2 - 1)
    rows = (span + covs + 8 + genes, span + covs + 8, genes)
    return [jax.ShapeDtypeStruct((r, columns), jnp.float32) for r in rows]


def first_products(sid, e, gt, dt, parts):
    rows, width = e.shape
    covs = dt.shape[0]
    columns = LANES + gt.shape[0]
    left = jax.ShapeDtypeStruct((width + covs + 16, rows), jnp.bfloat16)
    return call(
        functools.partial(first_kernel, parts, covs),
        [left] + product_shapes(parts, covs, width // parts, columns),
        "first_products",
        2 * rows * width * columns,
        (sid, e, gt, dt),
        scratch=[pltpu.VMEM((width, rows), jnp.bfloat16)],
    )


def next_products(left, blocks, parts, covs, tokens):
    rows = left.shape[1]
    width = left.shape[0] - covs - 16
    columns = sum(b.shape[0] for b in blocks)
    return call(
        functools.partial(next_kernel, parts, covs, len(blocks)),
        product_shapes(parts, covs, width // parts, columns),
        "next_products",
        2 * rows * width * columns,
        (left, *blocks, *tokens),
        scalars=0,
        tokens=len(tokens),
    )


def add_kernel(genes, deep, other_ref, came_ref, *out_refs):
    span = genes * len(out_refs)
    for i, out_ref in enumerate(out_refs):
        rows = slice(i * genes, (i + 1) * genes)
        out_ref[:genes] = other_ref[rows] + came_ref[rows]
        out_ref[genes:] = other_ref[span:] + came_ref[span : span + deep]


def add_cores(other, came, genes, deep):
    chips = (other.shape[0] - deep) // genes
    shape = jax.ShapeDtypeStruct((genes + deep, other.shape[1]), jnp.float32)
    return call(
        functools.partial(add_kernel, genes, deep),
        [shape] * chips,
        "add_cores",
        other.size,
        (other, came),
        scalars=0,
    )


def chunk_sums(genes, deep, mine_ref, came_ref, sent_ref, got_refs):
    corr = mine_ref[...] + came_ref[came_ref.shape[0] - genes :]
    fits = sent_ref[genes:]
    for got_ref in got_refs:
        corr = corr + got_ref[:genes]
        fits = fits + got_ref[genes:]
    return corr, fits


def solve_kernel(chips, covs, dof, weight_ref, mine_ref, came_ref, sent_ref, *rest):
    got_refs, (bins_ref, folds_ref, solved_ref, scale_ref) = rest[:chips], rest[chips : chips + 4]
    genes = mine_ref.shape[0]
    rank, deep = covs + 1, covs + 8
    corr, fits = chunk_sums(genes, deep, mine_ref, came_ref, sent_ref, got_refs)
    cross, gram = corr[:, :LANES], fits[:, :LANES]
    row = lax.broadcasted_iota(jnp.int32, gram.shape, 0)
    lane = lax.broadcasted_iota(jnp.int32, gram.shape, 1)
    inside = jnp.logical_and(row < rank, lane < rank)
    a = jnp.where(inside, gram, jnp.where(row == lane, 1.0, 0.0))
    for k in range(0, rank, 2):
        down0 = jnp.broadcast_to(a[:, k : k + 1], a.shape)
        down1 = jnp.broadcast_to(a[:, k + 1 : k + 2], a.shape)
        p00, p01, p11 = down0[k : k + 1], down1[k : k + 1], down1[k + 1 : k + 2]
        inv = 1.0 / (p00 * p11 - p01 * p01)
        q00, q01, q11 = p11 * inv, -p01 * inv, p00 * inv
        row0, row1 = a[k : k + 1], a[k + 1 : k + 2]
        first = q00 * row0 + q01 * row1
        second = q01 * row0 + q11 * row1
        swept = a - down0 * first - down1 * second
        swept = jnp.where(lane == k, down0 * q00 + down1 * q01, swept)
        swept = jnp.where(lane == k + 1, down0 * q01 + down1 * q11, swept)
        first = jnp.where(lane[:1] == k, -q00, jnp.where(lane[:1] == k + 1, -q01, first))
        second = jnp.where(lane[:1] == k, -q01, jnp.where(lane[:1] == k + 1, -q11, second))
        a = jnp.where(row == k, first, jnp.where(row == k + 1, second, swept))
    inverse = jnp.where(inside, -a, 0.0)
    lane = lax.broadcasted_iota(jnp.int32, cross.shape, 1)
    squares = jnp.sum(jnp.where(lane == rank, cross, 0.0), axis=1, keepdims=True)
    cross = jnp.where(lane < rank, cross, 0.0)
    beta = lax.dot_general(cross, inverse, NT, precision=HIGHEST, preferred_element_type=jnp.float32)
    norm = squares - jnp.sum(beta * cross[:, :deep], axis=1, keepdims=True)
    norm = jnp.maximum(norm, 1e-06 * squares) + EPS
    solved_ref[:genes] = beta
    solved_ref[genes:] = inverse[:, :deep]

    bins, folds = bins_ref[...], folds_ref[...]
    tile = jnp.zeros(bins.shape, jnp.float32)
    for b in range(weight_ref.shape[1]):
        of_bin = jnp.zeros(folds.shape, jnp.float32)
        for f in range(weight_ref.shape[0]):
            of_bin = jnp.where(folds == f, weight_ref[f, b], of_bin)
        tile = jnp.where(bins == b, of_bin, tile)
    tile = tile.T * (dof / norm)
    width = scale_ref.shape[1] // tile.shape[1]
    for t in range(0, tile.shape[1], 2):
        pair = [jnp.broadcast_to(tile[:, i : i + 1], (genes, width)) for i in (t, t + 1)]
        scale_ref[:, t * width : (t + 2) * width] = jnp.concatenate(pair, axis=1)


def solve(weights, mine, came, sent, got, bins, folds, covs, dof, variants):
    genes = mine.shape[0]
    outs = [
        jax.ShapeDtypeStruct((genes + covs + 8, covs + 8), jnp.float32),
        jax.ShapeDtypeStruct((genes, variants), jnp.float32),
    ]
    return call(
        functools.partial(solve_kernel, len(got), covs, dof),
        outs,
        "solve",
        10**8,
        (weights, mine, came, sent, *got, bins, folds),
    )


def fitted_stat(covs, skip, solved_ref, mine_ref, came_ref, sent_ref, got_refs):
    genes = mine_ref.shape[0]
    corr, fits = chunk_sums(genes, covs + 8, mine_ref, came_ref, sent_ref, got_refs)
    corr, fits = corr[:, skip:], fits[:, skip:]
    row = lax.broadcasted_iota(jnp.int32, fits.shape, 0)
    squares = fits[covs + 1 : covs + 2]
    fits = jnp.where(row <= covs, fits, 0.0)
    both = lax.dot_general(solved_ref[...], fits, NN, precision=HIGHEST, preferred_element_type=jnp.float32)
    norm = squares - jnp.sum(both[genes:] * fits, axis=0, keepdims=True)
    norm = jnp.maximum(norm, 1e-06 * squares) + EPS
    corr = corr - both[:genes]
    return corr * corr * (1.0 / norm)


def stat_kernel(chips, covs, skip, solved_ref, mine_ref, came_ref, sent_ref, *rest):
    rest[-1][...] = fitted_stat(covs, skip, solved_ref, mine_ref, came_ref, sent_ref, rest[:chips])


def chunk_stat(solved, mine, came, sent, got, covs, skip):
    return call(
        functools.partial(stat_kernel, len(got), covs, skip),
        jax.ShapeDtypeStruct((mine.shape[0], mine.shape[1] - skip), jnp.float32),
        "chunk_stat",
        10**8,
        (solved, mine, came, sent, *got),
        scalars=0,
    )


def finish_kernel(chips, covs, ring, order, here_ref, solved_ref, scale_ref, *rest):
    stats, last, (out_ref, held) = rest[: ring // 2], rest[ring // 2 : -2], rest[-2:]
    variants = held.shape[2]
    for k, stat in enumerate(stats):
        if k == 0:
            held[0] = stat[...]
        else:
            held[ring - k] = stat[:, :variants]
            held[k] = stat[:, variants:]
    held[ring // 2] = fitted_stat(covs, 0, solved_ref, *last[:3], last[3:])
    here = here_ref[0]
    position = {index: i for i, index in enumerate(order)}
    mine = jnp.int32(0)
    for index in range(ring):
        mine = jnp.where(here == index, position[index], mine)
    group = LANES // math.gcd(variants, LANES)
    for j in range(0, ring, group):
        pieces = [held[lax.rem(position[j + b] - mine + ring, ring)] for b in range(group)]
        span = slice(j * variants, (j + group) * variants)
        out_ref[:, span] = jnp.concatenate(pieces, axis=1) * scale_ref[:, span]


def finish(here, solved, scale, stats, last, covs, ring, order, chips):
    genes, variants = last[0].shape
    return call(
        functools.partial(finish_kernel, chips, covs, ring, order),
        jax.ShapeDtypeStruct(scale.shape, jnp.float32),
        "finish",
        10**8,
        (here, solved, scale, *stats, *last),
        scratch=[pltpu.VMEM((ring, genes, variants), jnp.float32)],
    )


def shards(order, expression, genotypes, covariates, distance_bins, gene_folds, fold_weights):
    parts, ring = lax.axis_size("samp"), lax.axis_size("var")
    rows, width = expression.shape
    covs = covariates.shape[1]
    genes = width // parts
    deep = covs + 8
    dof = float(rows * parts - covs - 2)
    gt = genotypes.T
    variants = gt.shape[0]
    middle = ring // 2
    sid = lax.axis_index("samp").astype(jnp.int32)[None]
    here = lax.axis_index("var").astype(jnp.int32)[None]

    def exchange(x, d):
        return lax.ppermute(x, "samp", [(s, s ^ d) for s in range(parts)])

    forward = [(order[i], order[(i + 1) % ring]) for i in range(ring)]
    backward = [(b, a) for a, b in forward]

    def right(x):
        return lax.ppermute(x, "var", forward)

    def left(x):
        return lax.ppermute(x, "var", backward)

    blocks = [(gt, gt)]
    for k in range(1, middle):
        blocks.append((right(blocks[-1][0]), left(blocks[-1][1])))
    blocks.append((right(blocks[-1][0][: variants // 2]), left(blocks[-1][1][variants // 2 :])))

    chunks, stats = [], []
    lhs = solved = scale = None

    done = {}

    def after(*names):
        return [done[name] for name in names if name in done]

    for k in range(middle + 1):
        if k == 0:
            lhs, send, other, mine = first_products(sid, expression, gt, covariates.T, parts)
        else:
            tokens = after(("got", k - 2), *([("sent", k - 1)] if k == middle else []))
            send, other, mine = next_products(lhs, blocks[k], parts, covs, tokens)
        came = exchange(send, 1)
        sent = add_cores(other, came, genes, deep)
        got = [exchange(sent[i], 2 * (i + 1)) for i in range(len(sent))]
        chunks.append((mine, came, sent[0], *got))
        done["came", k], done["sent", k], done["got", k] = came, sent[0], got[-1]
        if k == 0:
            solved, scale = solve(
                fold_weights, mine, came, sent[0], got, distance_bins, gene_folds[None], covs, dof, ring * variants
            )
            done["solved", 0] = solved
        if k < middle:
            stats.append(chunk_stat(solved, mine, came, sent[0], got, covs, LANES if k == 0 else 0))
            done["stat", k] = stats[k]
    return finish(here, solved, scale, stats, chunks[middle], covs, ring, tuple(order), len(got))


def solution(mesh):
    return jax.shard_map(
        functools.partial(shards, ring_order(mesh)),
        mesh=mesh,
        in_specs=(
            P(("groups", "samp"), "var"),
            P(("groups", "samp"), "var"),
            P(("groups", "samp"), None),
            P("groups", ("var", "samp")),
            P(("groups", "var", "samp")),
            P(),
        ),
        out_specs=P(("groups", "var", "samp"), None),
        check_vma=False,
    )
```

```python
import functools
import math

import jax
import jax.numpy as jnp
from jax import lax
from jax.experimental import pallas as pl
from jax.experimental.pallas import tpu as pltpu
from jax.sharding import PartitionSpec as P

LANES = 128
EPS = 1e-06
COST = {'products': 1, 'add': 10000000000, 'solve': 10000000000, 'stat': 1, 'place': 1, 'finish': 1, 'gate': 1000000000000}
VMEM_LIMIT = 16 * 1024 * 1024

NT = (((1,), (1,)), ((), ()))
NN = (((1,), (0,)), ((), ()))
HIGHEST = lax.Precision.HIGHEST


def ring_order(mesh):
    members = list(mesh.devices[0, 0])
    places = [getattr(device, "coords", None) for device in members]
    if len(members) < 2 or any(place is None for place in places):
        return list(range(len(members)))
    axis = [i for i in range(len(places[0])) if places[0][i] != places[1][i]][0]
    columns = {}
    for index, place in enumerate(places):
        columns.setdefault(place[axis], []).append(index)
    order = []
    for step, key in enumerate(sorted(columns)):
        order += columns[key] if step % 2 == 0 else columns[key][::-1]
    return order


def call(kernel, out_shape, name, flops, operands, scratch=(), scalars=1, tokens=0):
    vmem = pl.BlockSpec(memory_space=pltpu.VMEM)
    smem = pl.BlockSpec(memory_space=pltpu.SMEM)
    rest = len(operands) - scalars - tokens
    return pl.pallas_call(
        kernel,
        out_shape=out_shape,
        in_specs=[smem] * scalars + [vmem] * rest + [pl.BlockSpec(memory_space=pl.ANY)] * tokens,
        out_specs=jax.tree.map(lambda _: vmem, out_shape),
        scratch_shapes=list(scratch),
        compiler_params=pltpu.CompilerParams(vmem_limit_bytes=VMEM_LIMIT),
        cost_estimate=pl.CostEstimate(flops=flops, bytes_accessed=0, transcendentals=0),
        name=name,
    )(*operands)


def gate_kernel(*refs):
    pass


def gate(blocks, tokens):
    anywhere = pl.BlockSpec(memory_space=pl.ANY)
    return pl.pallas_call(
        gate_kernel,
        out_shape=[jax.ShapeDtypeStruct(b.shape, b.dtype) for b in blocks],
        in_specs=[anywhere] * (len(blocks) + len(tokens)),
        out_specs=[anywhere] * len(blocks),
        input_output_aliases={i: i for i in range(len(blocks))},
        cost_estimate=pl.CostEstimate(flops=COST["gate"], bytes_accessed=0, transcendentals=0),
        name="gate",
    )(*blocks, *tokens)


def first_kernel(parts, covs, sid_ref, e_ref, gt_ref, dt_ref, left_ref, send_ref, other_ref, mine_ref, wide):
    width = e_ref.shape[1]
    genes = width // parts
    sid = sid_ref[0]
    wide[...] = e_ref[...].T
    owners = [sid ^ 1 ^ d for d in range(2, parts, 2)] + [sid ^ 1]
    owners += [sid ^ d for d in range(2, parts, 2)] + [sid]
    for i, owner in enumerate(owners):
        start = pl.multiple_of(owner * genes, 16)
        left_ref[i * genes : (i + 1) * genes] = wide[pl.ds(start, genes), :]
    rows = dt_ref.shape[1]
    left_ref[width : width + covs] = dt_ref[...]
    first = lax.broadcasted_iota(jnp.int32, (16, rows), 0) == 0
    left_ref[width + covs :] = first.astype(jnp.float32).astype(jnp.bfloat16)
    design = left_ref[width:]
    right = jnp.concatenate([design, jnp.zeros((LANES - design.shape[0], rows), jnp.bfloat16)], axis=0)
    right = jnp.concatenate([right, gt_ref[...]], axis=0)
    split(parts, covs, genes, left_ref, right, send_ref, other_ref, mine_ref, True)


def next_kernel(parts, covs, blocks, left_ref, *rest):
    right = jnp.concatenate([ref[...] for ref in rest[:blocks]], axis=0)
    send_ref, other_ref, mine_ref = rest[-3:]
    genes = mine_ref.shape[0]
    split(parts, covs, genes, left_ref, right, send_ref, other_ref, mine_ref, False)


def split(parts, covs, genes, left_ref, right, send_ref, other_ref, mine_ref, squares):
    width = genes * parts
    span = genes * (parts // 2 - 1)
    deep = covs + 8

    prod = lax.dot_general(left_ref[...], right, NT, preferred_element_type=jnp.float32)
    outs = prod[:width]
    if squares:
        a = left_ref[:width].astype(jnp.float32)
        lane = lax.broadcasted_iota(jnp.int32, outs.shape, 1)
        outs = jnp.where(lane == covs + 1, jnp.sum(a * a, axis=1, keepdims=True), outs)
    send_ref[:span] = outs[:span]
    send_ref[span + deep :] = outs[span : span + genes]
    other_ref[:span] = outs[span + genes : 2 * span + genes]
    mine_ref[...] = outs[2 * span + genes :]
    square = right.astype(jnp.float32)
    square = square * square
    high = square.astype(jnp.bfloat16)
    low = (square - high.astype(jnp.float32)).astype(jnp.bfloat16)
    ones = jnp.ones((16, right.shape[1]), jnp.bfloat16)
    total = lax.dot_general(ones, high, NT, preferred_element_type=jnp.float32)
    total += lax.dot_general(ones, low, NT, preferred_element_type=jnp.float32)
    fits = prod[width : width + deep]
    row = lax.broadcasted_iota(jnp.int32, fits.shape, 0)
    fits = jnp.where(row == covs + 1, total[:1], fits)
    send_ref[span : span + deep] = fits
    other_ref[span:] = fits


def product_shapes(parts, covs, genes, columns):
    span = genes * (parts // 2 - 1)
    rows = (span + covs + 8 + genes, span + covs + 8, genes)
    return [jax.ShapeDtypeStruct((r, columns), jnp.float32) for r in rows]


def first_products(sid, e, gt, dt, parts):
    rows, width = e.shape
    covs = dt.shape[0]
    columns = LANES + gt.shape[0]
    left = jax.ShapeDtypeStruct((width + covs + 16, rows), jnp.bfloat16)
    return call(
        functools.partial(first_kernel, parts, covs),
        [left] + product_shapes(parts, covs, width // parts, columns),
        "first_products",
        COST["products"],
        (sid, e, gt, dt),
        scratch=[pltpu.VMEM((width, rows), jnp.bfloat16)],
    )


def next_products(left, blocks, parts, covs, tokens):
    rows = left.shape[1]
    width = left.shape[0] - covs - 16
    columns = sum(b.shape[0] for b in blocks)
    return call(
        functools.partial(next_kernel, parts, covs, len(blocks)),
        product_shapes(parts, covs, width // parts, columns),
        "next_products",
        COST["products"],
        (left, *blocks, *tokens),
        scalars=0,
        tokens=len(tokens),
    )


def packed_rows(tall, columns):
    return tall + -(-tall // 16) * 8 if columns == LANES + LANES // 2 else 0


def pack(block):
    tall = block.shape[0]
    fold = -(-tall // 16) * 8
    rest = block[:, LANES:]
    rest = jnp.concatenate([rest, jnp.zeros((2 * fold - tall, LANES // 2), rest.dtype)], axis=0)
    return jnp.concatenate([block[:, :LANES], jnp.concatenate([rest[:fold], rest[fold:]], axis=1)], axis=0)


def unpack(block, tall):
    fold = -(-tall // 16) * 8
    rest = block[tall:]
    rest = jnp.concatenate([rest[:, : LANES // 2], rest[: tall - fold, LANES // 2 :]], axis=0)
    return jnp.concatenate([block[:tall], rest], axis=1)


def add_kernel(genes, deep, other_ref, came_ref, *out_refs):
    cuts = len(out_refs) * genes // (other_ref.shape[0] - deep)
    span = other_ref.shape[0] - deep
    for i in range(span // genes):
        start = i * genes
        total = other_ref[start : start + genes] + came_ref[start : start + genes]
        fits = other_ref[span:] + came_ref[span : span + deep]
        total = jnp.concatenate([total, fits], axis=0)
        if out_refs[i * cuts].shape[0] > genes + deep:
            total = pack(total)
        row = 0
        for out_ref in out_refs[i * cuts : (i + 1) * cuts]:
            out_ref[...] = total[row : row + out_ref.shape[0]]
            row += out_ref.shape[0]


def add_cores(other, came, genes, deep, cuts):
    chips = (other.shape[0] - deep) // genes
    tall = genes + deep
    dense = packed_rows(tall, other.shape[1])
    if dense:
        heights, columns, cuts = [dense], LANES, 1
    else:
        heights, columns = [tall] if cuts == 1 else [tall // 16 * 8, tall - tall // 16 * 8], other.shape[1]
    shapes = [jax.ShapeDtypeStruct((h, columns), jnp.float32) for h in heights]
    out = call(
        functools.partial(add_kernel, genes, deep),
        shapes * chips,
        "add_cores",
        COST["add"],
        (other, came),
        scalars=0,
    )
    return [out[i * cuts : (i + 1) * cuts] for i in range(chips)]


def chunk_sums(genes, deep, mine_ref, came_ref, refs):
    tall = genes + deep
    blocks, rows = [], []
    for ref in refs:
        rows.append(unpack(ref[...], tall) if ref.shape[0] > tall else ref[...])
        if sum(r.shape[0] for r in rows) == tall:
            blocks.append(jnp.concatenate(rows, axis=0) if len(rows) > 1 else rows[0])
            rows = []
    corr = mine_ref[...] + came_ref[came_ref.shape[0] - genes :]
    fits = blocks[0][genes:]
    for block in blocks[1:]:
        corr = corr + block[:genes]
        fits = fits + block[genes:]
    return corr, fits


def solve_kernel(covs, dof, weight_ref, mine_ref, came_ref, *rest):
    refs, (bins_ref, folds_ref, solved_ref, scale_ref) = rest[:-4], rest[-4:]
    genes = mine_ref.shape[0]
    rank, deep = covs + 1, covs + 8
    corr, fits = chunk_sums(genes, deep, mine_ref, came_ref, refs)
    cross, gram = corr[:, :LANES], fits[:, :LANES]
    row = lax.broadcasted_iota(jnp.int32, gram.shape, 0)
    lane = lax.broadcasted_iota(jnp.int32, gram.shape, 1)
    inside = jnp.logical_and(row < rank, lane < rank)
    a = jnp.where(inside, gram, jnp.where(row == lane, 1.0, 0.0))
    for k in range(0, rank, 2):
        down0 = jnp.broadcast_to(a[:, k : k + 1], a.shape)
        down1 = jnp.broadcast_to(a[:, k + 1 : k + 2], a.shape)
        p00, p01, p11 = down0[k : k + 1], down1[k : k + 1], down1[k + 1 : k + 2]
        inv = 1.0 / (p00 * p11 - p01 * p01)
        q00, q01, q11 = p11 * inv, -p01 * inv, p00 * inv
        row0, row1 = a[k : k + 1], a[k + 1 : k + 2]
        first = q00 * row0 + q01 * row1
        second = q01 * row0 + q11 * row1
        swept = a - down0 * first - down1 * second
        swept = jnp.where(lane == k, down0 * q00 + down1 * q01, swept)
        swept = jnp.where(lane == k + 1, down0 * q01 + down1 * q11, swept)
        first = jnp.where(lane[:1] == k, -q00, jnp.where(lane[:1] == k + 1, -q01, first))
        second = jnp.where(lane[:1] == k, -q01, jnp.where(lane[:1] == k + 1, -q11, second))
        a = jnp.where(row == k, first, jnp.where(row == k + 1, second, swept))
    inverse = jnp.where(inside, -a, 0.0)
    lane = lax.broadcasted_iota(jnp.int32, cross.shape, 1)
    squares = jnp.sum(jnp.where(lane == rank, cross, 0.0), axis=1, keepdims=True)
    cross = jnp.where(lane < rank, cross, 0.0)
    beta = lax.dot_general(cross, inverse, NT, precision=HIGHEST, preferred_element_type=jnp.float32)
    norm = squares - jnp.sum(beta * cross[:, :deep], axis=1, keepdims=True)
    norm = jnp.maximum(norm, 1e-06 * squares) + EPS
    solved_ref[:genes] = beta
    solved_ref[genes:] = inverse[:, :deep]

    bins, folds = bins_ref[...], folds_ref[...]
    tile = jnp.zeros(bins.shape, jnp.float32)
    for b in range(weight_ref.shape[1]):
        of_bin = jnp.zeros(folds.shape, jnp.float32)
        for f in range(weight_ref.shape[0]):
            of_bin = jnp.where(folds == f, weight_ref[f, b], of_bin)
        tile = jnp.where(bins == b, of_bin, tile)
    tile = tile.T * (dof / norm)
    width = scale_ref.shape[1] // tile.shape[1]
    for t in range(0, tile.shape[1], 2):
        pair = [jnp.broadcast_to(tile[:, i : i + 1], (genes, width)) for i in (t, t + 1)]
        scale_ref[:, t * width : (t + 2) * width] = jnp.concatenate(pair, axis=1)


def solve(weights, mine, came, swapped, bins, folds, covs, dof, variants):
    genes = mine.shape[0]
    outs = [
        jax.ShapeDtypeStruct((genes + covs + 8, covs + 8), jnp.float32),
        jax.ShapeDtypeStruct((genes, variants), jnp.float32),
    ]
    return call(
        functools.partial(solve_kernel, covs, dof),
        outs,
        "solve",
        COST["solve"],
        (weights, mine, came, *swapped, bins, folds),
    )


def fitted_stat(covs, skip, solved_ref, mine_ref, came_ref, refs):
    genes = mine_ref.shape[0]
    corr, fits = chunk_sums(genes, covs + 8, mine_ref, came_ref, refs)
    corr, fits = corr[:, skip:], fits[:, skip:]
    row = lax.broadcasted_iota(jnp.int32, fits.shape, 0)
    squares = fits[covs + 1 : covs + 2]
    fits = jnp.where(row <= covs, fits, 0.0)
    both = lax.dot_general(solved_ref[...], fits, NN, precision=HIGHEST, preferred_element_type=jnp.float32)
    norm = squares - jnp.sum(both[genes:] * fits, axis=0, keepdims=True)
    norm = jnp.maximum(norm, 1e-06 * squares) + EPS
    corr = corr - both[:genes]
    return corr * corr * (1.0 / norm)


def stat_kernel(covs, skip, solved_ref, mine_ref, came_ref, *rest):
    rest[-1][...] = fitted_stat(covs, skip, solved_ref, mine_ref, came_ref, rest[:-1])


def chunk_stat(solved, mine, came, swapped, covs, skip):
    return call(
        functools.partial(stat_kernel, covs, skip),
        jax.ShapeDtypeStruct((mine.shape[0], mine.shape[1] - skip), jnp.float32),
        "chunk_stat",
        COST["stat"],
        (solved, mine, came, *swapped),
        scalars=0,
    )


def slot_of(index, here, ring, order):
    position = {block: i for i, block in enumerate(order)}
    mine = jnp.int32(0)
    for block in range(ring):
        mine = jnp.where(here == block, position[block], mine)
    return lax.rem(position[index] - mine + ring, ring)


def place_kernel(ring, order, here_ref, scale_ref, *rest):
    stats, (out_ref, held) = rest[:-2], rest[-2:]
    variants = held.shape[2]
    held[ring // 2] = jnp.zeros_like(held[0])
    for k, stat in enumerate(stats):
        if k == 0:
            held[0] = stat[...]
        else:
            held[ring - k] = stat[:, :variants]
            held[k] = stat[:, variants:]
    group = LANES // math.gcd(variants, LANES)
    for j in range(0, ring, group):
        pieces = [held[slot_of(j + b, here_ref[0], ring, order)] for b in range(group)]
        span = slice(j * variants, (j + group) * variants)
        out_ref[:, span] = jnp.concatenate(pieces, axis=1) * scale_ref[:, span]


def place(here, scale, stats, ring, order):
    genes, total = scale.shape
    return call(
        functools.partial(place_kernel, ring, order),
        jax.ShapeDtypeStruct(scale.shape, jnp.float32),
        "place",
        COST["place"],
        (here, scale, *stats),
        scratch=[pltpu.VMEM((ring, genes, total // ring), jnp.float32)],
    )


def finish_kernel(covs, ring, order, here_ref, solved_ref, scale_ref, placed_ref, mine_ref, came_ref, *rest):
    out_ref = rest[-1]
    variants = mine_ref.shape[1]
    group = LANES // math.gcd(variants, LANES)
    width = group * variants
    stat = fitted_stat(covs, 0, solved_ref, mine_ref, came_ref, rest[:-1])
    out_ref[...] = placed_ref[...]
    index = jnp.int32(0)
    for block in range(ring):
        index = jnp.where(slot_of(block, here_ref[0], ring, order) == ring // 2, block, index)
    span = pl.ds(pl.multiple_of(index // group * width, LANES), width)
    stat = jnp.concatenate([stat] * group, axis=1)
    lane = lax.broadcasted_iota(jnp.int32, stat.shape, 1)
    first = lax.rem(index, group) * variants
    inside = jnp.logical_and(lane >= first, lane < first + variants)
    out_ref[:, span] = jnp.where(inside, stat * scale_ref[:, span], placed_ref[:, span])


def finish(here, solved, scale, placed, last, covs, ring, order):
    return call(
        functools.partial(finish_kernel, covs, ring, order),
        jax.ShapeDtypeStruct(scale.shape, jnp.float32),
        "finish",
        COST["finish"],
        (here, solved, scale, placed, *last),
    )


def shards(order, expression, genotypes, covariates, distance_bins, gene_folds, fold_weights):
    parts, ring = lax.axis_size("samp"), lax.axis_size("var")
    rows, width = expression.shape
    covs = covariates.shape[1]
    genes = width // parts
    deep = covs + 8
    dof = float(rows * parts - covs - 2)
    gt = genotypes.T
    variants = gt.shape[0]
    middle = ring // 2
    sid = lax.axis_index("samp").astype(jnp.int32)[None]
    here = lax.axis_index("var").astype(jnp.int32)[None]

    def exchange(x, d):
        return lax.ppermute(x, "samp", [(s, s ^ d) for s in range(parts)])

    forward = [(order[i], order[(i + 1) % ring]) for i in range(ring)]
    backward = [(b, a) for a, b in forward]

    def right(x):
        return lax.ppermute(x, "var", forward)

    def left(x):
        return lax.ppermute(x, "var", backward)

    stats = []
    lhs = solved = scale = None

    done = {}

    def after(*names):
        return [done[name] for name in names if name in done]

    block = (gt, gt)
    for k in range(middle + 1):
        if k > 0 and True:
            block = gate(block, after(*{3: (('sent', 2),)}.get(k, ())))
        if k < middle - 1:
            ahead = (right(block[0]), left(block[-1]))
        elif k == middle - 1:
            ahead = (right(block[0][: variants // 2]), left(block[-1][variants // 2 :]))
        if k == 0:
            lhs, send, other, mine = first_products(sid, expression, gt, covariates.T, parts)
        else:
            tokens = after(*{2: (('got', 0), ('came', 1)), 3: (('got', 1), ('sent', 2)), 4: (('sent', 3), ('got', 2))}.get(k, ()))
            send, other, mine = next_products(lhs, block, parts, covs, tokens)
        came = exchange(send, 1)
        sent = add_cores(other, came, genes, deep, 2 if k in () else 1)
        got = [[exchange(x, 2 * (i + 1)) for x in cut] for i, cut in enumerate(sent)]
        swapped = [*sent[0], *sum(got, [])]
        done["came", k], done["sent", k] = came, sent[0][0]
        done["got", k], done["rest", k] = got[-1][0], got[-1][-1]
        if k == 0:
            solved, scale = solve(
                fold_weights, mine, came, swapped, distance_bins, gene_folds[None], covs, dof, ring * variants
            )
            done["solved", 0] = solved
        if k < middle:
            stats.append(chunk_stat(solved, mine, came, swapped, covs, LANES if k == 0 else 0))
            done["stat", k] = stats[k]
            block = ahead
    placed = place(here, scale, stats, ring, tuple(order))
    return finish(here, solved, scale, placed, (mine, came, *swapped), covs, ring, tuple(order))


def solution(mesh):
    return jax.shard_map(
        functools.partial(shards, ring_order(mesh)),
        mesh=mesh,
        in_specs=(
            P(("groups", "samp"), "var"),
            P(("groups", "samp"), "var"),
            P(("groups", "samp"), None),
            P("groups", ("var", "samp")),
            P(("groups", "var", "samp")),
            P(),
        ),
        out_specs=P(("groups", "var", "samp"), None),
        check_vma=False,
    )
```

```python
import functools
import math

import jax
import jax.numpy as jnp
from jax import lax
from jax.experimental import pallas as pl
from jax.experimental.pallas import tpu as pltpu
from jax.sharding import PartitionSpec as P

LANES = 128
EPS = 1e-06
COST = {'products': 100000000, 'add': 1, 'solve': 100000000, 'stat': 100000000, 'place': 1, 'finish': 1}
VMEM_LIMIT = 10 * 1024 * 1024

NT = (((1,), (1,)), ((), ()))
NN = (((1,), (0,)), ((), ()))
HIGHEST = lax.Precision.HIGHEST


def ring_order(mesh):
    members = list(mesh.devices[0, 0])
    places = [getattr(device, "coords", None) for device in members]
    if len(members) < 2 or any(place is None for place in places):
        return list(range(len(members)))
    axis = [i for i in range(len(places[0])) if places[0][i] != places[1][i]][0]
    columns = {}
    for index, place in enumerate(places):
        columns.setdefault(place[axis], []).append(index)
    order = []
    for step, key in enumerate(sorted(columns)):
        order += columns[key] if step % 2 == 0 else columns[key][::-1]
    return order


def call(kernel, out_shape, name, flops, operands, scratch=(), scalars=1, tokens=0):
    vmem = pl.BlockSpec(memory_space=pltpu.VMEM)
    smem = pl.BlockSpec(memory_space=pltpu.SMEM)
    rest = len(operands) - scalars - tokens
    return pl.pallas_call(
        kernel,
        out_shape=out_shape,
        in_specs=[smem] * scalars + [vmem] * rest + [pl.BlockSpec(memory_space=pl.ANY)] * tokens,
        out_specs=jax.tree.map(lambda _: vmem, out_shape),
        scratch_shapes=list(scratch),
        compiler_params=pltpu.CompilerParams(vmem_limit_bytes=VMEM_LIMIT),
        cost_estimate=pl.CostEstimate(flops=flops, bytes_accessed=0, transcendentals=0),
        name=name,
    )(*operands)


def first_kernel(parts, covs, sid_ref, e_ref, gt_ref, dt_ref, left_ref, send_ref, other_ref, mine_ref, wide):
    width = e_ref.shape[1]
    genes = width // parts
    sid = sid_ref[0]
    wide[...] = e_ref[...].T
    owners = [sid ^ 1 ^ d for d in range(2, parts, 2)] + [sid ^ 1]
    owners += [sid ^ d for d in range(2, parts, 2)] + [sid]
    for i, owner in enumerate(owners):
        start = pl.multiple_of(owner * genes, 16)
        left_ref[i * genes : (i + 1) * genes] = wide[pl.ds(start, genes), :]
    rows = dt_ref.shape[1]
    left_ref[width : width + covs] = dt_ref[...]
    first = lax.broadcasted_iota(jnp.int32, (16, rows), 0) == 0
    left_ref[width + covs :] = first.astype(jnp.float32).astype(jnp.bfloat16)
    design = left_ref[width:]
    right = jnp.concatenate([design, jnp.zeros((LANES - design.shape[0], rows), jnp.bfloat16)], axis=0)
    right = jnp.concatenate([right, gt_ref[...]], axis=0)
    split(parts, covs, genes, left_ref, right, send_ref, other_ref, mine_ref, True)


def next_kernel(parts, covs, blocks, left_ref, *rest):
    right = jnp.concatenate([ref[...] for ref in rest[:blocks]], axis=0)
    send_ref, other_ref, mine_ref = rest[-3:]
    genes = mine_ref.shape[0]
    split(parts, covs, genes, left_ref, right, send_ref, other_ref, mine_ref, False)


def split(parts, covs, genes, left_ref, right, send_ref, other_ref, mine_ref, squares):
    width = genes * parts
    span = genes * (parts // 2 - 1)
    deep = covs + 8

    prod = lax.dot_general(left_ref[...], right, NT, preferred_element_type=jnp.float32)
    outs = prod[:width]
    if squares:
        a = left_ref[:width].astype(jnp.float32)
        lane = lax.broadcasted_iota(jnp.int32, outs.shape, 1)
        outs = jnp.where(lane == covs + 1, jnp.sum(a * a, axis=1, keepdims=True), outs)
    send_ref[:span] = outs[:span]
    send_ref[span + deep :] = outs[span : span + genes]
    other_ref[:span] = outs[span + genes : 2 * span + genes]
    mine_ref[...] = outs[2 * span + genes :]
    square = right.astype(jnp.float32)
    square = square * square
    high = square.astype(jnp.bfloat16)
    low = (square - high.astype(jnp.float32)).astype(jnp.bfloat16)
    ones = jnp.ones((16, right.shape[1]), jnp.bfloat16)
    total = lax.dot_general(ones, high, NT, preferred_element_type=jnp.float32)
    total += lax.dot_general(ones, low, NT, preferred_element_type=jnp.float32)
    fits = prod[width : width + deep]
    row = lax.broadcasted_iota(jnp.int32, fits.shape, 0)
    fits = jnp.where(row == covs + 1, total[:1], fits)
    send_ref[span : span + deep] = fits
    other_ref[span:] = fits


def product_shapes(parts, covs, genes, columns):
    span = genes * (parts // 2 - 1)
    rows = (span + covs + 8 + genes, span + covs + 8, genes)
    return [jax.ShapeDtypeStruct((r, columns), jnp.float32) for r in rows]


def first_products(sid, e, gt, dt, parts):
    rows, width = e.shape
    covs = dt.shape[0]
    columns = LANES + gt.shape[0]
    left = jax.ShapeDtypeStruct((width + covs + 16, rows), jnp.bfloat16)
    return call(
        functools.partial(first_kernel, parts, covs),
        [left] + product_shapes(parts, covs, width // parts, columns),
        "first_products",
        COST["products"],
        (sid, e, gt, dt),
        scratch=[pltpu.VMEM((width, rows), jnp.bfloat16)],
    )


def next_products(left, blocks, parts, covs, tokens):
    rows = left.shape[1]
    width = left.shape[0] - covs - 16
    columns = sum(b.shape[0] for b in blocks)
    return call(
        functools.partial(next_kernel, parts, covs, len(blocks)),
        product_shapes(parts, covs, width // parts, columns),
        "next_products",
        COST["products"],
        (left, *blocks, *tokens),
        scalars=0,
        tokens=len(tokens),
    )


def packed_rows(tall, columns):
    return tall + -(-tall // 16) * 8 if columns == LANES + LANES // 2 else 0


def pack(block):
    tall = block.shape[0]
    fold = -(-tall // 16) * 8
    rest = block[:, LANES:]
    rest = jnp.concatenate([rest, jnp.zeros((2 * fold - tall, LANES // 2), rest.dtype)], axis=0)
    return jnp.concatenate([block[:, :LANES], jnp.concatenate([rest[:fold], rest[fold:]], axis=1)], axis=0)


def unpack(block, tall):
    fold = -(-tall // 16) * 8
    rest = block[tall:]
    rest = jnp.concatenate([rest[:, : LANES // 2], rest[: tall - fold, LANES // 2 :]], axis=0)
    return jnp.concatenate([block[:tall], rest], axis=1)


def add_kernel(genes, deep, other_ref, came_ref, *out_refs):
    cuts = len(out_refs) * genes // (other_ref.shape[0] - deep)
    span = other_ref.shape[0] - deep
    for i in range(span // genes):
        start = i * genes
        total = other_ref[start : start + genes] + came_ref[start : start + genes]
        fits = other_ref[span:] + came_ref[span : span + deep]
        total = jnp.concatenate([total, fits], axis=0)
        if out_refs[i * cuts].shape[0] > genes + deep:
            total = pack(total)
        row = 0
        for out_ref in out_refs[i * cuts : (i + 1) * cuts]:
            out_ref[...] = total[row : row + out_ref.shape[0]]
            row += out_ref.shape[0]


def add_cores(other, came, genes, deep, cuts):
    chips = (other.shape[0] - deep) // genes
    tall = genes + deep
    dense = packed_rows(tall, other.shape[1])
    if dense:
        heights, columns, cuts = [dense], LANES, 1
    else:
        heights, columns = [tall] if cuts == 1 else [tall // 16 * 8, tall - tall // 16 * 8], other.shape[1]
    shapes = [jax.ShapeDtypeStruct((h, columns), jnp.float32) for h in heights]
    out = call(
        functools.partial(add_kernel, genes, deep),
        shapes * chips,
        "add_cores",
        COST["add"],
        (other, came),
        scalars=0,
    )
    return [out[i * cuts : (i + 1) * cuts] for i in range(chips)]


def chunk_sums(genes, deep, mine_ref, came_ref, refs):
    tall = genes + deep
    blocks, rows = [], []
    for ref in refs:
        rows.append(unpack(ref[...], tall) if ref.shape[0] > tall else ref[...])
        if sum(r.shape[0] for r in rows) == tall:
            blocks.append(jnp.concatenate(rows, axis=0) if len(rows) > 1 else rows[0])
            rows = []
    corr = mine_ref[...] + came_ref[came_ref.shape[0] - genes :]
    fits = blocks[0][genes:]
    for block in blocks[1:]:
        corr = corr + block[:genes]
        fits = fits + block[genes:]
    return corr, fits


def solve_kernel(covs, dof, weight_ref, mine_ref, came_ref, *rest):
    refs, (bins_ref, folds_ref, solved_ref, scale_ref) = rest[:-4], rest[-4:]
    genes = mine_ref.shape[0]
    rank, deep = covs + 1, covs + 8
    corr, fits = chunk_sums(genes, deep, mine_ref, came_ref, refs)
    cross, gram = corr[:, :LANES], fits[:, :LANES]
    row = lax.broadcasted_iota(jnp.int32, gram.shape, 0)
    lane = lax.broadcasted_iota(jnp.int32, gram.shape, 1)
    inside = jnp.logical_and(row < rank, lane < rank)
    a = jnp.where(inside, gram, jnp.where(row == lane, 1.0, 0.0))
    for k in range(0, rank, 2):
        down0 = jnp.broadcast_to(a[:, k : k + 1], a.shape)
        down1 = jnp.broadcast_to(a[:, k + 1 : k + 2], a.shape)
        p00, p01, p11 = down0[k : k + 1], down1[k : k + 1], down1[k + 1 : k + 2]
        inv = 1.0 / (p00 * p11 - p01 * p01)
        q00, q01, q11 = p11 * inv, -p01 * inv, p00 * inv
        row0, row1 = a[k : k + 1], a[k + 1 : k + 2]
        first = q00 * row0 + q01 * row1
        second = q01 * row0 + q11 * row1
        swept = a - down0 * first - down1 * second
        swept = jnp.where(lane == k, down0 * q00 + down1 * q01, swept)
        swept = jnp.where(lane == k + 1, down0 * q01 + down1 * q11, swept)
        first = jnp.where(lane[:1] == k, -q00, jnp.where(lane[:1] == k + 1, -q01, first))
        second = jnp.where(lane[:1] == k, -q01, jnp.where(lane[:1] == k + 1, -q11, second))
        a = jnp.where(row == k, first, jnp.where(row == k + 1, second, swept))
    inverse = jnp.where(inside, -a, 0.0)
    lane = lax.broadcasted_iota(jnp.int32, cross.shape, 1)
    squares = jnp.sum(jnp.where(lane == rank, cross, 0.0), axis=1, keepdims=True)
    cross = jnp.where(lane < rank, cross, 0.0)
    beta = lax.dot_general(cross, inverse, NT, precision=HIGHEST, preferred_element_type=jnp.float32)
    norm = squares - jnp.sum(beta * cross[:, :deep], axis=1, keepdims=True)
    norm = jnp.maximum(norm, 1e-06 * squares) + EPS
    solved_ref[:genes] = beta
    solved_ref[genes:] = inverse[:, :deep]

    bins, folds = bins_ref[...], folds_ref[...]
    tile = jnp.zeros(bins.shape, jnp.float32)
    for b in range(weight_ref.shape[1]):
        of_bin = jnp.zeros(folds.shape, jnp.float32)
        for f in range(weight_ref.shape[0]):
            of_bin = jnp.where(folds == f, weight_ref[f, b], of_bin)
        tile = jnp.where(bins == b, of_bin, tile)
    tile = tile.T * (dof / norm)
    width = scale_ref.shape[1] // tile.shape[1]
    for t in range(0, tile.shape[1], 2):
        pair = [jnp.broadcast_to(tile[:, i : i + 1], (genes, width)) for i in (t, t + 1)]
        scale_ref[:, t * width : (t + 2) * width] = jnp.concatenate(pair, axis=1)


def solve(weights, mine, came, swapped, bins, folds, covs, dof, variants):
    genes = mine.shape[0]
    outs = [
        jax.ShapeDtypeStruct((genes + covs + 8, covs + 8), jnp.float32),
        jax.ShapeDtypeStruct((genes, variants), jnp.float32),
    ]
    return call(
        functools.partial(solve_kernel, covs, dof),
        outs,
        "solve",
        COST["solve"],
        (weights, mine, came, *swapped, bins, folds),
    )


def fitted_stat(covs, skip, solved_ref, mine_ref, came_ref, refs):
    genes = mine_ref.shape[0]
    corr, fits = chunk_sums(genes, covs + 8, mine_ref, came_ref, refs)
    corr, fits = corr[:, skip:], fits[:, skip:]
    row = lax.broadcasted_iota(jnp.int32, fits.shape, 0)
    squares = fits[covs + 1 : covs + 2]
    fits = jnp.where(row <= covs, fits, 0.0)
    both = lax.dot_general(solved_ref[...], fits, NN, precision=HIGHEST, preferred_element_type=jnp.float32)
    norm = squares - jnp.sum(both[genes:] * fits, axis=0, keepdims=True)
    norm = jnp.maximum(norm, 1e-06 * squares) + EPS
    corr = corr - both[:genes]
    return corr * corr * (1.0 / norm)


def stat_kernel(covs, skip, solved_ref, mine_ref, came_ref, *rest):
    rest[-1][...] = fitted_stat(covs, skip, solved_ref, mine_ref, came_ref, rest[:-1])


def chunk_stat(solved, mine, came, swapped, covs, skip):
    return call(
        functools.partial(stat_kernel, covs, skip),
        jax.ShapeDtypeStruct((mine.shape[0], mine.shape[1] - skip), jnp.float32),
        "chunk_stat",
        COST["stat"],
        (solved, mine, came, *swapped),
        scalars=0,
    )


def slot_of(index, here, ring, order):
    position = {block: i for i, block in enumerate(order)}
    mine = jnp.int32(0)
    for block in range(ring):
        mine = jnp.where(here == block, position[block], mine)
    return lax.rem(position[index] - mine + ring, ring)


def place_kernel(ring, order, here_ref, scale_ref, *rest):
    stats, (out_ref, held) = rest[:-2], rest[-2:]
    variants = held.shape[2]
    held[ring // 2] = jnp.zeros_like(held[0])
    for k, stat in enumerate(stats):
        if k == 0:
            held[0] = stat[...]
        else:
            held[ring - k] = stat[:, :variants]
            held[k] = stat[:, variants:]
    group = LANES // math.gcd(variants, LANES)
    for j in range(0, ring, group):
        pieces = [held[slot_of(j + b, here_ref[0], ring, order)] for b in range(group)]
        span = slice(j * variants, (j + group) * variants)
        out_ref[:, span] = jnp.concatenate(pieces, axis=1) * scale_ref[:, span]


def place(here, scale, stats, ring, order):
    genes, total = scale.shape
    return call(
        functools.partial(place_kernel, ring, order),
        jax.ShapeDtypeStruct(scale.shape, jnp.float32),
        "place",
        COST["place"],
        (here, scale, *stats),
        scratch=[pltpu.VMEM((ring, genes, total // ring), jnp.float32)],
    )


def finish_kernel(covs, ring, order, here_ref, solved_ref, scale_ref, placed_ref, mine_ref, came_ref, *rest):
    out_ref = rest[-1]
    variants = mine_ref.shape[1]
    group = LANES // math.gcd(variants, LANES)
    width = group * variants
    stat = fitted_stat(covs, 0, solved_ref, mine_ref, came_ref, rest[:-1])
    out_ref[...] = placed_ref[...]
    index = jnp.int32(0)
    for block in range(ring):
        index = jnp.where(slot_of(block, here_ref[0], ring, order) == ring // 2, block, index)
    span = pl.ds(pl.multiple_of(index // group * width, LANES), width)
    stat = jnp.concatenate([stat] * group, axis=1)
    lane = lax.broadcasted_iota(jnp.int32, stat.shape, 1)
    first = lax.rem(index, group) * variants
    inside = jnp.logical_and(lane >= first, lane < first + variants)
    out_ref[:, span] = jnp.where(inside, stat * scale_ref[:, span], placed_ref[:, span])


def finish(here, solved, scale, placed, last, covs, ring, order):
    return call(
        functools.partial(finish_kernel, covs, ring, order),
        jax.ShapeDtypeStruct(scale.shape, jnp.float32),
        "finish",
        COST["finish"],
        (here, solved, scale, placed, *last),
    )


def shards(order, expression, genotypes, covariates, distance_bins, gene_folds, fold_weights):
    parts, ring = lax.axis_size("samp"), lax.axis_size("var")
    rows, width = expression.shape
    covs = covariates.shape[1]
    genes = width // parts
    deep = covs + 8
    dof = float(rows * parts - covs - 2)
    gt = genotypes.T
    variants = gt.shape[0]
    middle = ring // 2
    sid = lax.axis_index("samp").astype(jnp.int32)[None]
    here = lax.axis_index("var").astype(jnp.int32)[None]

    def exchange(x, d):
        return lax.ppermute(x, "samp", [(s, s ^ d) for s in range(parts)])

    forward = [(order[i], order[(i + 1) % ring]) for i in range(ring)]
    backward = [(b, a) for a, b in forward]

    def right(x):
        return lax.ppermute(x, "var", forward)

    def left(x):
        return lax.ppermute(x, "var", backward)

    stats = []
    lhs = solved = scale = None

    done = {}

    def after(*names):
        return [done[name] for name in names if name in done]

    block = (gt, gt)
    for k in range(middle + 1):
        if k < middle - 1:
            ahead = (right(block[0]), left(block[-1]))
        elif k == middle - 1:
            ahead = (right(block[0][: variants // 2]), left(block[-1][variants // 2 :]))
        if k == 0:
            lhs, send, other, mine = first_products(sid, expression, gt, covariates.T, parts)
        else:
            tokens = after(("got", k - 2), *([("sent", k - 1)] if k == middle else []))
            send, other, mine = next_products(lhs, block, parts, covs, tokens)
        came = exchange(send, 1)
        sent = add_cores(other, came, genes, deep, 1)
        got = [[exchange(x, 2 * (i + 1)) for x in cut] for i, cut in enumerate(sent)]
        swapped = [*sent[0], *sum(got, [])]
        done["came", k], done["sent", k] = came, sent[0][0]
        done["got", k], done["rest", k] = got[-1][0], got[-1][-1]
        if k == 0:
            solved, scale = solve(
                fold_weights, mine, came, swapped, distance_bins, gene_folds[None], covs, dof, ring * variants
            )
            done["solved", 0] = solved
        if k < middle:
            stats.append(chunk_stat(solved, mine, came, swapped, covs, LANES if k == 0 else 0))
            done["stat", k] = stats[k]
            block = ahead
    placed = place(here, scale, stats, ring, tuple(order))
    return finish(here, solved, scale, placed, (mine, came, *swapped), covs, ring, tuple(order))


def solution(mesh):
    return jax.shard_map(
        functools.partial(shards, ring_order(mesh)),
        mesh=mesh,
        in_specs=(
            P(("groups", "samp"), "var"),
            P(("groups", "samp"), "var"),
            P(("groups", "samp"), None),
            P("groups", ("var", "samp")),
            P(("groups", "var", "samp")),
            P(),
        ),
        out_specs=P(("groups", "var", "samp"), None),
        check_vma=False,
    )
```

```python
import functools
import math

import jax
import jax.numpy as jnp
from jax import lax
from jax.experimental import pallas as pl
from jax.experimental.pallas import tpu as pltpu
from jax.sharding import PartitionSpec as P

LANES = 128
EPS = 1e-06
COST = {'products': 100000000, 'add': 1, 'solve': 100000000, 'stat': 100000000, 'place': 1, 'finish': 1}
VMEM_LIMIT = 10 * 1024 * 1024

NT = (((1,), (1,)), ((), ()))
NN = (((1,), (0,)), ((), ()))
HIGHEST = lax.Precision.HIGHEST


def ring_order(mesh):
    members = list(mesh.devices[0, 0])
    places = [getattr(device, "coords", None) for device in members]
    if len(members) < 2 or any(place is None for place in places):
        return list(range(len(members)))
    axis = [i for i in range(len(places[0])) if places[0][i] != places[1][i]][0]
    columns = {}
    for index, place in enumerate(places):
        columns.setdefault(place[axis], []).append(index)
    order = []
    for step, key in enumerate(sorted(columns)):
        order += columns[key] if step % 2 == 0 else columns[key][::-1]
    return order


def call(kernel, out_shape, name, flops, operands, scratch=(), scalars=1, tokens=0):
    vmem = pl.BlockSpec(memory_space=pltpu.VMEM)
    smem = pl.BlockSpec(memory_space=pltpu.SMEM)
    rest = len(operands) - scalars - tokens
    return pl.pallas_call(
        kernel,
        out_shape=out_shape,
        in_specs=[smem] * scalars + [vmem] * rest + [pl.BlockSpec(memory_space=pl.ANY)] * tokens,
        out_specs=jax.tree.map(lambda _: vmem, out_shape),
        scratch_shapes=list(scratch),
        compiler_params=pltpu.CompilerParams(vmem_limit_bytes=VMEM_LIMIT),
        cost_estimate=pl.CostEstimate(flops=flops, bytes_accessed=0, transcendentals=0),
        name=name,
    )(*operands)


def first_kernel(parts, covs, ids_ref, e_ref, gt_ref, dt_ref, left_ref, send_ref, other_ref, mine_ref, wide):
    width = e_ref.shape[1]
    genes = width // parts
    sid = ids_ref[0]
    wide[...] = e_ref[...].T
    owners = [sid ^ 1 ^ d for d in range(2, parts, 2)] + [sid ^ 1]
    owners += [sid ^ d for d in range(2, parts, 2)] + [sid]
    for i, owner in enumerate(owners):
        start = pl.multiple_of(owner * genes, 16)
        left_ref[i * genes : (i + 1) * genes] = wide[pl.ds(start, genes), :]
    rows = dt_ref.shape[1]
    left_ref[width : width + covs] = dt_ref[...]
    first = lax.broadcasted_iota(jnp.int32, (16, rows), 0) == 0
    left_ref[width + covs :] = first.astype(jnp.float32).astype(jnp.bfloat16)
    design = left_ref[width:]
    right = jnp.concatenate([design, jnp.zeros((LANES - design.shape[0], rows), jnp.bfloat16)], axis=0)
    right = jnp.concatenate([right, gt_ref[...]], axis=0)
    split(parts, covs, genes, left_ref, right, send_ref, other_ref, mine_ref, True)


def next_kernel(parts, covs, blocks, left_ref, *rest):
    right = jnp.concatenate([ref[...] for ref in rest[:blocks]], axis=0)
    send_ref, other_ref, mine_ref = rest[-3:]
    genes = mine_ref.shape[0]
    split(parts, covs, genes, left_ref, right, send_ref, other_ref, mine_ref, False)


def split(parts, covs, genes, left_ref, right, send_ref, other_ref, mine_ref, squares):
    width = genes * parts
    span = genes * (parts // 2 - 1)
    deep = covs + 8

    prod = lax.dot_general(left_ref[...], right, NT, preferred_element_type=jnp.float32)
    outs = prod[:width]
    if squares:
        a = left_ref[:width].astype(jnp.float32)
        lane = lax.broadcasted_iota(jnp.int32, outs.shape, 1)
        outs = jnp.where(lane == covs + 1, jnp.sum(a * a, axis=1, keepdims=True), outs)
    send_ref[:span] = outs[:span]
    send_ref[span + deep :] = outs[span : span + genes]
    other_ref[:span] = outs[span + genes : 2 * span + genes]
    mine_ref[...] = outs[2 * span + genes :]
    square = right.astype(jnp.float32)
    square = square * square
    high = square.astype(jnp.bfloat16)
    low = (square - high.astype(jnp.float32)).astype(jnp.bfloat16)
    ones = jnp.ones((16, right.shape[1]), jnp.bfloat16)
    total = lax.dot_general(ones, high, NT, preferred_element_type=jnp.float32)
    total += lax.dot_general(ones, low, NT, preferred_element_type=jnp.float32)
    fits = prod[width : width + deep]
    row = lax.broadcasted_iota(jnp.int32, fits.shape, 0)
    fits = jnp.where(row == covs + 1, total[:1], fits)
    send_ref[span : span + deep] = fits
    other_ref[span:] = fits


def product_shapes(parts, covs, genes, columns):
    span = genes * (parts // 2 - 1)
    rows = (span + covs + 8 + genes, span + covs + 8, genes)
    return [jax.ShapeDtypeStruct((r, columns), jnp.float32) for r in rows]


def first_products(ids, e, gt, dt, parts):
    rows, width = e.shape
    covs = dt.shape[0]
    columns = LANES + gt.shape[0]
    left = jax.ShapeDtypeStruct((width + covs + 16, rows), jnp.bfloat16)
    return call(
        functools.partial(first_kernel, parts, covs),
        [left] + product_shapes(parts, covs, width // parts, columns),
        "first_products",
        COST["products"],
        (ids, e, gt, dt),
        scratch=[pltpu.VMEM((width, rows), jnp.bfloat16)],
    )


def next_products(left, blocks, parts, covs, tokens):
    rows = left.shape[1]
    width = left.shape[0] - covs - 16
    columns = sum(b.shape[0] for b in blocks)
    return call(
        functools.partial(next_kernel, parts, covs, len(blocks)),
        product_shapes(parts, covs, width // parts, columns),
        "next_products",
        COST["products"],
        (left, *blocks, *tokens),
        scalars=0,
        tokens=len(tokens),
    )


def packed_rows(tall, columns):
    return tall + -(-tall // 16) * 8 if columns == LANES + LANES // 2 else 0


def pack(block):
    tall = block.shape[0]
    fold = -(-tall // 16) * 8
    rest = block[:, LANES:]
    rest = jnp.concatenate([rest, jnp.zeros((2 * fold - tall, LANES // 2), rest.dtype)], axis=0)
    return jnp.concatenate([block[:, :LANES], jnp.concatenate([rest[:fold], rest[fold:]], axis=1)], axis=0)


def unpack(block, tall):
    fold = -(-tall // 16) * 8
    rest = block[tall:]
    rest = jnp.concatenate([rest[:, : LANES // 2], rest[: tall - fold, LANES // 2 :]], axis=0)
    return jnp.concatenate([block[:tall], rest], axis=1)


def add_kernel(genes, deep, other_ref, came_ref, *out_refs):
    cuts = len(out_refs) * genes // (other_ref.shape[0] - deep)
    span = other_ref.shape[0] - deep
    for i in range(span // genes):
        start = i * genes
        total = other_ref[start : start + genes] + came_ref[start : start + genes]
        fits = other_ref[span:] + came_ref[span : span + deep]
        total = jnp.concatenate([total, fits], axis=0)
        if out_refs[i * cuts].shape[0] > genes + deep:
            total = pack(total)
        row = 0
        for out_ref in out_refs[i * cuts : (i + 1) * cuts]:
            out_ref[...] = total[row : row + out_ref.shape[0]]
            row += out_ref.shape[0]


def add_cores(other, came, genes, deep, cuts):
    chips = (other.shape[0] - deep) // genes
    tall = genes + deep
    dense = packed_rows(tall, other.shape[1])
    if dense:
        heights, columns, cuts = [dense], LANES, 1
    else:
        heights, columns = [tall] if cuts == 1 else [tall // 16 * 8, tall - tall // 16 * 8], other.shape[1]
    shapes = [jax.ShapeDtypeStruct((h, columns), jnp.float32) for h in heights]
    out = call(
        functools.partial(add_kernel, genes, deep),
        shapes * chips,
        "add_cores",
        COST["add"],
        (other, came),
        scalars=0,
    )
    return [out[i * cuts : (i + 1) * cuts] for i in range(chips)]


def chunk_sums(genes, deep, mine_ref, came_ref, refs):
    tall = genes + deep
    blocks, rows = [], []
    for ref in refs:
        rows.append(unpack(ref[...], tall) if ref.shape[0] > tall else ref[...])
        if sum(r.shape[0] for r in rows) == tall:
            blocks.append(jnp.concatenate(rows, axis=0) if len(rows) > 1 else rows[0])
            rows = []
    corr = mine_ref[...] + came_ref[came_ref.shape[0] - genes :]
    fits = blocks[0][genes:]
    for block in blocks[1:]:
        corr = corr + block[:genes]
        fits = fits + block[genes:]
    return corr, fits


def solve_kernel(covs, dof, weight_ref, mine_ref, came_ref, *rest):
    refs, (bins_ref, folds_ref, solved_ref, scale_ref) = rest[:-4], rest[-4:]
    genes = mine_ref.shape[0]
    rank, deep = covs + 1, covs + 8
    corr, fits = chunk_sums(genes, deep, mine_ref, came_ref, refs)
    cross, gram = corr[:, :LANES], fits[:, :LANES]
    row = lax.broadcasted_iota(jnp.int32, gram.shape, 0)
    lane = lax.broadcasted_iota(jnp.int32, gram.shape, 1)
    inside = jnp.logical_and(row < rank, lane < rank)
    a = jnp.where(inside, gram, jnp.where(row == lane, 1.0, 0.0))
    for k in range(0, rank, 2):
        down0 = jnp.broadcast_to(a[:, k : k + 1], a.shape)
        down1 = jnp.broadcast_to(a[:, k + 1 : k + 2], a.shape)
        p00, p01, p11 = down0[k : k + 1], down1[k : k + 1], down1[k + 1 : k + 2]
        inv = 1.0 / (p00 * p11 - p01 * p01)
        q00, q01, q11 = p11 * inv, -p01 * inv, p00 * inv
        row0, row1 = a[k : k + 1], a[k + 1 : k + 2]
        first = q00 * row0 + q01 * row1
        second = q01 * row0 + q11 * row1
        swept = a - down0 * first - down1 * second
        swept = jnp.where(lane == k, down0 * q00 + down1 * q01, swept)
        swept = jnp.where(lane == k + 1, down0 * q01 + down1 * q11, swept)
        first = jnp.where(lane[:1] == k, -q00, jnp.where(lane[:1] == k + 1, -q01, first))
        second = jnp.where(lane[:1] == k, -q01, jnp.where(lane[:1] == k + 1, -q11, second))
        a = jnp.where(row == k, first, jnp.where(row == k + 1, second, swept))
    inverse = jnp.where(inside, -a, 0.0)
    lane = lax.broadcasted_iota(jnp.int32, cross.shape, 1)
    squares = jnp.sum(jnp.where(lane == rank, cross, 0.0), axis=1, keepdims=True)
    cross = jnp.where(lane < rank, cross, 0.0)
    beta = lax.dot_general(cross, inverse, NT, precision=HIGHEST, preferred_element_type=jnp.float32)
    norm = squares - jnp.sum(beta * cross[:, :deep], axis=1, keepdims=True)
    norm = jnp.maximum(norm, 1e-06 * squares) + EPS
    solved_ref[:genes] = beta
    solved_ref[genes:] = inverse[:, :deep]

    bins, folds = bins_ref[...], folds_ref[...]
    tile = jnp.zeros(bins.shape, jnp.float32)
    for b in range(weight_ref.shape[1]):
        of_bin = jnp.zeros(folds.shape, jnp.float32)
        for f in range(weight_ref.shape[0]):
            of_bin = jnp.where(folds == f, weight_ref[f, b], of_bin)
        tile = jnp.where(bins == b, of_bin, tile)
    tile = tile.T * (dof / norm)
    width = scale_ref.shape[1] // tile.shape[1]
    for t in range(0, tile.shape[1], 2):
        pair = [jnp.broadcast_to(tile[:, i : i + 1], (genes, width)) for i in (t, t + 1)]
        scale_ref[:, t * width : (t + 2) * width] = jnp.concatenate(pair, axis=1)


def solve(weights, mine, came, swapped, bins, folds, covs, dof, variants):
    genes = mine.shape[0]
    outs = [
        jax.ShapeDtypeStruct((genes + covs + 8, covs + 8), jnp.float32),
        jax.ShapeDtypeStruct((genes, variants), jnp.float32),
    ]
    return call(
        functools.partial(solve_kernel, covs, dof),
        outs,
        "solve",
        COST["solve"],
        (weights, mine, came, *swapped, bins, folds),
    )


def fitted_stat(covs, skip, solved_ref, mine_ref, came_ref, refs):
    genes = mine_ref.shape[0]
    corr, fits = chunk_sums(genes, covs + 8, mine_ref, came_ref, refs)
    corr, fits = corr[:, skip:], fits[:, skip:]
    row = lax.broadcasted_iota(jnp.int32, fits.shape, 0)
    squares = fits[covs + 1 : covs + 2]
    fits = jnp.where(row <= covs, fits, 0.0)
    both = lax.dot_general(solved_ref[...], fits, NN, precision=HIGHEST, preferred_element_type=jnp.float32)
    norm = squares - jnp.sum(both[genes:] * fits, axis=0, keepdims=True)
    norm = jnp.maximum(norm, 1e-06 * squares) + EPS
    corr = corr - both[:genes]
    return corr * corr * (1.0 / norm)


def stat_kernel(covs, skip, solved_ref, mine_ref, came_ref, *rest):
    rest[-1][...] = fitted_stat(covs, skip, solved_ref, mine_ref, came_ref, rest[:-1])


def chunk_stat(solved, mine, came, swapped, covs, skip):
    return call(
        functools.partial(stat_kernel, covs, skip),
        jax.ShapeDtypeStruct((mine.shape[0], mine.shape[1] - skip), jnp.float32),
        "chunk_stat",
        COST["stat"],
        (solved, mine, came, *swapped),
        scalars=0,
    )


def slot_of(index, here, ring, order):
    position = {block: i for i, block in enumerate(order)}
    mine = jnp.int32(0)
    for block in range(ring):
        mine = jnp.where(here == block, position[block], mine)
    return lax.rem(position[index] - mine + ring, ring)


def place_kernel(ring, order, ids_ref, scale_ref, *rest):
    stats, (out_ref, held) = rest[:-2], rest[-2:]
    variants = held.shape[2]
    held[ring // 2] = jnp.zeros_like(held[0])
    for k, stat in enumerate(stats):
        if k == 0:
            held[0] = stat[...]
        else:
            held[ring - k] = stat[:, :variants]
            held[k] = stat[:, variants:]
    group = LANES // math.gcd(variants, LANES)
    for j in range(0, ring, group):
        pieces = [held[slot_of(j + b, ids_ref[1], ring, order)] for b in range(group)]
        span = slice(j * variants, (j + group) * variants)
        out_ref[:, span] = jnp.concatenate(pieces, axis=1) * scale_ref[:, span]


def place(ids, scale, stats, ring, order):
    genes, total = scale.shape
    return call(
        functools.partial(place_kernel, ring, order),
        jax.ShapeDtypeStruct(scale.shape, jnp.float32),
        "place",
        COST["place"],
        (ids, scale, *stats),
        scratch=[pltpu.VMEM((ring, genes, total // ring), jnp.float32)],
    )


def finish_kernel(covs, ring, order, ids_ref, solved_ref, scale_ref, placed_ref, mine_ref, came_ref, *rest):
    out_ref = rest[-1]
    variants = mine_ref.shape[1]
    group = LANES // math.gcd(variants, LANES)
    width = group * variants
    stat = fitted_stat(covs, 0, solved_ref, mine_ref, came_ref, rest[:-1])
    out_ref[...] = placed_ref[...]
    index = jnp.int32(0)
    for block in range(ring):
        index = jnp.where(slot_of(block, ids_ref[1], ring, order) == ring // 2, block, index)
    span = pl.ds(pl.multiple_of(index // group * width, LANES), width)
    stat = jnp.concatenate([stat] * group, axis=1)
    lane = lax.broadcasted_iota(jnp.int32, stat.shape, 1)
    first = lax.rem(index, group) * variants
    inside = jnp.logical_and(lane >= first, lane < first + variants)
    out_ref[:, span] = jnp.where(inside, stat * scale_ref[:, span], placed_ref[:, span])


def finish(ids, solved, scale, placed, last, covs, ring, order):
    return call(
        functools.partial(finish_kernel, covs, ring, order),
        jax.ShapeDtypeStruct(scale.shape, jnp.float32),
        "finish",
        COST["finish"],
        (ids, solved, scale, placed, *last),
    )


def shards(order, expression, genotypes, covariates, distance_bins, gene_folds, fold_weights):
    parts, ring = lax.axis_size("samp"), lax.axis_size("var")
    rows, width = expression.shape
    covs = covariates.shape[1]
    genes = width // parts
    deep = covs + 8
    dof = float(rows * parts - covs - 2)
    gt = genotypes.T
    variants = gt.shape[0]
    middle = ring // 2
    ids = jnp.stack([lax.axis_index("samp"), lax.axis_index("var")]).astype(jnp.int32)

    def exchange(x, d):
        return lax.ppermute(x, "samp", [(s, s ^ d) for s in range(parts)])

    forward = [(order[i], order[(i + 1) % ring]) for i in range(ring)]
    backward = [(b, a) for a, b in forward]

    def right(x):
        return lax.ppermute(x, "var", forward)

    def left(x):
        return lax.ppermute(x, "var", backward)

    stats = []
    lhs = solved = scale = None

    done = {}

    def after(*names):
        return [done[name] for name in names if name in done]

    block = (gt, gt)
    for k in range(middle + 1):
        if k < middle - 1:
            ahead = (right(block[0]), left(block[-1]))
        elif k == middle - 1:
            ahead = (right(block[0][: variants // 2]), left(block[-1][variants // 2 :]))
        if k == 0:
            lhs, send, other, mine = first_products(ids, expression, gt, covariates.T, parts)
        else:
            tokens = after(("got", k - 2), *([("sent", k - 1)] if k == middle else []))
            send, other, mine = next_products(lhs, block, parts, covs, tokens)
        came = exchange(send, 1)
        sent = add_cores(other, came, genes, deep, 1)
        got = [[exchange(x, 2 * (i + 1)) for x in cut] for i, cut in enumerate(sent)]
        swapped = [*sent[0], *sum(got, [])]
        done["came", k], done["sent", k] = came, sent[0][0]
        done["got", k], done["rest", k] = got[-1][0], got[-1][-1]
        if k == 0:
            solved, scale = solve(
                fold_weights, mine, came, swapped, distance_bins, gene_folds[None], covs, dof, ring * variants
            )
            done["solved", 0] = solved
        if k < middle:
            stats.append(chunk_stat(solved, mine, came, swapped, covs, LANES if k == 0 else 0))
            done["stat", k] = stats[k]
            block = ahead
    placed = place(ids, scale, stats, ring, tuple(order))
    return finish(ids, solved, scale, placed, (mine, came, *swapped), covs, ring, tuple(order))


def solution(mesh):
    return jax.shard_map(
        functools.partial(shards, ring_order(mesh)),
        mesh=mesh,
        in_specs=(
            P(("groups", "samp"), "var"),
            P(("groups", "samp"), "var"),
            P(("groups", "samp"), None),
            P("groups", ("var", "samp")),
            P(("groups", "var", "samp")),
            P(),
        ),
        out_specs=P(("groups", "var", "samp"), None),
        check_vma=False,
    )
```

```python
import functools
import math

import jax
import jax.numpy as jnp
from jax import lax
from jax.experimental import pallas as pl
from jax.experimental.pallas import tpu as pltpu
from jax.sharding import PartitionSpec as P

LANES = 128
EPS = 1e-06
COST = {'products': 1, 'add': 1, 'solve': 5000000000, 'stat': 1000000000, 'place': 1, 'finish': 1, 'gate': 1000000000000}
VMEM_LIMIT = 10 * 1024 * 1024

NT = (((1,), (1,)), ((), ()))
NN = (((1,), (0,)), ((), ()))
HIGHEST = lax.Precision.HIGHEST


def ring_order(mesh):
    members = list(mesh.devices[0, 0])
    places = [getattr(device, "coords", None) for device in members]
    if len(members) < 2 or any(place is None for place in places):
        return list(range(len(members)))
    axis = [i for i in range(len(places[0])) if places[0][i] != places[1][i]][0]
    columns = {}
    for index, place in enumerate(places):
        columns.setdefault(place[axis], []).append(index)
    order = []
    for step, key in enumerate(sorted(columns)):
        order += columns[key] if step % 2 == 0 else columns[key][::-1]
    return order


def call(kernel, out_shape, name, flops, operands, scratch=(), scalars=1, tokens=0):
    vmem = pl.BlockSpec(memory_space=pltpu.VMEM)
    smem = pl.BlockSpec(memory_space=pltpu.SMEM)
    rest = len(operands) - scalars - tokens
    return pl.pallas_call(
        kernel,
        out_shape=out_shape,
        in_specs=[smem] * scalars + [vmem] * rest + [pl.BlockSpec(memory_space=pl.ANY)] * tokens,
        out_specs=jax.tree.map(lambda _: vmem, out_shape),
        scratch_shapes=list(scratch),
        compiler_params=pltpu.CompilerParams(vmem_limit_bytes=VMEM_LIMIT),
        cost_estimate=pl.CostEstimate(flops=flops, bytes_accessed=0, transcendentals=0),
        name=name,
    )(*operands)


def gate_kernel(*refs):
    pass


def gate(blocks, tokens):
    vmem = pl.BlockSpec(memory_space=pltpu.VMEM)
    return pl.pallas_call(
        gate_kernel,
        out_shape=[jax.ShapeDtypeStruct(b.shape, b.dtype) for b in blocks],
        in_specs=[vmem] * len(blocks) + [pl.BlockSpec(memory_space=pl.ANY)] * len(tokens),
        out_specs=[vmem] * len(blocks),
        input_output_aliases={i: i for i in range(len(blocks))},
        compiler_params=pltpu.CompilerParams(vmem_limit_bytes=VMEM_LIMIT),
        cost_estimate=pl.CostEstimate(flops=COST["gate"], bytes_accessed=0, transcendentals=0),
        name="gate",
    )(*blocks, *tokens)


def first_kernel(parts, covs, ids_ref, e_ref, gt_ref, dt_ref, left_ref, send_ref, other_ref, mine_ref, wide):
    width = e_ref.shape[1]
    genes = width // parts
    sid = ids_ref[0]
    wide[...] = e_ref[...].T
    owners = [sid ^ 1 ^ d for d in range(2, parts, 2)] + [sid ^ 1]
    owners += [sid ^ d for d in range(2, parts, 2)] + [sid]
    for i, owner in enumerate(owners):
        start = pl.multiple_of(owner * genes, 16)
        left_ref[i * genes : (i + 1) * genes] = wide[pl.ds(start, genes), :]
    rows = dt_ref.shape[1]
    left_ref[width : width + covs] = dt_ref[...]
    first = lax.broadcasted_iota(jnp.int32, (16, rows), 0) == 0
    left_ref[width + covs :] = first.astype(jnp.float32).astype(jnp.bfloat16)
    design = left_ref[width:]
    right = jnp.concatenate([design, jnp.zeros((LANES - design.shape[0], rows), jnp.bfloat16)], axis=0)
    right = jnp.concatenate([right, gt_ref[...]], axis=0)
    split(parts, covs, genes, left_ref, right, send_ref, other_ref, mine_ref, True)


def next_kernel(parts, covs, blocks, left_ref, *rest):
    right = jnp.concatenate([ref[...] for ref in rest[:blocks]], axis=0)
    send_ref, other_ref, mine_ref = rest[-3:]
    genes = mine_ref.shape[0]
    split(parts, covs, genes, left_ref, right, send_ref, other_ref, mine_ref, False)


def split(parts, covs, genes, left_ref, right, send_ref, other_ref, mine_ref, squares):
    width = genes * parts
    span = genes * (parts // 2 - 1)
    deep = covs + 8

    prod = lax.dot_general(left_ref[...], right, NT, preferred_element_type=jnp.float32)
    outs = prod[:width]
    if squares:
        a = left_ref[:width].astype(jnp.float32)
        lane = lax.broadcasted_iota(jnp.int32, outs.shape, 1)
        outs = jnp.where(lane == covs + 1, jnp.sum(a * a, axis=1, keepdims=True), outs)
    send_ref[:span] = outs[:span]
    send_ref[span + deep :] = outs[span : span + genes]
    other_ref[:span] = outs[span + genes : 2 * span + genes]
    mine_ref[...] = outs[2 * span + genes :]
    square = right.astype(jnp.float32)
    square = square * square
    high = square.astype(jnp.bfloat16)
    low = (square - high.astype(jnp.float32)).astype(jnp.bfloat16)
    ones = jnp.ones((16, right.shape[1]), jnp.bfloat16)
    total = lax.dot_general(ones, high, NT, preferred_element_type=jnp.float32)
    total += lax.dot_general(ones, low, NT, preferred_element_type=jnp.float32)
    fits = prod[width : width + deep]
    row = lax.broadcasted_iota(jnp.int32, fits.shape, 0)
    fits = jnp.where(row == covs + 1, total[:1], fits)
    send_ref[span : span + deep] = fits
    other_ref[span:] = fits


def product_shapes(parts, covs, genes, columns):
    span = genes * (parts // 2 - 1)
    rows = (span + covs + 8 + genes, span + covs + 8, genes)
    return [jax.ShapeDtypeStruct((r, columns), jnp.float32) for r in rows]


def first_products(ids, e, gt, dt, parts):
    rows, width = e.shape
    covs = dt.shape[0]
    columns = LANES + gt.shape[0]
    left = jax.ShapeDtypeStruct((width + covs + 16, rows), jnp.bfloat16)
    return call(
        functools.partial(first_kernel, parts, covs),
        [left] + product_shapes(parts, covs, width // parts, columns),
        "first_products",
        COST["products"],
        (ids, e, gt, dt),
        scratch=[pltpu.VMEM((width, rows), jnp.bfloat16)],
    )


def next_products(left, blocks, parts, covs, tokens):
    rows = left.shape[1]
    width = left.shape[0] - covs - 16
    columns = sum(b.shape[0] for b in blocks)
    return call(
        functools.partial(next_kernel, parts, covs, len(blocks)),
        product_shapes(parts, covs, width // parts, columns),
        "next_products",
        COST["products"],
        (left, *blocks, *tokens),
        scalars=0,
        tokens=len(tokens),
    )


def packed_rows(tall, columns):
    return tall * (columns // LANES) + -(-tall // 16) * 8 if columns % LANES == LANES // 2 and columns > LANES else 0


def pack(block):
    tall, columns = block.shape
    fold = -(-tall // 16) * 8
    whole = columns // LANES
    rest = block[:, whole * LANES :]
    rest = jnp.concatenate([rest, jnp.zeros((2 * fold - tall, LANES // 2), rest.dtype)], axis=0)
    tiles = [block[:, i * LANES : (i + 1) * LANES] for i in range(whole)]
    return jnp.concatenate([*tiles, jnp.concatenate([rest[:fold], rest[fold:]], axis=1)], axis=0)


def unpack(block, tall):
    fold = -(-tall // 16) * 8
    whole = block.shape[0] // tall
    rest = block[whole * tall :]
    rest = jnp.concatenate([rest[:, : LANES // 2], rest[: tall - fold, LANES // 2 :]], axis=0)
    tiles = [block[i * tall : (i + 1) * tall] for i in range(whole)]
    return jnp.concatenate([*tiles, rest], axis=1)


def add_kernel(genes, deep, other_ref, came_ref, *out_refs):
    cuts = len(out_refs) * genes // (other_ref.shape[0] - deep)
    span = other_ref.shape[0] - deep
    for i in range(span // genes):
        start = i * genes
        total = other_ref[start : start + genes] + came_ref[start : start + genes]
        fits = other_ref[span:] + came_ref[span : span + deep]
        total = jnp.concatenate([total, fits], axis=0)
        if out_refs[i * cuts].shape[0] > genes + deep:
            total = pack(total)
        row = 0
        for out_ref in out_refs[i * cuts : (i + 1) * cuts]:
            out_ref[...] = total[row : row + out_ref.shape[0]]
            row += out_ref.shape[0]


def add_cores(other, came, genes, deep, cuts):
    chips = (other.shape[0] - deep) // genes
    tall = genes + deep
    dense = packed_rows(tall, other.shape[1])
    if dense:
        heights, columns, cuts = [dense], LANES, 1
    else:
        heights, columns = [tall] if cuts == 1 else [tall // 16 * 8, tall - tall // 16 * 8], other.shape[1]
    shapes = [jax.ShapeDtypeStruct((h, columns), jnp.float32) for h in heights]
    out = call(
        functools.partial(add_kernel, genes, deep),
        shapes * chips,
        "add_cores",
        COST["add"],
        (other, came),
        scalars=0,
    )
    return [out[i * cuts : (i + 1) * cuts] for i in range(chips)]


def chunk_sums(genes, deep, mine_ref, came_ref, refs):
    tall = genes + deep
    blocks, rows = [], []
    for ref in refs:
        rows.append(unpack(ref[...], tall) if ref.shape[0] > tall else ref[...])
        if sum(r.shape[0] for r in rows) == tall:
            blocks.append(jnp.concatenate(rows, axis=0) if len(rows) > 1 else rows[0])
            rows = []
    corr = mine_ref[...] + came_ref[came_ref.shape[0] - genes :]
    fits = blocks[0][genes:]
    for block in blocks[1:]:
        corr = corr + block[:genes]
        fits = fits + block[genes:]
    return corr, fits


def solve_kernel(covs, dof, weight_ref, mine_ref, came_ref, *rest):
    refs, (bins_ref, folds_ref, solved_ref, scale_ref) = rest[:-4], rest[-4:]
    genes = mine_ref.shape[0]
    rank, deep = covs + 1, covs + 8
    corr, fits = chunk_sums(genes, deep, mine_ref, came_ref, refs)
    cross, gram = corr[:, :LANES], fits[:, :LANES]
    row = lax.broadcasted_iota(jnp.int32, gram.shape, 0)
    lane = lax.broadcasted_iota(jnp.int32, gram.shape, 1)
    inside = jnp.logical_and(row < rank, lane < rank)
    a = jnp.where(inside, gram, jnp.where(row == lane, 1.0, 0.0))
    for k in range(0, rank, 2):
        down0 = jnp.broadcast_to(a[:, k : k + 1], a.shape)
        down1 = jnp.broadcast_to(a[:, k + 1 : k + 2], a.shape)
        p00, p01, p11 = down0[k : k + 1], down1[k : k + 1], down1[k + 1 : k + 2]
        inv = 1.0 / (p00 * p11 - p01 * p01)
        q00, q01, q11 = p11 * inv, -p01 * inv, p00 * inv
        row0, row1 = a[k : k + 1], a[k + 1 : k + 2]
        first = q00 * row0 + q01 * row1
        second = q01 * row0 + q11 * row1
        swept = a - down0 * first - down1 * second
        swept = jnp.where(lane == k, down0 * q00 + down1 * q01, swept)
        swept = jnp.where(lane == k + 1, down0 * q01 + down1 * q11, swept)
        first = jnp.where(lane[:1] == k, -q00, jnp.where(lane[:1] == k + 1, -q01, first))
        second = jnp.where(lane[:1] == k, -q01, jnp.where(lane[:1] == k + 1, -q11, second))
        a = jnp.where(row == k, first, jnp.where(row == k + 1, second, swept))
    inverse = jnp.where(inside, -a, 0.0)
    lane = lax.broadcasted_iota(jnp.int32, cross.shape, 1)
    squares = jnp.sum(jnp.where(lane == rank, cross, 0.0), axis=1, keepdims=True)
    cross = jnp.where(lane < rank, cross, 0.0)
    beta = lax.dot_general(cross, inverse, NT, precision=HIGHEST, preferred_element_type=jnp.float32)
    norm = squares - jnp.sum(beta * cross[:, :deep], axis=1, keepdims=True)
    norm = jnp.maximum(norm, 1e-06 * squares) + EPS
    solved_ref[:genes] = beta
    solved_ref[genes:] = inverse[:, :deep]

    bins, folds = bins_ref[...], folds_ref[...]
    tile = jnp.zeros(bins.shape, jnp.float32)
    for b in range(weight_ref.shape[1]):
        of_bin = jnp.zeros(folds.shape, jnp.float32)
        for f in range(weight_ref.shape[0]):
            of_bin = jnp.where(folds == f, weight_ref[f, b], of_bin)
        tile = jnp.where(bins == b, of_bin, tile)
    tile = tile.T * (dof / norm)
    width = scale_ref.shape[1] // tile.shape[1]
    for t in range(0, tile.shape[1], 2):
        pair = [jnp.broadcast_to(tile[:, i : i + 1], (genes, width)) for i in (t, t + 1)]
        scale_ref[:, t * width : (t + 2) * width] = jnp.concatenate(pair, axis=1)


def solve(weights, mine, came, swapped, bins, folds, covs, dof, variants):
    genes = mine.shape[0]
    outs = [
        jax.ShapeDtypeStruct((genes + covs + 8, covs + 8), jnp.float32),
        jax.ShapeDtypeStruct((genes, variants), jnp.float32),
    ]
    return call(
        functools.partial(solve_kernel, covs, dof),
        outs,
        "solve",
        COST["solve"],
        (weights, mine, came, *swapped, bins, folds),
    )


def fitted_stat(covs, skip, solved_ref, mine_ref, came_ref, refs):
    genes = mine_ref.shape[0]
    corr, fits = chunk_sums(genes, covs + 8, mine_ref, came_ref, refs)
    corr, fits = corr[:, skip:], fits[:, skip:]
    row = lax.broadcasted_iota(jnp.int32, fits.shape, 0)
    squares = fits[covs + 1 : covs + 2]
    fits = jnp.where(row <= covs, fits, 0.0)
    both = lax.dot_general(solved_ref[...], fits, NN, precision=HIGHEST, preferred_element_type=jnp.float32)
    norm = squares - jnp.sum(both[genes:] * fits, axis=0, keepdims=True)
    norm = jnp.maximum(norm, 1e-06 * squares) + EPS
    corr = corr - both[:genes]
    return corr * corr * (1.0 / norm)


def stat_kernel(covs, skip, solved_ref, mine_ref, came_ref, *rest):
    rest[-1][...] = fitted_stat(covs, skip, solved_ref, mine_ref, came_ref, rest[:-1])


def chunk_stat(solved, mine, came, swapped, covs, skip):
    return call(
        functools.partial(stat_kernel, covs, skip),
        jax.ShapeDtypeStruct((mine.shape[0], mine.shape[1] - skip), jnp.float32),
        "chunk_stat",
        COST["stat"],
        (solved, mine, came, *swapped),
        scalars=0,
    )


def slot_of(index, here, ring, order):
    position = {block: i for i, block in enumerate(order)}
    mine = jnp.int32(0)
    for block in range(ring):
        mine = jnp.where(here == block, position[block], mine)
    return lax.rem(position[index] - mine + ring, ring)


def place_kernel(ring, order, ids_ref, scale_ref, *rest):
    stats, (out_ref, held) = rest[:-2], rest[-2:]
    variants = held.shape[2]
    held[ring // 2] = jnp.zeros_like(held[0])
    for k, stat in enumerate(stats):
        if k == 0:
            held[0] = stat[...]
        else:
            held[ring - k] = stat[:, :variants]
            held[k] = stat[:, variants:]
    group = LANES // math.gcd(variants, LANES)
    for j in range(0, ring, group):
        pieces = [held[slot_of(j + b, ids_ref[1], ring, order)] for b in range(group)]
        span = slice(j * variants, (j + group) * variants)
        out_ref[:, span] = jnp.concatenate(pieces, axis=1) * scale_ref[:, span]


def place(ids, scale, stats, ring, order):
    genes, total = scale.shape
    return call(
        functools.partial(place_kernel, ring, order),
        jax.ShapeDtypeStruct(scale.shape, jnp.float32),
        "place",
        COST["place"],
        (ids, scale, *stats),
        scratch=[pltpu.VMEM((ring, genes, total // ring), jnp.float32)],
    )


def finish_kernel(covs, ring, order, ids_ref, solved_ref, scale_ref, placed_ref, mine_ref, came_ref, *rest):
    out_ref = rest[-1]
    variants = mine_ref.shape[1]
    group = LANES // math.gcd(variants, LANES)
    width = group * variants
    stat = fitted_stat(covs, 0, solved_ref, mine_ref, came_ref, rest[:-1])
    out_ref[...] = placed_ref[...]
    index = jnp.int32(0)
    for block in range(ring):
        index = jnp.where(slot_of(block, ids_ref[1], ring, order) == ring // 2, block, index)
    span = pl.ds(pl.multiple_of(index // group * width, LANES), width)
    stat = jnp.concatenate([stat] * group, axis=1)
    lane = lax.broadcasted_iota(jnp.int32, stat.shape, 1)
    first = lax.rem(index, group) * variants
    inside = jnp.logical_and(lane >= first, lane < first + variants)
    out_ref[:, span] = jnp.where(inside, stat * scale_ref[:, span], placed_ref[:, span])


def finish(ids, solved, scale, placed, last, covs, ring, order):
    return call(
        functools.partial(finish_kernel, covs, ring, order),
        jax.ShapeDtypeStruct(scale.shape, jnp.float32),
        "finish",
        COST["finish"],
        (ids, solved, scale, placed, *last),
    )


def shards(order, expression, genotypes, covariates, distance_bins, gene_folds, fold_weights):
    parts, ring = lax.axis_size("samp"), lax.axis_size("var")
    rows, width = expression.shape
    covs = covariates.shape[1]
    genes = width // parts
    deep = covs + 8
    dof = float(rows * parts - covs - 2)
    gt = genotypes.T
    variants = gt.shape[0]
    middle = ring // 2
    ids = jnp.stack([lax.axis_index("samp"), lax.axis_index("var")]).astype(jnp.int32)

    def exchange(x, d):
        return lax.ppermute(x, "samp", [(s, s ^ d) for s in range(parts)])

    forward = [(order[i], order[(i + 1) % ring]) for i in range(ring)]
    backward = [(b, a) for a, b in forward]

    def right(x):
        return lax.ppermute(x, "var", forward)

    def left(x):
        return lax.ppermute(x, "var", backward)

    stats = []
    lhs = solved = scale = None

    done = {}

    def after(*names):
        return [done[name] for name in names if name in done]

    block = (gt, gt)
    for k in range(middle + 1):
        if k > 0 and True:
            block = gate(block, after(*{3: (('sent', 2),)}.get(k, ())))
        if k < middle - 1:
            ahead = (right(block[0]), left(block[-1]))
        elif k == middle - 1:
            ahead = (right(block[0][: variants // 2]), left(block[-1][variants // 2 :]))
        if k == 0:
            lhs, send, other, mine = first_products(ids, expression, gt, covariates.T, parts)
        else:
            tokens = after(*{1: (('came', 0),), 2: (('got', 0), ('sent', 1)), 3: (('got', 2),), 4: (('sent', 3),)}.get(k, ()))
            send, other, mine = next_products(lhs, block, parts, covs, tokens)
        came = exchange(send, 1)
        sent = add_cores(other, came, genes, deep, 2 if k in () else 1)
        got = [[exchange(x, 2 * (i + 1)) for x in cut] for i, cut in enumerate(sent)]
        swapped = [*sent[0], *sum(got, [])]
        done["came", k], done["sent", k] = came, sent[0][0]
        done["got", k], done["rest", k] = got[-1][0], got[-1][-1]
        if k == 0:
            solved, scale = solve(
                fold_weights, mine, came, swapped, distance_bins, gene_folds[None], covs, dof, ring * variants
            )
            done["solved", 0] = solved
        if k < middle:
            stats.append(chunk_stat(solved, mine, came, swapped, covs, LANES if k == 0 else 0))
            done["stat", k] = stats[k]
            block = ahead
    placed = place(ids, scale, stats, ring, tuple(order))
    return finish(ids, solved, scale, placed, (mine, came, *swapped), covs, ring, tuple(order))


def solution(mesh):
    return jax.shard_map(
        functools.partial(shards, ring_order(mesh)),
        mesh=mesh,
        in_specs=(
            P(("groups", "samp"), "var"),
            P(("groups", "samp"), "var"),
            P(("groups", "samp"), None),
            P("groups", ("var", "samp")),
            P(("groups", "var", "samp")),
            P(),
        ),
        out_specs=P(("groups", "var", "samp"), None),
        check_vma=False,
    )
```

```python
import functools
import math

import jax
import jax.numpy as jnp
from jax import lax
from jax.experimental import pallas as pl
from jax.experimental.pallas import tpu as pltpu
from jax.sharding import PartitionSpec as P

LANES = 128
EPS = 1e-06
COST = {'products': 100000000, 'add': 1, 'solve': 100000000, 'stat': 1, 'place': 1, 'finish': 1, 'gate': 100000000000}
VMEM_LIMIT = 10 * 1024 * 1024

NT = (((1,), (1,)), ((), ()))
NN = (((1,), (0,)), ((), ()))
HIGHEST = lax.Precision.HIGHEST


def ring_order(mesh):
    members = list(mesh.devices[0, 0])
    places = [getattr(device, "coords", None) for device in members]
    if len(members) < 2 or any(place is None for place in places):
        return list(range(len(members)))
    axis = [i for i in range(len(places[0])) if places[0][i] != places[1][i]][0]
    columns = {}
    for index, place in enumerate(places):
        columns.setdefault(place[axis], []).append(index)
    order = []
    for step, key in enumerate(sorted(columns)):
        order += columns[key] if step % 2 == 0 else columns[key][::-1]
    return order


def call(kernel, out_shape, name, flops, operands, scratch=(), scalars=1, tokens=0):
    vmem = pl.BlockSpec(memory_space=pltpu.VMEM)
    smem = pl.BlockSpec(memory_space=pltpu.SMEM)
    rest = len(operands) - scalars - tokens
    return pl.pallas_call(
        kernel,
        out_shape=out_shape,
        in_specs=[smem] * scalars + [vmem] * rest + [pl.BlockSpec(memory_space=pl.ANY)] * tokens,
        out_specs=jax.tree.map(lambda _: vmem, out_shape),
        scratch_shapes=list(scratch),
        compiler_params=pltpu.CompilerParams(vmem_limit_bytes=VMEM_LIMIT),
        cost_estimate=pl.CostEstimate(flops=flops, bytes_accessed=0, transcendentals=0),
        name=name,
    )(*operands)


def gate_kernel(*refs):
    pass


def gate(blocks, tokens):
    vmem = pl.BlockSpec(memory_space=pltpu.VMEM)
    return pl.pallas_call(
        gate_kernel,
        out_shape=[jax.ShapeDtypeStruct(b.shape, b.dtype) for b in blocks],
        in_specs=[vmem] * len(blocks) + [pl.BlockSpec(memory_space=pl.ANY)] * len(tokens),
        out_specs=[vmem] * len(blocks),
        input_output_aliases={i: i for i in range(len(blocks))},
        compiler_params=pltpu.CompilerParams(vmem_limit_bytes=VMEM_LIMIT),
        cost_estimate=pl.CostEstimate(flops=COST["gate"], bytes_accessed=0, transcendentals=0),
        name="gate",
    )(*blocks, *tokens)


def first_kernel(parts, covs, ids_ref, e_ref, gt_ref, dt_ref, left_ref, send_ref, other_ref, mine_ref, wide):
    width = e_ref.shape[1]
    genes = width // parts
    sid = ids_ref[0]
    wide[...] = e_ref[...].T
    owners = [sid ^ 1 ^ d for d in range(2, parts, 2)] + [sid ^ 1]
    owners += [sid ^ d for d in range(2, parts, 2)] + [sid]
    for i, owner in enumerate(owners):
        start = pl.multiple_of(owner * genes, 16)
        left_ref[i * genes : (i + 1) * genes] = wide[pl.ds(start, genes), :]
    rows = dt_ref.shape[1]
    left_ref[width : width + covs] = dt_ref[...]
    first = lax.broadcasted_iota(jnp.int32, (16, rows), 0) == 0
    left_ref[width + covs :] = first.astype(jnp.float32).astype(jnp.bfloat16)
    design = left_ref[width:]
    right = jnp.concatenate([design, jnp.zeros((LANES - design.shape[0], rows), jnp.bfloat16)], axis=0)
    right = jnp.concatenate([right, gt_ref[...]], axis=0)
    split(parts, covs, genes, left_ref, right, send_ref, other_ref, mine_ref, True)


def next_kernel(parts, covs, blocks, left_ref, *rest):
    right = jnp.concatenate([ref[...] for ref in rest[:blocks]], axis=0)
    send_ref, other_ref, mine_ref = rest[-3:]
    genes = mine_ref.shape[0]
    split(parts, covs, genes, left_ref, right, send_ref, other_ref, mine_ref, False)


def split(parts, covs, genes, left_ref, right, send_ref, other_ref, mine_ref, squares):
    width = genes * parts
    span = genes * (parts // 2 - 1)
    deep = covs + 8

    prod = lax.dot_general(left_ref[...], right, NT, preferred_element_type=jnp.float32)
    outs = prod[:width]
    if squares:
        a = left_ref[:width].astype(jnp.float32)
        lane = lax.broadcasted_iota(jnp.int32, outs.shape, 1)
        outs = jnp.where(lane == covs + 1, jnp.sum(a * a, axis=1, keepdims=True), outs)
    send_ref[:span] = outs[:span]
    send_ref[span + deep :] = outs[span : span + genes]
    other_ref[:span] = outs[span + genes : 2 * span + genes]
    mine_ref[...] = outs[2 * span + genes :]
    square = right.astype(jnp.float32)
    square = square * square
    high = square.astype(jnp.bfloat16)
    low = (square - high.astype(jnp.float32)).astype(jnp.bfloat16)
    ones = jnp.ones((16, right.shape[1]), jnp.bfloat16)
    total = lax.dot_general(ones, high, NT, preferred_element_type=jnp.float32)
    total += lax.dot_general(ones, low, NT, preferred_element_type=jnp.float32)
    fits = prod[width : width + deep]
    row = lax.broadcasted_iota(jnp.int32, fits.shape, 0)
    fits = jnp.where(row == covs + 1, total[:1], fits)
    send_ref[span : span + deep] = fits
    other_ref[span:] = fits


def product_shapes(parts, covs, genes, columns):
    span = genes * (parts // 2 - 1)
    rows = (span + covs + 8 + genes, span + covs + 8, genes)
    return [jax.ShapeDtypeStruct((r, columns), jnp.float32) for r in rows]


def first_products(ids, e, gt, dt, parts):
    rows, width = e.shape
    covs = dt.shape[0]
    columns = LANES + gt.shape[0]
    left = jax.ShapeDtypeStruct((width + covs + 16, rows), jnp.bfloat16)
    return call(
        functools.partial(first_kernel, parts, covs),
        [left] + product_shapes(parts, covs, width // parts, columns),
        "first_products",
        COST["products"],
        (ids, e, gt, dt),
        scratch=[pltpu.VMEM((width, rows), jnp.bfloat16)],
    )


def next_products(left, blocks, parts, covs, tokens):
    rows = left.shape[1]
    width = left.shape[0] - covs - 16
    columns = sum(b.shape[0] for b in blocks)
    return call(
        functools.partial(next_kernel, parts, covs, len(blocks)),
        product_shapes(parts, covs, width // parts, columns),
        "next_products",
        COST["products"],
        (left, *blocks, *tokens),
        scalars=0,
        tokens=len(tokens),
    )


def packed_rows(tall, columns):
    return tall * (columns // LANES) + -(-tall // 16) * 8 if columns % LANES == LANES // 2 and columns > LANES else 0


def pack(block):
    tall, columns = block.shape
    fold = -(-tall // 16) * 8
    whole = columns // LANES
    rest = block[:, whole * LANES :]
    rest = jnp.concatenate([rest, jnp.zeros((2 * fold - tall, LANES // 2), rest.dtype)], axis=0)
    tiles = [block[:, i * LANES : (i + 1) * LANES] for i in range(whole)]
    return jnp.concatenate([*tiles, jnp.concatenate([rest[:fold], rest[fold:]], axis=1)], axis=0)


def unpack(block, tall):
    fold = -(-tall // 16) * 8
    whole = block.shape[0] // tall
    rest = block[whole * tall :]
    rest = jnp.concatenate([rest[:, : LANES // 2], rest[: tall - fold, LANES // 2 :]], axis=0)
    tiles = [block[i * tall : (i + 1) * tall] for i in range(whole)]
    return jnp.concatenate([*tiles, rest], axis=1)


def add_kernel(genes, deep, other_ref, came_ref, *out_refs):
    cuts = len(out_refs) * genes // (other_ref.shape[0] - deep)
    span = other_ref.shape[0] - deep
    for i in range(span // genes):
        start = i * genes
        total = other_ref[start : start + genes] + came_ref[start : start + genes]
        fits = other_ref[span:] + came_ref[span : span + deep]
        total = jnp.concatenate([total, fits], axis=0)
        if out_refs[i * cuts].shape[0] > genes + deep:
            total = pack(total)
        row = 0
        for out_ref in out_refs[i * cuts : (i + 1) * cuts]:
            out_ref[...] = total[row : row + out_ref.shape[0]]
            row += out_ref.shape[0]


def add_cores(other, came, genes, deep, cuts):
    chips = (other.shape[0] - deep) // genes
    tall = genes + deep
    dense = packed_rows(tall, other.shape[1])
    if dense:
        heights, columns, cuts = [dense], LANES, 1
    else:
        heights, columns = [tall] if cuts == 1 else [tall // 16 * 8, tall - tall // 16 * 8], other.shape[1]
    shapes = [jax.ShapeDtypeStruct((h, columns), jnp.float32) for h in heights]
    out = call(
        functools.partial(add_kernel, genes, deep),
        shapes * chips,
        "add_cores",
        COST["add"],
        (other, came),
        scalars=0,
    )
    return [out[i * cuts : (i + 1) * cuts] for i in range(chips)]


def chunk_sums(genes, deep, mine_ref, came_ref, refs):
    tall = genes + deep
    blocks, rows = [], []
    for ref in refs:
        rows.append(unpack(ref[...], tall) if ref.shape[0] > tall else ref[...])
        if sum(r.shape[0] for r in rows) == tall:
            blocks.append(jnp.concatenate(rows, axis=0) if len(rows) > 1 else rows[0])
            rows = []
    corr = mine_ref[...] + came_ref[came_ref.shape[0] - genes :]
    fits = blocks[0][genes:]
    for block in blocks[1:]:
        corr = corr + block[:genes]
        fits = fits + block[genes:]
    return corr, fits


def solve_kernel(covs, dof, weight_ref, mine_ref, came_ref, *rest):
    refs, (bins_ref, folds_ref, solved_ref, scale_ref) = rest[:-4], rest[-4:]
    genes = mine_ref.shape[0]
    rank, deep = covs + 1, covs + 8
    corr, fits = chunk_sums(genes, deep, mine_ref, came_ref, refs)
    cross, gram = corr[:, :LANES], fits[:, :LANES]
    row = lax.broadcasted_iota(jnp.int32, gram.shape, 0)
    lane = lax.broadcasted_iota(jnp.int32, gram.shape, 1)
    inside = jnp.logical_and(row < rank, lane < rank)
    a = jnp.where(inside, gram, jnp.where(row == lane, 1.0, 0.0))
    for k in range(0, rank, 2):
        down0 = jnp.broadcast_to(a[:, k : k + 1], a.shape)
        down1 = jnp.broadcast_to(a[:, k + 1 : k + 2], a.shape)
        p00, p01, p11 = down0[k : k + 1], down1[k : k + 1], down1[k + 1 : k + 2]
        inv = 1.0 / (p00 * p11 - p01 * p01)
        q00, q01, q11 = p11 * inv, -p01 * inv, p00 * inv
        row0, row1 = a[k : k + 1], a[k + 1 : k + 2]
        first = q00 * row0 + q01 * row1
        second = q01 * row0 + q11 * row1
        swept = a - down0 * first - down1 * second
        swept = jnp.where(lane == k, down0 * q00 + down1 * q01, swept)
        swept = jnp.where(lane == k + 1, down0 * q01 + down1 * q11, swept)
        first = jnp.where(lane[:1] == k, -q00, jnp.where(lane[:1] == k + 1, -q01, first))
        second = jnp.where(lane[:1] == k, -q01, jnp.where(lane[:1] == k + 1, -q11, second))
        a = jnp.where(row == k, first, jnp.where(row == k + 1, second, swept))
    inverse = jnp.where(inside, -a, 0.0)
    lane = lax.broadcasted_iota(jnp.int32, cross.shape, 1)
    squares = jnp.sum(jnp.where(lane == rank, cross, 0.0), axis=1, keepdims=True)
    cross = jnp.where(lane < rank, cross, 0.0)
    beta = lax.dot_general(cross, inverse, NT, precision=HIGHEST, preferred_element_type=jnp.float32)
    norm = squares - jnp.sum(beta * cross[:, :deep], axis=1, keepdims=True)
    norm = jnp.maximum(norm, 1e-06 * squares) + EPS
    solved_ref[:genes] = beta
    solved_ref[genes:] = inverse[:, :deep]

    bins, folds = bins_ref[...], folds_ref[...]
    tile = jnp.zeros(bins.shape, jnp.float32)
    for b in range(weight_ref.shape[1]):
        of_bin = jnp.zeros(folds.shape, jnp.float32)
        for f in range(weight_ref.shape[0]):
            of_bin = jnp.where(folds == f, weight_ref[f, b], of_bin)
        tile = jnp.where(bins == b, of_bin, tile)
    tile = tile.T * (dof / norm)
    width = scale_ref.shape[1] // tile.shape[1]
    for t in range(0, tile.shape[1], 2):
        pair = [jnp.broadcast_to(tile[:, i : i + 1], (genes, width)) for i in (t, t + 1)]
        scale_ref[:, t * width : (t + 2) * width] = jnp.concatenate(pair, axis=1)


def solve(weights, mine, came, swapped, bins, folds, covs, dof, variants):
    genes = mine.shape[0]
    outs = [
        jax.ShapeDtypeStruct((genes + covs + 8, covs + 8), jnp.float32),
        jax.ShapeDtypeStruct((genes, variants), jnp.float32),
    ]
    return call(
        functools.partial(solve_kernel, covs, dof),
        outs,
        "solve",
        COST["solve"],
        (weights, mine, came, *swapped, bins, folds),
    )


def fitted_stat(covs, skip, solved_ref, mine_ref, came_ref, refs):
    genes = mine_ref.shape[0]
    corr, fits = chunk_sums(genes, covs + 8, mine_ref, came_ref, refs)
    corr, fits = corr[:, skip:], fits[:, skip:]
    row = lax.broadcasted_iota(jnp.int32, fits.shape, 0)
    squares = fits[covs + 1 : covs + 2]
    fits = jnp.where(row <= covs, fits, 0.0)
    both = lax.dot_general(solved_ref[...], fits, NN, precision=HIGHEST, preferred_element_type=jnp.float32)
    norm = squares - jnp.sum(both[genes:] * fits, axis=0, keepdims=True)
    norm = jnp.maximum(norm, 1e-06 * squares) + EPS
    corr = corr - both[:genes]
    return corr * corr * (1.0 / norm)


def stat_kernel(covs, skip, solved_ref, mine_ref, came_ref, *rest):
    rest[-1][...] = fitted_stat(covs, skip, solved_ref, mine_ref, came_ref, rest[:-1])


def chunk_stat(solved, mine, came, swapped, covs, skip):
    return call(
        functools.partial(stat_kernel, covs, skip),
        jax.ShapeDtypeStruct((mine.shape[0], mine.shape[1] - skip), jnp.float32),
        "chunk_stat",
        COST["stat"],
        (solved, mine, came, *swapped),
        scalars=0,
    )


def slot_of(index, here, ring, order):
    position = {block: i for i, block in enumerate(order)}
    mine = jnp.int32(0)
    for block in range(ring):
        mine = jnp.where(here == block, position[block], mine)
    return lax.rem(position[index] - mine + ring, ring)


def place_kernel(ring, order, ids_ref, scale_ref, *rest):
    stats, (out_ref, held) = rest[:-2], rest[-2:]
    variants = held.shape[2]
    held[ring // 2] = jnp.zeros_like(held[0])
    for k, stat in enumerate(stats):
        if k == 0:
            held[0] = stat[...]
        else:
            held[ring - k] = stat[:, :variants]
            held[k] = stat[:, variants:]
    group = LANES // math.gcd(variants, LANES)
    for j in range(0, ring, group):
        pieces = [held[slot_of(j + b, ids_ref[1], ring, order)] for b in range(group)]
        span = slice(j * variants, (j + group) * variants)
        out_ref[:, span] = jnp.concatenate(pieces, axis=1) * scale_ref[:, span]


def place(ids, scale, stats, ring, order):
    genes, total = scale.shape
    return call(
        functools.partial(place_kernel, ring, order),
        jax.ShapeDtypeStruct(scale.shape, jnp.float32),
        "place",
        COST["place"],
        (ids, scale, *stats),
        scratch=[pltpu.VMEM((ring, genes, total // ring), jnp.float32)],
    )


def finish_kernel(covs, ring, order, ids_ref, solved_ref, scale_ref, placed_ref, mine_ref, came_ref, *rest):
    out_ref = rest[-1]
    variants = mine_ref.shape[1]
    group = LANES // math.gcd(variants, LANES)
    width = group * variants
    stat = fitted_stat(covs, 0, solved_ref, mine_ref, came_ref, rest[:-1])
    out_ref[...] = placed_ref[...]
    index = jnp.int32(0)
    for block in range(ring):
        index = jnp.where(slot_of(block, ids_ref[1], ring, order) == ring // 2, block, index)
    span = pl.ds(pl.multiple_of(index // group * width, LANES), width)
    stat = jnp.concatenate([stat] * group, axis=1)
    lane = lax.broadcasted_iota(jnp.int32, stat.shape, 1)
    first = lax.rem(index, group) * variants
    inside = jnp.logical_and(lane >= first, lane < first + variants)
    out_ref[:, span] = jnp.where(inside, stat * scale_ref[:, span], placed_ref[:, span])


def finish(ids, solved, scale, placed, last, covs, ring, order):
    return call(
        functools.partial(finish_kernel, covs, ring, order),
        jax.ShapeDtypeStruct(scale.shape, jnp.float32),
        "finish",
        COST["finish"],
        (ids, solved, scale, placed, *last),
    )


def shards(order, expression, genotypes, covariates, distance_bins, gene_folds, fold_weights):
    parts, ring = lax.axis_size("samp"), lax.axis_size("var")
    rows, width = expression.shape
    covs = covariates.shape[1]
    genes = width // parts
    deep = covs + 8
    dof = float(rows * parts - covs - 2)
    gt = genotypes.T
    variants = gt.shape[0]
    middle = ring // 2
    ids = jnp.stack([lax.axis_index("samp"), lax.axis_index("var")]).astype(jnp.int32)

    def exchange(x, d):
        return lax.ppermute(x, "samp", [(s, s ^ d) for s in range(parts)])

    forward = [(order[i], order[(i + 1) % ring]) for i in range(ring)]
    backward = [(b, a) for a, b in forward]

    def right(x):
        return lax.ppermute(x, "var", forward)

    def left(x):
        return lax.ppermute(x, "var", backward)

    stats = []
    lhs = solved = scale = None

    done = {}

    def after(*names):
        return [done[name] for name in names if name in done]

    block = (gt, gt)
    for k in range(middle + 1):
        if k > 0 and True:
            block = gate(block, after(*{2: (('got', 0),), 3: (('got', 1), ('solved', 0))}.get(k, ())))
        if k < middle - 1:
            ahead = (right(block[0]), left(block[-1]))
        elif k == middle - 1:
            ahead = (right(block[0][: variants // 2]), left(block[-1][variants // 2 :]))
        if k == 0:
            lhs, send, other, mine = first_products(ids, expression, gt, covariates.T, parts)
        else:
            tokens = after(*{1: (('came', 0),), 2: (('got', 0),), 3: (('got', 1), ('sent', 2)), 4: (('sent', 3), ('got', 2))}.get(k, ()))
            send, other, mine = next_products(lhs, block, parts, covs, tokens)
        came = exchange(send, 1)
        sent = add_cores(other, came, genes, deep, 2 if k in () else 1)
        got = [[exchange(x, 2 * (i + 1)) for x in cut] for i, cut in enumerate(sent)]
        swapped = [*sent[0], *sum(got, [])]
        done["came", k], done["sent", k] = came, sent[0][0]
        done["got", k], done["rest", k] = got[-1][0], got[-1][-1]
        if k == 0:
            solved, scale = solve(
                fold_weights, mine, came, swapped, distance_bins, gene_folds[None], covs, dof, ring * variants
            )
            done["solved", 0] = solved
        if k < middle:
            stats.append(chunk_stat(solved, mine, came, swapped, covs, LANES if k == 0 else 0))
            done["stat", k] = stats[k]
            block = ahead
    placed = place(ids, scale, stats, ring, tuple(order))
    return finish(ids, solved, scale, placed, (mine, came, *swapped), covs, ring, tuple(order))


def solution(mesh):
    return jax.shard_map(
        functools.partial(shards, ring_order(mesh)),
        mesh=mesh,
        in_specs=(
            P(("groups", "samp"), "var"),
            P(("groups", "samp"), "var"),
            P(("groups", "samp"), None),
            P("groups", ("var", "samp")),
            P(("groups", "var", "samp")),
            P(),
        ),
        out_specs=P(("groups", "var", "samp"), None),
        check_vma=False,
    )
```

```python
import functools
import math

import jax
import jax.numpy as jnp
from jax import lax
from jax.experimental import pallas as pl
from jax.experimental.pallas import tpu as pltpu
from jax.sharding import PartitionSpec as P

LANES = 128
EPS = 1e-06
COST = {'products': 10**8, 'add': 1, 'solve': 10**8, 'stat': 1, 'place': 1, 'finish': 1, 'gate': 10**11}
VMEM_LIMIT = 10 * 1024 * 1024

NT = (((1,), (1,)), ((), ()))
NN = (((1,), (0,)), ((), ()))
HIGHEST = lax.Precision.HIGHEST


def ring_order(mesh):
    members = list(mesh.devices[0, 0])
    places = [getattr(device, "coords", None) for device in members]
    if len(members) < 2 or any(place is None for place in places):
        return list(range(len(members)))
    axis = [i for i in range(len(places[0])) if places[0][i] != places[1][i]][0]
    columns = {}
    for index, place in enumerate(places):
        columns.setdefault(place[axis], []).append(index)
    order = []
    for step, key in enumerate(sorted(columns)):
        order += columns[key] if step % 2 == 0 else columns[key][::-1]
    return order


def call(kernel, out_shape, name, flops, operands, scratch=(), scalars=1, tokens=0):
    vmem = pl.BlockSpec(memory_space=pltpu.VMEM)
    smem = pl.BlockSpec(memory_space=pltpu.SMEM)
    rest = len(operands) - scalars - tokens
    return pl.pallas_call(
        kernel,
        out_shape=out_shape,
        in_specs=[smem] * scalars + [vmem] * rest + [pl.BlockSpec(memory_space=pl.ANY)] * tokens,
        out_specs=jax.tree.map(lambda _: vmem, out_shape),
        scratch_shapes=list(scratch),
        compiler_params=pltpu.CompilerParams(vmem_limit_bytes=VMEM_LIMIT),
        cost_estimate=pl.CostEstimate(flops=flops, bytes_accessed=0, transcendentals=0),
        name=name,
    )(*operands)


def gate_kernel(*refs):
    pass


def gate(blocks, tokens):
    vmem = pl.BlockSpec(memory_space=pltpu.VMEM)
    return pl.pallas_call(
        gate_kernel,
        out_shape=[jax.ShapeDtypeStruct(b.shape, b.dtype) for b in blocks],
        in_specs=[vmem] * len(blocks) + [pl.BlockSpec(memory_space=pl.ANY)] * len(tokens),
        out_specs=[vmem] * len(blocks),
        input_output_aliases={i: i for i in range(len(blocks))},
        compiler_params=pltpu.CompilerParams(vmem_limit_bytes=VMEM_LIMIT),
        cost_estimate=pl.CostEstimate(flops=COST["gate"], bytes_accessed=0, transcendentals=0),
        name="gate",
    )(*blocks, *tokens)


def first_kernel(parts, covs, ids_ref, e_ref, gt_ref, dt_ref, left_ref, send_ref, other_ref, mine_ref, wide):
    width = e_ref.shape[1]
    genes = width // parts
    sid = ids_ref[0]
    wide[...] = e_ref[...].T
    owners = [sid ^ 1 ^ d for d in range(2, parts, 2)] + [sid ^ 1]
    owners += [sid ^ d for d in range(2, parts, 2)] + [sid]
    for i, owner in enumerate(owners):
        start = pl.multiple_of(owner * genes, 16)
        left_ref[i * genes : (i + 1) * genes] = wide[pl.ds(start, genes), :]
    rows = dt_ref.shape[1]
    left_ref[width : width + covs] = dt_ref[...]
    first = lax.broadcasted_iota(jnp.int32, (16, rows), 0) == 0
    left_ref[width + covs :] = first.astype(jnp.float32).astype(jnp.bfloat16)
    design = left_ref[width:]
    right = jnp.concatenate([design, jnp.zeros((LANES - design.shape[0], rows), jnp.bfloat16)], axis=0)
    right = jnp.concatenate([right, gt_ref[...]], axis=0)
    split(parts, covs, genes, left_ref, right, send_ref, other_ref, mine_ref, True)


def next_kernel(parts, covs, blocks, left_ref, *rest):
    right = jnp.concatenate([ref[...] for ref in rest[:blocks]], axis=0)
    send_ref, other_ref, mine_ref = rest[-3:]
    genes = mine_ref.shape[0]
    split(parts, covs, genes, left_ref, right, send_ref, other_ref, mine_ref, False)


def split(parts, covs, genes, left_ref, right, send_ref, other_ref, mine_ref, squares):
    width = genes * parts
    span = genes * (parts // 2 - 1)
    deep = covs + 8

    prod = lax.dot_general(left_ref[...], right, NT, preferred_element_type=jnp.float32)
    outs = prod[:width]
    if squares:
        a = left_ref[:width].astype(jnp.float32)
        lane = lax.broadcasted_iota(jnp.int32, outs.shape, 1)
        outs = jnp.where(lane == covs + 1, jnp.sum(a * a, axis=1, keepdims=True), outs)
    send_ref[:span] = outs[:span]
    send_ref[span + deep :] = outs[span : span + genes]
    other_ref[:span] = outs[span + genes : 2 * span + genes]
    mine_ref[...] = outs[2 * span + genes :]
    square = right.astype(jnp.float32)
    square = square * square
    high = square.astype(jnp.bfloat16)
    low = (square - high.astype(jnp.float32)).astype(jnp.bfloat16)
    ones = jnp.ones((16, right.shape[1]), jnp.bfloat16)
    total = lax.dot_general(ones, high, NT, preferred_element_type=jnp.float32)
    total += lax.dot_general(ones, low, NT, preferred_element_type=jnp.float32)
    fits = prod[width : width + deep]
    row = lax.broadcasted_iota(jnp.int32, fits.shape, 0)
    fits = jnp.where(row == covs + 1, total[:1], fits)
    send_ref[span : span + deep] = fits
    other_ref[span:] = fits


def product_shapes(parts, covs, genes, columns):
    span = genes * (parts // 2 - 1)
    rows = (span + covs + 8 + genes, span + covs + 8, genes)
    return [jax.ShapeDtypeStruct((r, columns), jnp.float32) for r in rows]


def first_products(ids, e, gt, dt, parts):
    rows, width = e.shape
    covs = dt.shape[0]
    columns = LANES + gt.shape[0]
    left = jax.ShapeDtypeStruct((width + covs + 16, rows), jnp.bfloat16)
    return call(
        functools.partial(first_kernel, parts, covs),
        [left] + product_shapes(parts, covs, width // parts, columns),
        "first_products",
        COST["products"],
        (ids, e, gt, dt),
        scratch=[pltpu.VMEM((width, rows), jnp.bfloat16)],
    )


def next_products(left, blocks, parts, covs, tokens):
    rows = left.shape[1]
    width = left.shape[0] - covs - 16
    columns = sum(b.shape[0] for b in blocks)
    return call(
        functools.partial(next_kernel, parts, covs, len(blocks)),
        product_shapes(parts, covs, width // parts, columns),
        "next_products",
        COST["products"],
        (left, *blocks, *tokens),
        scalars=0,
        tokens=len(tokens),
    )


def packed_rows(tall, columns):
    return tall * (columns // LANES) + -(-tall // 16) * 8 if columns % LANES == LANES // 2 and columns > LANES else 0


def pack(block):
    tall, columns = block.shape
    fold = -(-tall // 16) * 8
    whole = columns // LANES
    rest = block[:, whole * LANES :]
    rest = jnp.concatenate([rest, jnp.zeros((2 * fold - tall, LANES // 2), rest.dtype)], axis=0)
    tiles = [block[:, i * LANES : (i + 1) * LANES] for i in range(whole)]
    return jnp.concatenate([*tiles, jnp.concatenate([rest[:fold], rest[fold:]], axis=1)], axis=0)


def unpack(block, tall):
    fold = -(-tall // 16) * 8
    whole = block.shape[0] // tall
    rest = block[whole * tall :]
    rest = jnp.concatenate([rest[:, : LANES // 2], rest[: tall - fold, LANES // 2 :]], axis=0)
    tiles = [block[i * tall : (i + 1) * tall] for i in range(whole)]
    return jnp.concatenate([*tiles, rest], axis=1)


def add_kernel(genes, deep, tokens, other_ref, came_ref, *rest):
    out_refs = rest[tokens:]
    cuts = len(out_refs) * genes // (other_ref.shape[0] - deep)
    span = other_ref.shape[0] - deep
    for i in range(span // genes):
        start = i * genes
        total = other_ref[start : start + genes] + came_ref[start : start + genes]
        fits = other_ref[span:] + came_ref[span : span + deep]
        total = jnp.concatenate([total, fits], axis=0)
        if out_refs[i * cuts].shape[0] > genes + deep:
            total = pack(total)
        row = 0
        for out_ref in out_refs[i * cuts : (i + 1) * cuts]:
            out_ref[...] = total[row : row + out_ref.shape[0]]
            row += out_ref.shape[0]


def add_cores(other, came, genes, deep, cuts, tokens):
    chips = (other.shape[0] - deep) // genes
    tall = genes + deep
    dense = packed_rows(tall, other.shape[1])
    if dense:
        heights, columns, cuts = [dense], LANES, 1
    else:
        heights, columns = [tall] if cuts == 1 else [tall // 16 * 8, tall - tall // 16 * 8], other.shape[1]
    shapes = [jax.ShapeDtypeStruct((h, columns), jnp.float32) for h in heights]
    out = call(
        functools.partial(add_kernel, genes, deep, len(tokens)),
        shapes * chips,
        "add_cores",
        COST["add"],
        (other, came, *tokens),
        scalars=0,
        tokens=len(tokens),
    )
    return [out[i * cuts : (i + 1) * cuts] for i in range(chips)]


def chunk_sums(genes, deep, mine_ref, came_ref, refs):
    tall = genes + deep
    blocks, rows = [], []
    for ref in refs:
        rows.append(unpack(ref[...], tall) if ref.shape[0] > tall else ref[...])
        if sum(r.shape[0] for r in rows) == tall:
            blocks.append(jnp.concatenate(rows, axis=0) if len(rows) > 1 else rows[0])
            rows = []
    corr = mine_ref[...] + came_ref[came_ref.shape[0] - genes :]
    fits = blocks[0][genes:]
    for block in blocks[1:]:
        corr = corr + block[:genes]
        fits = fits + block[genes:]
    return corr, fits


def solve_kernel(covs, dof, weight_ref, mine_ref, came_ref, *rest):
    refs, (bins_ref, folds_ref, solved_ref, scale_ref) = rest[:-4], rest[-4:]
    genes = mine_ref.shape[0]
    rank, deep = covs + 1, covs + 8
    corr, fits = chunk_sums(genes, deep, mine_ref, came_ref, refs)
    cross, gram = corr[:, :LANES], fits[:, :LANES]
    row = lax.broadcasted_iota(jnp.int32, gram.shape, 0)
    lane = lax.broadcasted_iota(jnp.int32, gram.shape, 1)
    inside = jnp.logical_and(row < rank, lane < rank)
    a = jnp.where(inside, gram, jnp.where(row == lane, 1.0, 0.0))
    for k in range(0, rank, 2):
        down0 = jnp.broadcast_to(a[:, k : k + 1], a.shape)
        down1 = jnp.broadcast_to(a[:, k + 1 : k + 2], a.shape)
        p00, p01, p11 = down0[k : k + 1], down1[k : k + 1], down1[k + 1 : k + 2]
        inv = 1.0 / (p00 * p11 - p01 * p01)
        q00, q01, q11 = p11 * inv, -p01 * inv, p00 * inv
        row0, row1 = a[k : k + 1], a[k + 1 : k + 2]
        first = q00 * row0 + q01 * row1
        second = q01 * row0 + q11 * row1
        swept = a - down0 * first - down1 * second
        swept = jnp.where(lane == k, down0 * q00 + down1 * q01, swept)
        swept = jnp.where(lane == k + 1, down0 * q01 + down1 * q11, swept)
        first = jnp.where(lane[:1] == k, -q00, jnp.where(lane[:1] == k + 1, -q01, first))
        second = jnp.where(lane[:1] == k, -q01, jnp.where(lane[:1] == k + 1, -q11, second))
        a = jnp.where(row == k, first, jnp.where(row == k + 1, second, swept))
    inverse = jnp.where(inside, -a, 0.0)
    lane = lax.broadcasted_iota(jnp.int32, cross.shape, 1)
    squares = jnp.sum(jnp.where(lane == rank, cross, 0.0), axis=1, keepdims=True)
    cross = jnp.where(lane < rank, cross, 0.0)
    beta = lax.dot_general(cross, inverse, NT, precision=HIGHEST, preferred_element_type=jnp.float32)
    norm = squares - jnp.sum(beta * cross[:, :deep], axis=1, keepdims=True)
    norm = jnp.maximum(norm, 1e-06 * squares) + EPS
    solved_ref[:genes] = beta
    solved_ref[genes:] = inverse[:, :deep]

    bins, folds = bins_ref[...], folds_ref[...]
    tile = jnp.zeros(bins.shape, jnp.float32)
    for b in range(weight_ref.shape[1]):
        of_bin = jnp.zeros(folds.shape, jnp.float32)
        for f in range(weight_ref.shape[0]):
            of_bin = jnp.where(folds == f, weight_ref[f, b], of_bin)
        tile = jnp.where(bins == b, of_bin, tile)
    tile = tile.T * (dof / norm)
    width = scale_ref.shape[1] // tile.shape[1]
    for t in range(0, tile.shape[1], 2):
        pair = [jnp.broadcast_to(tile[:, i : i + 1], (genes, width)) for i in (t, t + 1)]
        scale_ref[:, t * width : (t + 2) * width] = jnp.concatenate(pair, axis=1)


def solve(weights, mine, came, swapped, bins, folds, covs, dof, variants):
    genes = mine.shape[0]
    outs = [
        jax.ShapeDtypeStruct((genes + covs + 8, covs + 8), jnp.float32),
        jax.ShapeDtypeStruct((genes, variants), jnp.float32),
    ]
    return call(
        functools.partial(solve_kernel, covs, dof),
        outs,
        "solve",
        COST["solve"],
        (weights, mine, came, *swapped, bins, folds),
    )


def fitted_stat(covs, skip, solved_ref, mine_ref, came_ref, refs):
    genes = mine_ref.shape[0]
    corr, fits = chunk_sums(genes, covs + 8, mine_ref, came_ref, refs)
    corr, fits = corr[:, skip:], fits[:, skip:]
    row = lax.broadcasted_iota(jnp.int32, fits.shape, 0)
    squares = fits[covs + 1 : covs + 2]
    fits = jnp.where(row <= covs, fits, 0.0)
    both = lax.dot_general(solved_ref[...], fits, NN, precision=HIGHEST, preferred_element_type=jnp.float32)
    norm = squares - jnp.sum(both[genes:] * fits, axis=0, keepdims=True)
    norm = jnp.maximum(norm, 1e-06 * squares) + EPS
    corr = corr - both[:genes]
    return corr * corr * (1.0 / norm)


def stat_kernel(covs, skip, solved_ref, mine_ref, came_ref, *rest):
    rest[-1][...] = fitted_stat(covs, skip, solved_ref, mine_ref, came_ref, rest[:-1])


def chunk_stat(solved, mine, came, swapped, covs, skip):
    return call(
        functools.partial(stat_kernel, covs, skip),
        jax.ShapeDtypeStruct((mine.shape[0], mine.shape[1] - skip), jnp.float32),
        "chunk_stat",
        COST["stat"],
        (solved, mine, came, *swapped),
        scalars=0,
    )


def slot_of(index, here, ring, order):
    position = {block: i for i, block in enumerate(order)}
    mine = jnp.int32(0)
    for block in range(ring):
        mine = jnp.where(here == block, position[block], mine)
    return lax.rem(position[index] - mine + ring, ring)


def place_kernel(ring, order, ids_ref, scale_ref, *rest):
    stats, (out_ref, held) = rest[:-2], rest[-2:]
    variants = held.shape[2]
    held[ring // 2] = jnp.zeros_like(held[0])
    for k, stat in enumerate(stats):
        if k == 0:
            held[0] = stat[...]
        else:
            held[ring - k] = stat[:, :variants]
            held[k] = stat[:, variants:]
    group = LANES // math.gcd(variants, LANES)
    for j in range(0, ring, group):
        pieces = [held[slot_of(j + b, ids_ref[1], ring, order)] for b in range(group)]
        span = slice(j * variants, (j + group) * variants)
        out_ref[:, span] = jnp.concatenate(pieces, axis=1) * scale_ref[:, span]


def place(ids, scale, stats, ring, order):
    genes, total = scale.shape
    return call(
        functools.partial(place_kernel, ring, order),
        jax.ShapeDtypeStruct(scale.shape, jnp.float32),
        "place",
        COST["place"],
        (ids, scale, *stats),
        scratch=[pltpu.VMEM((ring, genes, total // ring), jnp.float32)],
    )


def finish_kernel(covs, ring, order, ids_ref, solved_ref, scale_ref, placed_ref, mine_ref, came_ref, *rest):
    out_ref = rest[-1]
    variants = mine_ref.shape[1]
    group = LANES // math.gcd(variants, LANES)
    width = group * variants
    stat = fitted_stat(covs, 0, solved_ref, mine_ref, came_ref, rest[:-1])
    out_ref[...] = placed_ref[...]
    index = jnp.int32(0)
    for block in range(ring):
        index = jnp.where(slot_of(block, ids_ref[1], ring, order) == ring // 2, block, index)
    span = pl.ds(pl.multiple_of(index // group * width, LANES), width)
    stat = jnp.concatenate([stat] * group, axis=1)
    lane = lax.broadcasted_iota(jnp.int32, stat.shape, 1)
    first = lax.rem(index, group) * variants
    inside = jnp.logical_and(lane >= first, lane < first + variants)
    out_ref[:, span] = jnp.where(inside, stat * scale_ref[:, span], placed_ref[:, span])


def finish(ids, solved, scale, placed, last, covs, ring, order):
    return call(
        functools.partial(finish_kernel, covs, ring, order),
        jax.ShapeDtypeStruct(scale.shape, jnp.float32),
        "finish",
        COST["finish"],
        (ids, solved, scale, placed, *last),
    )


def shards(order, expression, genotypes, covariates, distance_bins, gene_folds, fold_weights):
    parts, ring = lax.axis_size("samp"), lax.axis_size("var")
    rows, width = expression.shape
    covs = covariates.shape[1]
    genes = width // parts
    deep = covs + 8
    dof = float(rows * parts - covs - 2)
    gt = genotypes.T
    variants = gt.shape[0]
    middle = ring // 2
    ids = jnp.stack([lax.axis_index("samp"), lax.axis_index("var")]).astype(jnp.int32)

    def exchange(x, d):
        return lax.ppermute(x, "samp", [(s, s ^ d) for s in range(parts)])

    forward = [(order[i], order[(i + 1) % ring]) for i in range(ring)]
    backward = [(b, a) for a, b in forward]

    def right(x):
        return lax.ppermute(x, "var", forward)

    def left(x):
        return lax.ppermute(x, "var", backward)

    stats = []
    lhs = solved = scale = None

    done = {}

    def starts(k):
        return [("came", 0) if k == 1 else ("got", 0) if k == 2 else ("sent", k - 1)]

    def turns(k):
        return ([("got", k - 2)] if 1 < k < middle else []) + ([("solved", 0)] if k == middle - 1 else [])

    def ends(k):
        return [("got", k - 2)] if k == middle else []

    def after(*names):
        return [done[name] for name in names if name in done]

    block = (gt, gt)
    for k in range(middle + 1):
        if k > 0:
            block = gate(block, after(*turns(k)))
        if k < middle - 1:
            ahead = (right(block[0]), left(block[-1]))
        elif k == middle - 1:
            ahead = (right(block[0][: variants // 2]), left(block[-1][variants // 2 :]))
        if k == 0:
            lhs, send, other, mine = first_products(ids, expression, gt, covariates.T, parts)
        else:
            tokens = after(*starts(k))
            send, other, mine = next_products(lhs, block, parts, covs, tokens)
        came = exchange(send, 1)
        sent = add_cores(other, came, genes, deep, 1, after(*ends(k)))
        got = [[exchange(x, 2 * (i + 1)) for x in cut] for i, cut in enumerate(sent)]
        swapped = [*sent[0], *sum(got, [])]
        done["came", k], done["sent", k] = came, sent[0][0]
        done["got", k], done["rest", k] = got[-1][0], got[-1][-1]
        if k == 0:
            solved, scale = solve(
                fold_weights, mine, came, swapped, distance_bins, gene_folds[None], covs, dof, ring * variants
            )
            done["solved", 0] = solved
        if k < middle:
            stats.append(chunk_stat(solved, mine, came, swapped, covs, LANES if k == 0 else 0))
            done["stat", k] = stats[k]
            block = ahead
    placed = place(ids, scale, stats, ring, tuple(order))
    return finish(ids, solved, scale, placed, (mine, came, *swapped), covs, ring, tuple(order))


def solution(mesh):
    return jax.shard_map(
        functools.partial(shards, ring_order(mesh)),
        mesh=mesh,
        in_specs=(
            P(("groups", "samp"), "var"),
            P(("groups", "samp"), "var"),
            P(("groups", "samp"), None),
            P("groups", ("var", "samp")),
            P(("groups", "var", "samp")),
            P(),
        ),
        out_specs=P(("groups", "var", "samp"), None),
        check_vma=False,
    )
```

```python
import functools
import math

import jax
import jax.numpy as jnp
from jax import lax
from jax.experimental import pallas as pl
from jax.experimental.pallas import tpu as pltpu
from jax.sharding import PartitionSpec as P

LANES = 128
EPS = 1e-06
COST = {'products': 10**8, 'add': 1, 'solve': 10**8, 'stat': 1, 'place': 1, 'finish': 1, 'gate': 10**10}
VMEM_LIMIT = 10 * 1024 * 1024

NT = (((1,), (1,)), ((), ()))
NN = (((1,), (0,)), ((), ()))
HIGHEST = lax.Precision.HIGHEST


def ring_order(mesh):
    members = list(mesh.devices[0, 0])
    places = [getattr(device, "coords", None) for device in members]
    if len(members) < 2 or any(place is None for place in places):
        return list(range(len(members)))
    axis = [i for i in range(len(places[0])) if places[0][i] != places[1][i]][0]
    columns = {}
    for index, place in enumerate(places):
        columns.setdefault(place[axis], []).append(index)
    order = []
    for step, key in enumerate(sorted(columns)):
        order += columns[key] if step % 2 == 0 else columns[key][::-1]
    return order


def call(kernel, out_shape, name, flops, operands, scratch=(), scalars=1, tokens=0):
    vmem = pl.BlockSpec(memory_space=pltpu.VMEM)
    smem = pl.BlockSpec(memory_space=pltpu.SMEM)
    rest = len(operands) - scalars - tokens
    return pl.pallas_call(
        kernel,
        out_shape=out_shape,
        in_specs=[smem] * scalars + [vmem] * rest + [pl.BlockSpec(memory_space=pl.ANY)] * tokens,
        out_specs=jax.tree.map(lambda _: vmem, out_shape),
        scratch_shapes=list(scratch),
        compiler_params=pltpu.CompilerParams(vmem_limit_bytes=VMEM_LIMIT),
        cost_estimate=pl.CostEstimate(flops=flops, bytes_accessed=0, transcendentals=0),
        name=name,
    )(*operands)


def gate_kernel(*refs):
    pass


def gate(blocks, tokens):
    vmem = pl.BlockSpec(memory_space=pltpu.VMEM)
    return pl.pallas_call(
        gate_kernel,
        out_shape=[jax.ShapeDtypeStruct(b.shape, b.dtype) for b in blocks],
        in_specs=[vmem] * len(blocks) + [pl.BlockSpec(memory_space=pl.ANY)] * len(tokens),
        out_specs=[vmem] * len(blocks),
        input_output_aliases={i: i for i in range(len(blocks))},
        compiler_params=pltpu.CompilerParams(vmem_limit_bytes=VMEM_LIMIT),
        cost_estimate=pl.CostEstimate(flops=COST["gate"], bytes_accessed=0, transcendentals=0),
        name="gate",
    )(*blocks, *tokens)


def first_kernel(parts, covs, ids_ref, e_ref, gt_ref, dt_ref, left_ref, send_ref, other_ref, mine_ref, wide):
    width = e_ref.shape[1]
    genes = width // parts
    sid = ids_ref[0]
    wide[...] = e_ref[...].T
    owners = [sid ^ 1 ^ d for d in range(2, parts, 2)] + [sid ^ 1]
    owners += [sid ^ d for d in range(2, parts, 2)] + [sid]
    for i, owner in enumerate(owners):
        start = pl.multiple_of(owner * genes, 16)
        left_ref[i * genes : (i + 1) * genes] = wide[pl.ds(start, genes), :]
    rows = dt_ref.shape[1]
    left_ref[width : width + covs] = dt_ref[...]
    first = lax.broadcasted_iota(jnp.int32, (16, rows), 0) == 0
    left_ref[width + covs :] = first.astype(jnp.float32).astype(jnp.bfloat16)
    design = left_ref[width:]
    right = jnp.concatenate([design, jnp.zeros((LANES - design.shape[0], rows), jnp.bfloat16)], axis=0)
    right = jnp.concatenate([right, gt_ref[...]], axis=0)
    split(parts, covs, genes, left_ref, right, send_ref, other_ref, mine_ref, True)


def next_kernel(parts, covs, blocks, left_ref, *rest):
    right = jnp.concatenate([ref[...] for ref in rest[:blocks]], axis=0)
    send_ref, other_ref, mine_ref = rest[-3:]
    genes = mine_ref.shape[0]
    split(parts, covs, genes, left_ref, right, send_ref, other_ref, mine_ref, False)


def split(parts, covs, genes, left_ref, right, send_ref, other_ref, mine_ref, squares):
    width = genes * parts
    span = genes * (parts // 2 - 1)
    deep = covs + 8

    prod = lax.dot_general(left_ref[...], right, NT, preferred_element_type=jnp.float32)
    outs = prod[:width]
    if squares:
        a = left_ref[:width].astype(jnp.float32)
        lane = lax.broadcasted_iota(jnp.int32, outs.shape, 1)
        outs = jnp.where(lane == covs + 1, jnp.sum(a * a, axis=1, keepdims=True), outs)
    send_ref[:span] = outs[:span]
    send_ref[span + deep :] = outs[span : span + genes]
    other_ref[:span] = outs[span + genes : 2 * span + genes]
    mine_ref[...] = outs[2 * span + genes :]
    square = right.astype(jnp.float32)
    square = square * square
    high = square.astype(jnp.bfloat16)
    low = (square - high.astype(jnp.float32)).astype(jnp.bfloat16)
    ones = jnp.ones((16, right.shape[1]), jnp.bfloat16)
    total = lax.dot_general(ones, high, NT, preferred_element_type=jnp.float32)
    total += lax.dot_general(ones, low, NT, preferred_element_type=jnp.float32)
    fits = prod[width : width + deep]
    row = lax.broadcasted_iota(jnp.int32, fits.shape, 0)
    fits = jnp.where(row == covs + 1, total[:1], fits)
    send_ref[span : span + deep] = fits
    other_ref[span:] = fits


def product_shapes(parts, covs, genes, columns):
    span = genes * (parts // 2 - 1)
    rows = (span + covs + 8 + genes, span + covs + 8, genes)
    return [jax.ShapeDtypeStruct((r, columns), jnp.float32) for r in rows]


def first_products(ids, e, gt, dt, parts):
    rows, width = e.shape
    covs = dt.shape[0]
    columns = LANES + gt.shape[0]
    left = jax.ShapeDtypeStruct((width + covs + 16, rows), jnp.bfloat16)
    return call(
        functools.partial(first_kernel, parts, covs),
        [left] + product_shapes(parts, covs, width // parts, columns),
        "first_products",
        COST["products"],
        (ids, e, gt, dt),
        scratch=[pltpu.VMEM((width, rows), jnp.bfloat16)],
    )


def next_products(left, blocks, parts, covs, tokens):
    rows = left.shape[1]
    width = left.shape[0] - covs - 16
    columns = sum(b.shape[0] for b in blocks)
    return call(
        functools.partial(next_kernel, parts, covs, len(blocks)),
        product_shapes(parts, covs, width // parts, columns),
        "next_products",
        COST["products"],
        (left, *blocks, *tokens),
        scalars=0,
        tokens=len(tokens),
    )


def packed_rows(tall, columns):
    return tall * (columns // LANES) + -(-tall // 16) * 8 if columns % LANES == LANES // 2 and columns > LANES else 0


def pack(block):
    tall, columns = block.shape
    fold = -(-tall // 16) * 8
    whole = columns // LANES
    rest = block[:, whole * LANES :]
    rest = jnp.concatenate([rest, jnp.zeros((2 * fold - tall, LANES // 2), rest.dtype)], axis=0)
    tiles = [block[:, i * LANES : (i + 1) * LANES] for i in range(whole)]
    return jnp.concatenate([*tiles, jnp.concatenate([rest[:fold], rest[fold:]], axis=1)], axis=0)


def unpack(block, tall):
    fold = -(-tall // 16) * 8
    whole = block.shape[0] // tall
    rest = block[whole * tall :]
    rest = jnp.concatenate([rest[:, : LANES // 2], rest[: tall - fold, LANES // 2 :]], axis=0)
    tiles = [block[i * tall : (i + 1) * tall] for i in range(whole)]
    return jnp.concatenate([*tiles, rest], axis=1)


def add_kernel(genes, deep, tokens, other_ref, came_ref, *rest):
    out_refs = rest[tokens:]
    cuts = len(out_refs) * genes // (other_ref.shape[0] - deep)
    span = other_ref.shape[0] - deep
    for i in range(span // genes):
        start = i * genes
        total = other_ref[start : start + genes] + came_ref[start : start + genes]
        fits = other_ref[span:] + came_ref[span : span + deep]
        total = jnp.concatenate([total, fits], axis=0)
        if out_refs[i * cuts].shape[0] > genes + deep:
            total = pack(total)
        row = 0
        for out_ref in out_refs[i * cuts : (i + 1) * cuts]:
            out_ref[...] = total[row : row + out_ref.shape[0]]
            row += out_ref.shape[0]


def add_cores(other, came, genes, deep, cuts, tokens):
    chips = (other.shape[0] - deep) // genes
    tall = genes + deep
    dense = packed_rows(tall, other.shape[1])
    if dense:
        heights, columns, cuts = [dense], LANES, 1
    else:
        heights, columns = [tall] if cuts == 1 else [tall // 16 * 8, tall - tall // 16 * 8], other.shape[1]
    shapes = [jax.ShapeDtypeStruct((h, columns), jnp.float32) for h in heights]
    out = call(
        functools.partial(add_kernel, genes, deep, len(tokens)),
        shapes * chips,
        "add_cores",
        COST["add"],
        (other, came, *tokens),
        scalars=0,
        tokens=len(tokens),
    )
    return [out[i * cuts : (i + 1) * cuts] for i in range(chips)]


def chunk_sums(genes, deep, mine_ref, came_ref, refs):
    tall = genes + deep
    blocks, rows = [], []
    for ref in refs:
        rows.append(unpack(ref[...], tall) if ref.shape[0] > tall else ref[...])
        if sum(r.shape[0] for r in rows) == tall:
            blocks.append(jnp.concatenate(rows, axis=0) if len(rows) > 1 else rows[0])
            rows = []
    corr = mine_ref[...] + came_ref[came_ref.shape[0] - genes :]
    fits = blocks[0][genes:]
    for block in blocks[1:]:
        corr = corr + block[:genes]
        fits = fits + block[genes:]
    return corr, fits


def solve_kernel(covs, dof, mine_ref, came_ref, *rest):
    refs, (solved_ref, norm_ref) = rest[:-2], rest[-2:]
    genes = mine_ref.shape[0]
    rank, deep = covs + 1, covs + 8
    corr, fits = chunk_sums(genes, deep, mine_ref, came_ref, refs)
    cross, gram = corr[:, :LANES], fits[:, :LANES]
    row = lax.broadcasted_iota(jnp.int32, gram.shape, 0)
    lane = lax.broadcasted_iota(jnp.int32, gram.shape, 1)
    inside = jnp.logical_and(row < rank, lane < rank)
    a = jnp.where(inside, gram, jnp.where(row == lane, 1.0, 0.0))
    for k in range(0, rank, 2):
        down0 = jnp.broadcast_to(a[:, k : k + 1], a.shape)
        down1 = jnp.broadcast_to(a[:, k + 1 : k + 2], a.shape)
        p00, p01, p11 = down0[k : k + 1], down1[k : k + 1], down1[k + 1 : k + 2]
        inv = 1.0 / (p00 * p11 - p01 * p01)
        q00, q01, q11 = p11 * inv, -p01 * inv, p00 * inv
        row0, row1 = a[k : k + 1], a[k + 1 : k + 2]
        first = q00 * row0 + q01 * row1
        second = q01 * row0 + q11 * row1
        swept = a - down0 * first - down1 * second
        swept = jnp.where(lane == k, down0 * q00 + down1 * q01, swept)
        swept = jnp.where(lane == k + 1, down0 * q01 + down1 * q11, swept)
        first = jnp.where(lane[:1] == k, -q00, jnp.where(lane[:1] == k + 1, -q01, first))
        second = jnp.where(lane[:1] == k, -q01, jnp.where(lane[:1] == k + 1, -q11, second))
        a = jnp.where(row == k, first, jnp.where(row == k + 1, second, swept))
    inverse = jnp.where(inside, -a, 0.0)
    lane = lax.broadcasted_iota(jnp.int32, cross.shape, 1)
    squares = jnp.sum(jnp.where(lane == rank, cross, 0.0), axis=1, keepdims=True)
    cross = jnp.where(lane < rank, cross, 0.0)
    beta = lax.dot_general(cross, inverse, NT, precision=HIGHEST, preferred_element_type=jnp.float32)
    norm = squares - jnp.sum(beta * cross[:, :deep], axis=1, keepdims=True)
    norm = jnp.maximum(norm, 1e-06 * squares) + EPS
    solved_ref[:genes] = beta
    solved_ref[genes:] = inverse[:, :deep]

    norm_ref[...] = jnp.broadcast_to(dof / norm, norm_ref.shape)


def solve(mine, came, swapped, covs, dof):
    genes = mine.shape[0]
    outs = [
        jax.ShapeDtypeStruct((genes + covs + 8, covs + 8), jnp.float32),
        jax.ShapeDtypeStruct((genes, LANES), jnp.float32),
    ]
    return call(
        functools.partial(solve_kernel, covs, dof),
        outs,
        "solve",
        COST["solve"],
        (mine, came, *swapped),
        scalars=0,
    )


def widen_kernel(weight_ref, norm_ref, bins_ref, folds_ref, scale_ref):
    bins, folds = bins_ref[...], folds_ref[...]
    tile = jnp.zeros(bins.shape, jnp.float32)
    for b in range(weight_ref.shape[1]):
        of_bin = jnp.zeros(folds.shape, jnp.float32)
        for f in range(weight_ref.shape[0]):
            of_bin = jnp.where(folds == f, weight_ref[f, b], of_bin)
        tile = jnp.where(bins == b, of_bin, tile)
    tile = tile.T * norm_ref[:, :1]
    genes, width = tile.shape[0], scale_ref.shape[1] // tile.shape[1]
    for t in range(0, tile.shape[1], 2):
        pair = [jnp.broadcast_to(tile[:, i : i + 1], (genes, width)) for i in (t, t + 1)]
        scale_ref[:, t * width : (t + 2) * width] = jnp.concatenate(pair, axis=1)


def widen(weights, norm, bins, folds, variants):
    return call(
        widen_kernel,
        jax.ShapeDtypeStruct((norm.shape[0], variants), jnp.float32),
        "widen",
        COST["place"],
        (weights, norm, bins, folds),
    )


def fitted_stat(covs, skip, solved_ref, mine_ref, came_ref, refs):
    genes = mine_ref.shape[0]
    corr, fits = chunk_sums(genes, covs + 8, mine_ref, came_ref, refs)
    corr, fits = corr[:, skip:], fits[:, skip:]
    row = lax.broadcasted_iota(jnp.int32, fits.shape, 0)
    squares = fits[covs + 1 : covs + 2]
    fits = jnp.where(row <= covs, fits, 0.0)
    both = lax.dot_general(solved_ref[...], fits, NN, precision=HIGHEST, preferred_element_type=jnp.float32)
    norm = squares - jnp.sum(both[genes:] * fits, axis=0, keepdims=True)
    norm = jnp.maximum(norm, 1e-06 * squares) + EPS
    corr = corr - both[:genes]
    return corr * corr * (1.0 / norm)


def stat_kernel(covs, skip, solved_ref, mine_ref, came_ref, *rest):
    rest[-1][...] = fitted_stat(covs, skip, solved_ref, mine_ref, came_ref, rest[:-1])


def chunk_stat(solved, mine, came, swapped, covs, skip):
    return call(
        functools.partial(stat_kernel, covs, skip),
        jax.ShapeDtypeStruct((mine.shape[0], mine.shape[1] - skip), jnp.float32),
        "chunk_stat",
        COST["stat"],
        (solved, mine, came, *swapped),
        scalars=0,
    )


def slot_of(index, here, ring, order):
    position = {block: i for i, block in enumerate(order)}
    mine = jnp.int32(0)
    for block in range(ring):
        mine = jnp.where(here == block, position[block], mine)
    return lax.rem(position[index] - mine + ring, ring)


def place_kernel(ring, order, ids_ref, scale_ref, *rest):
    stats, (out_ref, held) = rest[:-2], rest[-2:]
    variants = held.shape[2]
    held[ring // 2] = jnp.zeros_like(held[0])
    for k, stat in enumerate(stats):
        if k == 0:
            held[0] = stat[...]
        else:
            held[ring - k] = stat[:, :variants]
            held[k] = stat[:, variants:]
    group = LANES // math.gcd(variants, LANES)
    for j in range(0, ring, group):
        pieces = [held[slot_of(j + b, ids_ref[1], ring, order)] for b in range(group)]
        span = slice(j * variants, (j + group) * variants)
        out_ref[:, span] = jnp.concatenate(pieces, axis=1) * scale_ref[:, span]


def place(ids, scale, stats, ring, order):
    genes, total = scale.shape
    return call(
        functools.partial(place_kernel, ring, order),
        jax.ShapeDtypeStruct(scale.shape, jnp.float32),
        "place",
        COST["place"],
        (ids, scale, *stats),
        scratch=[pltpu.VMEM((ring, genes, total // ring), jnp.float32)],
    )


def finish_kernel(covs, ring, order, ids_ref, solved_ref, scale_ref, placed_ref, mine_ref, came_ref, *rest):
    out_ref = rest[-1]
    variants = mine_ref.shape[1]
    group = LANES // math.gcd(variants, LANES)
    width = group * variants
    stat = fitted_stat(covs, 0, solved_ref, mine_ref, came_ref, rest[:-1])
    out_ref[...] = placed_ref[...]
    index = jnp.int32(0)
    for block in range(ring):
        index = jnp.where(slot_of(block, ids_ref[1], ring, order) == ring // 2, block, index)
    span = pl.ds(pl.multiple_of(index // group * width, LANES), width)
    stat = jnp.concatenate([stat] * group, axis=1)
    lane = lax.broadcasted_iota(jnp.int32, stat.shape, 1)
    first = lax.rem(index, group) * variants
    inside = jnp.logical_and(lane >= first, lane < first + variants)
    out_ref[:, span] = jnp.where(inside, stat * scale_ref[:, span], placed_ref[:, span])


def finish(ids, solved, scale, placed, last, covs, ring, order):
    return call(
        functools.partial(finish_kernel, covs, ring, order),
        jax.ShapeDtypeStruct(scale.shape, jnp.float32),
        "finish",
        COST["finish"],
        (ids, solved, scale, placed, *last),
    )


def shards(order, expression, genotypes, covariates, distance_bins, gene_folds, fold_weights):
    parts, ring = lax.axis_size("samp"), lax.axis_size("var")
    rows, width = expression.shape
    covs = covariates.shape[1]
    genes = width // parts
    deep = covs + 8
    dof = float(rows * parts - covs - 2)
    gt = genotypes.T
    variants = gt.shape[0]
    middle = ring // 2
    ids = jnp.stack([lax.axis_index("samp"), lax.axis_index("var")]).astype(jnp.int32)

    def exchange(x, d):
        return lax.ppermute(x, "samp", [(s, s ^ d) for s in range(parts)])

    forward = [(order[i], order[(i + 1) % ring]) for i in range(ring)]
    backward = [(b, a) for a, b in forward]

    def right(x):
        return lax.ppermute(x, "var", forward)

    def left(x):
        return lax.ppermute(x, "var", backward)

    stats = []
    lhs = solved = scale = None

    done = {}

    def starts(k):
        return [("came", 0) if k == 1 else ("got", 0) if k == 2 else ("sent", k - 1)]

    def turns(k):
        return ([("got", k - 2)] if 1 < k < middle else []) + ([("solved", 0)] if k == middle - 1 else [])

    def ends(k):
        return [("got", k - 2)] if k == middle else []

    def after(*names):
        return [done[name] for name in names if name in done]

    block = (gt, gt)
    for k in range(middle + 1):
        if k > 0:
            block = gate(block, after(*turns(k)))
        if k < middle - 1:
            ahead = (right(block[0]), left(block[-1]))
        elif k == middle - 1:
            ahead = (right(block[0][: variants // 2]), left(block[-1][variants // 2 :]))
        if k == 0:
            lhs, send, other, mine = first_products(ids, expression, gt, covariates.T, parts)
        else:
            tokens = after(*starts(k))
            send, other, mine = next_products(lhs, block, parts, covs, tokens)
        came = exchange(send, 1)
        sent = add_cores(other, came, genes, deep, 1, after(*ends(k)))
        got = [[exchange(x, 2 * (i + 1)) for x in cut] for i, cut in enumerate(sent)]
        swapped = [*sent[0], *sum(got, [])]
        done["came", k], done["sent", k] = came, sent[0][0]
        done["got", k], done["rest", k] = got[-1][0], got[-1][-1]
        if k == 0:
            solved, norm = solve(mine, came, swapped, covs, dof)
            scale = widen(fold_weights, norm, distance_bins, gene_folds[None], ring * variants)
            done["solved", 0] = solved
        if k < middle:
            stats.append(chunk_stat(solved, mine, came, swapped, covs, LANES if k == 0 else 0))
            done["stat", k] = stats[k]
            block = ahead
    placed = place(ids, scale, stats, ring, tuple(order))
    return finish(ids, solved, scale, placed, (mine, came, *swapped), covs, ring, tuple(order))


def solution(mesh):
    return jax.shard_map(
        functools.partial(shards, ring_order(mesh)),
        mesh=mesh,
        in_specs=(
            P(("groups", "samp"), "var"),
            P(("groups", "samp"), "var"),
            P(("groups", "samp"), None),
            P("groups", ("var", "samp")),
            P(("groups", "var", "samp")),
            P(),
        ),
        out_specs=P(("groups", "var", "samp"), None),
        check_vma=False,
    )
```

```python
import functools
import math

import jax
import jax.numpy as jnp
from jax import lax
from jax.experimental import pallas as pl
from jax.experimental.pallas import tpu as pltpu
from jax.sharding import PartitionSpec as P

LANES = 128
EPS = 1e-06
COST = {'products': 10**8, 'add': 1, 'solve': 10**8, 'stat': 1, 'place': 1, 'finish': 1, 'gate': 10**10}
VMEM_LIMIT = 10 * 1024 * 1024

NT = (((1,), (1,)), ((), ()))
NN = (((1,), (0,)), ((), ()))
HIGHEST = lax.Precision.HIGHEST


def ring_order(mesh):
    members = list(mesh.devices[0, 0])
    places = [getattr(device, "coords", None) for device in members]
    if len(members) < 2 or any(place is None for place in places):
        return list(range(len(members)))
    axis = [i for i in range(len(places[0])) if places[0][i] != places[1][i]][0]
    columns = {}
    for index, place in enumerate(places):
        columns.setdefault(place[axis], []).append(index)
    order = []
    for step, key in enumerate(sorted(columns)):
        order += columns[key] if step % 2 == 0 else columns[key][::-1]
    return order


def call(kernel, out_shape, name, flops, operands, scratch=(), scalars=1, tokens=0):
    vmem = pl.BlockSpec(memory_space=pltpu.VMEM)
    smem = pl.BlockSpec(memory_space=pltpu.SMEM)
    rest = len(operands) - scalars - tokens
    return pl.pallas_call(
        kernel,
        out_shape=out_shape,
        in_specs=[smem] * scalars + [vmem] * rest + [pl.BlockSpec(memory_space=pl.ANY)] * tokens,
        out_specs=jax.tree.map(lambda _: vmem, out_shape),
        scratch_shapes=list(scratch),
        compiler_params=pltpu.CompilerParams(vmem_limit_bytes=VMEM_LIMIT),
        cost_estimate=pl.CostEstimate(flops=flops, bytes_accessed=0, transcendentals=0),
        name=name,
    )(*operands)


def gate_kernel(*refs):
    pass


def gate(blocks, tokens):
    vmem = pl.BlockSpec(memory_space=pltpu.VMEM)
    return pl.pallas_call(
        gate_kernel,
        out_shape=[jax.ShapeDtypeStruct(b.shape, b.dtype) for b in blocks],
        in_specs=[vmem] * len(blocks) + [pl.BlockSpec(memory_space=pl.ANY)] * len(tokens),
        out_specs=[vmem] * len(blocks),
        input_output_aliases={i: i for i in range(len(blocks))},
        compiler_params=pltpu.CompilerParams(vmem_limit_bytes=VMEM_LIMIT),
        cost_estimate=pl.CostEstimate(flops=COST["gate"], bytes_accessed=0, transcendentals=0),
        name="gate",
    )(*blocks, *tokens)


def first_kernel(parts, covs, ids_ref, e_ref, gt_ref, dt_ref, left_ref, send_ref, other_ref, mine_ref, wide):
    width = e_ref.shape[1]
    genes = width // parts
    sid = ids_ref[0]
    wide[...] = e_ref[...].T
    owners = [sid ^ 1 ^ d for d in range(2, parts, 2)] + [sid ^ 1]
    owners += [sid ^ d for d in range(2, parts, 2)] + [sid]
    for i, owner in enumerate(owners):
        start = pl.multiple_of(owner * genes, 16)
        left_ref[i * genes : (i + 1) * genes] = wide[pl.ds(start, genes), :]
    rows = dt_ref.shape[1]
    left_ref[width : width + covs] = dt_ref[...]
    first = lax.broadcasted_iota(jnp.int32, (16, rows), 0) == 0
    left_ref[width + covs :] = first.astype(jnp.float32).astype(jnp.bfloat16)
    design = left_ref[width:]
    right = jnp.concatenate([design, jnp.zeros((LANES - design.shape[0], rows), jnp.bfloat16)], axis=0)
    right = jnp.concatenate([right, gt_ref[...]], axis=0)
    split(parts, covs, genes, left_ref, right, send_ref, other_ref, mine_ref, True)


def next_kernel(parts, covs, blocks, left_ref, *rest):
    right = jnp.concatenate([ref[...] for ref in rest[:blocks]], axis=0)
    send_ref, other_ref, mine_ref = rest[-3:]
    genes = mine_ref.shape[0]
    split(parts, covs, genes, left_ref, right, send_ref, other_ref, mine_ref, False)


def split(parts, covs, genes, left_ref, right, send_ref, other_ref, mine_ref, squares):
    width = genes * parts
    span = genes * (parts // 2 - 1)
    deep = covs + 8

    prod = lax.dot_general(left_ref[...], right, NT, preferred_element_type=jnp.float32)
    outs = prod[:width]
    if squares:
        a = left_ref[:width].astype(jnp.float32)
        lane = lax.broadcasted_iota(jnp.int32, outs.shape, 1)
        outs = jnp.where(lane == covs + 1, jnp.sum(a * a, axis=1, keepdims=True), outs)
    send_ref[:span] = outs[:span]
    send_ref[span + deep :] = outs[span : span + genes]
    other_ref[:span] = outs[span + genes : 2 * span + genes]
    mine_ref[...] = outs[2 * span + genes :]
    square = right.astype(jnp.float32)
    square = square * square
    high = square.astype(jnp.bfloat16)
    low = (square - high.astype(jnp.float32)).astype(jnp.bfloat16)
    ones = jnp.ones((16, right.shape[1]), jnp.bfloat16)
    total = lax.dot_general(ones, high, NT, preferred_element_type=jnp.float32)
    total += lax.dot_general(ones, low, NT, preferred_element_type=jnp.float32)
    fits = prod[width : width + deep]
    row = lax.broadcasted_iota(jnp.int32, fits.shape, 0)
    fits = jnp.where(row == covs + 1, total[:1], fits)
    send_ref[span : span + deep] = fits
    other_ref[span:] = fits


def product_shapes(parts, covs, genes, columns):
    span = genes * (parts // 2 - 1)
    rows = (span + covs + 8 + genes, span + covs + 8, genes)
    return [jax.ShapeDtypeStruct((r, columns), jnp.float32) for r in rows]


def first_products(ids, e, gt, dt, parts):
    rows, width = e.shape
    covs = dt.shape[0]
    columns = LANES + gt.shape[0]
    left = jax.ShapeDtypeStruct((width + covs + 16, rows), jnp.bfloat16)
    return call(
        functools.partial(first_kernel, parts, covs),
        [left] + product_shapes(parts, covs, width // parts, columns),
        "first_products",
        COST["products"],
        (ids, e, gt, dt),
        scratch=[pltpu.VMEM((width, rows), jnp.bfloat16)],
    )


def next_products(left, blocks, parts, covs, tokens):
    rows = left.shape[1]
    width = left.shape[0] - covs - 16
    columns = sum(b.shape[0] for b in blocks)
    return call(
        functools.partial(next_kernel, parts, covs, len(blocks)),
        product_shapes(parts, covs, width // parts, columns),
        "next_products",
        COST["products"],
        (left, *blocks, *tokens),
        scalars=0,
        tokens=len(tokens),
    )


def packed_rows(tall, columns):
    return tall * (columns // LANES) + -(-tall // 16) * 8 if columns % LANES == LANES // 2 and columns > LANES else 0


def pack(block):
    tall, columns = block.shape
    fold = -(-tall // 16) * 8
    whole = columns // LANES
    rest = block[:, whole * LANES :]
    rest = jnp.concatenate([rest, jnp.zeros((2 * fold - tall, LANES // 2), rest.dtype)], axis=0)
    tiles = [block[:, i * LANES : (i + 1) * LANES] for i in range(whole)]
    return jnp.concatenate([*tiles, jnp.concatenate([rest[:fold], rest[fold:]], axis=1)], axis=0)


def unpack(block, tall):
    fold = -(-tall // 16) * 8
    whole = block.shape[0] // tall
    rest = block[whole * tall :]
    rest = jnp.concatenate([rest[:, : LANES // 2], rest[: tall - fold, LANES // 2 :]], axis=0)
    tiles = [block[i * tall : (i + 1) * tall] for i in range(whole)]
    return jnp.concatenate([*tiles, rest], axis=1)


def add_kernel(genes, deep, tokens, other_ref, came_ref, *rest):
    out_refs = rest[tokens:]
    cuts = len(out_refs) * genes // (other_ref.shape[0] - deep)
    span = other_ref.shape[0] - deep
    for i in range(span // genes):
        start = i * genes
        total = other_ref[start : start + genes] + came_ref[start : start + genes]
        fits = other_ref[span:] + came_ref[span : span + deep]
        total = jnp.concatenate([total, fits], axis=0)
        if out_refs[i * cuts].shape[0] > genes + deep:
            total = pack(total)
        row = 0
        for out_ref in out_refs[i * cuts : (i + 1) * cuts]:
            out_ref[...] = total[row : row + out_ref.shape[0]]
            row += out_ref.shape[0]


def add_cores(other, came, genes, deep, cuts, tokens):
    chips = (other.shape[0] - deep) // genes
    tall = genes + deep
    dense = packed_rows(tall, other.shape[1])
    if dense:
        heights, columns, cuts = [dense], LANES, 1
    else:
        heights, columns = [tall] if cuts == 1 else [tall // 16 * 8, tall - tall // 16 * 8], other.shape[1]
    shapes = [jax.ShapeDtypeStruct((h, columns), jnp.float32) for h in heights]
    out = call(
        functools.partial(add_kernel, genes, deep, len(tokens)),
        shapes * chips,
        "add_cores",
        COST["add"],
        (other, came, *tokens),
        scalars=0,
        tokens=len(tokens),
    )
    return [out[i * cuts : (i + 1) * cuts] for i in range(chips)]


def chunk_sums(genes, deep, mine_ref, came_ref, refs):
    tall = genes + deep
    blocks, rows = [], []
    for ref in refs:
        rows.append(unpack(ref[...], tall) if ref.shape[0] > tall else ref[...])
        if sum(r.shape[0] for r in rows) == tall:
            blocks.append(jnp.concatenate(rows, axis=0) if len(rows) > 1 else rows[0])
            rows = []
    corr = mine_ref[...] + came_ref[came_ref.shape[0] - genes :]
    fits = blocks[0][genes:]
    for block in blocks[1:]:
        corr = corr + block[:genes]
        fits = fits + block[genes:]
    return corr, fits


def solve_kernel(covs, dof, mine_ref, came_ref, *rest):
    refs, (solved_ref, norm_ref) = rest[:-2], rest[-2:]
    genes = mine_ref.shape[0]
    rank, deep = covs + 1, covs + 8
    corr, fits = chunk_sums(genes, deep, mine_ref, came_ref, refs)
    cross, gram = corr[:, :LANES], fits[:, :LANES]
    row = lax.broadcasted_iota(jnp.int32, gram.shape, 0)
    lane = lax.broadcasted_iota(jnp.int32, gram.shape, 1)
    inside = jnp.logical_and(row < rank, lane < rank)
    a = jnp.where(inside, gram, jnp.where(row == lane, 1.0, 0.0))
    for k in range(0, rank, 2):
        down0 = jnp.broadcast_to(a[:, k : k + 1], a.shape)
        down1 = jnp.broadcast_to(a[:, k + 1 : k + 2], a.shape)
        p00, p01, p11 = down0[k : k + 1], down1[k : k + 1], down1[k + 1 : k + 2]
        inv = 1.0 / (p00 * p11 - p01 * p01)
        q00, q01, q11 = p11 * inv, -p01 * inv, p00 * inv
        row0, row1 = a[k : k + 1], a[k + 1 : k + 2]
        first = q00 * row0 + q01 * row1
        second = q01 * row0 + q11 * row1
        swept = a - down0 * first - down1 * second
        swept = jnp.where(lane == k, down0 * q00 + down1 * q01, swept)
        swept = jnp.where(lane == k + 1, down0 * q01 + down1 * q11, swept)
        first = jnp.where(lane[:1] == k, -q00, jnp.where(lane[:1] == k + 1, -q01, first))
        second = jnp.where(lane[:1] == k, -q01, jnp.where(lane[:1] == k + 1, -q11, second))
        a = jnp.where(row == k, first, jnp.where(row == k + 1, second, swept))
    inverse = jnp.where(inside, -a, 0.0)
    lane = lax.broadcasted_iota(jnp.int32, cross.shape, 1)
    squares = jnp.sum(jnp.where(lane == rank, cross, 0.0), axis=1, keepdims=True)
    cross = jnp.where(lane < rank, cross, 0.0)
    beta = lax.dot_general(cross, inverse, NT, precision=HIGHEST, preferred_element_type=jnp.float32)
    norm = squares - jnp.sum(beta * cross[:, :deep], axis=1, keepdims=True)
    norm = jnp.maximum(norm, 1e-06 * squares) + EPS
    solved_ref[:genes] = beta
    solved_ref[genes:] = inverse[:, :deep]

    norm_ref[...] = jnp.broadcast_to(dof / norm, norm_ref.shape)


def solve(mine, came, swapped, covs, dof):
    genes = mine.shape[0]
    outs = [
        jax.ShapeDtypeStruct((genes + covs + 8, covs + 8), jnp.float32),
        jax.ShapeDtypeStruct((genes, LANES), jnp.float32),
    ]
    return call(
        functools.partial(solve_kernel, covs, dof),
        outs,
        "solve",
        COST["solve"],
        (mine, came, *swapped),
        scalars=0,
    )


def widen_kernel(weight_ref, norm_ref, bins_ref, folds_ref, scale_ref):
    bins, folds = bins_ref[...], folds_ref[...]
    tile = jnp.zeros(bins.shape, jnp.float32)
    for b in range(weight_ref.shape[1]):
        of_bin = jnp.zeros(folds.shape, jnp.float32)
        for f in range(weight_ref.shape[0]):
            of_bin = jnp.where(folds == f, weight_ref[f, b], of_bin)
        tile = jnp.where(bins == b, of_bin, tile)
    tile = tile.T * norm_ref[:, :1]
    genes, width = tile.shape[0], scale_ref.shape[1] // tile.shape[1]
    for t in range(0, tile.shape[1], 2):
        pair = [jnp.broadcast_to(tile[:, i : i + 1], (genes, width)) for i in (t, t + 1)]
        scale_ref[:, t * width : (t + 2) * width] = jnp.concatenate(pair, axis=1)


def widen(weights, norm, bins, folds, variants):
    return call(
        widen_kernel,
        jax.ShapeDtypeStruct((norm.shape[0], variants), jnp.float32),
        "widen",
        COST["place"],
        (weights, norm, bins, folds),
    )


def fitted_stat(covs, skip, solved_ref, mine_ref, came_ref, refs):
    genes = mine_ref.shape[0]
    corr, fits = chunk_sums(genes, covs + 8, mine_ref, came_ref, refs)
    corr, fits = corr[:, skip:], fits[:, skip:]
    row = lax.broadcasted_iota(jnp.int32, fits.shape, 0)
    squares = fits[covs + 1 : covs + 2]
    fits = jnp.where(row <= covs, fits, 0.0)
    both = lax.dot_general(solved_ref[...], fits, NN, precision=HIGHEST, preferred_element_type=jnp.float32)
    norm = squares - jnp.sum(both[genes:] * fits, axis=0, keepdims=True)
    norm = jnp.maximum(norm, 1e-06 * squares) + EPS
    corr = corr - both[:genes]
    return corr * corr * (1.0 / norm)


def stat_kernel(covs, skip, solved_ref, mine_ref, came_ref, *rest):
    rest[-1][...] = fitted_stat(covs, skip, solved_ref, mine_ref, came_ref, rest[:-1])


def chunk_stat(solved, mine, came, swapped, covs, skip):
    return call(
        functools.partial(stat_kernel, covs, skip),
        jax.ShapeDtypeStruct((mine.shape[0], mine.shape[1] - skip), jnp.float32),
        "chunk_stat",
        COST["stat"],
        (solved, mine, came, *swapped),
        scalars=0,
    )


def slot_of(index, here, ring, order):
    position = {block: i for i, block in enumerate(order)}
    mine = jnp.int32(0)
    for block in range(ring):
        mine = jnp.where(here == block, position[block], mine)
    return lax.rem(position[index] - mine + ring, ring)


def place_kernel(ring, order, ids_ref, scale_ref, *rest):
    stats, (out_ref, held) = rest[:-2], rest[-2:]
    variants = held.shape[2]
    held[ring // 2] = jnp.zeros_like(held[0])
    for k, stat in enumerate(stats):
        if k == 0:
            held[0] = stat[...]
        else:
            held[ring - k] = stat[:, :variants]
            held[k] = stat[:, variants:]
    group = LANES // math.gcd(variants, LANES)
    for j in range(0, ring, group):
        pieces = [held[slot_of(j + b, ids_ref[1], ring, order)] for b in range(group)]
        span = slice(j * variants, (j + group) * variants)
        out_ref[:, span] = jnp.concatenate(pieces, axis=1) * scale_ref[:, span]


def place(ids, scale, stats, ring, order):
    genes, total = scale.shape
    return call(
        functools.partial(place_kernel, ring, order),
        jax.ShapeDtypeStruct(scale.shape, jnp.float32),
        "place",
        COST["place"],
        (ids, scale, *stats),
        scratch=[pltpu.VMEM((ring, genes, total // ring), jnp.float32)],
    )


def finish_kernel(covs, ring, order, ids_ref, solved_ref, scale_ref, placed_ref, mine_ref, came_ref, *rest):
    out_ref = rest[-1]
    variants = mine_ref.shape[1]
    group = LANES // math.gcd(variants, LANES)
    width = group * variants
    stat = fitted_stat(covs, 0, solved_ref, mine_ref, came_ref, rest[:-1])
    out_ref[...] = placed_ref[...]
    index = jnp.int32(0)
    for block in range(ring):
        index = jnp.where(slot_of(block, ids_ref[1], ring, order) == ring // 2, block, index)
    span = pl.ds(pl.multiple_of(index // group * width, LANES), width)
    stat = jnp.concatenate([stat] * group, axis=1)
    lane = lax.broadcasted_iota(jnp.int32, stat.shape, 1)
    first = lax.rem(index, group) * variants
    inside = jnp.logical_and(lane >= first, lane < first + variants)
    out_ref[:, span] = jnp.where(inside, stat * scale_ref[:, span], placed_ref[:, span])


def finish(ids, solved, scale, placed, last, covs, ring, order):
    return call(
        functools.partial(finish_kernel, covs, ring, order),
        jax.ShapeDtypeStruct(scale.shape, jnp.float32),
        "finish",
        COST["finish"],
        (ids, solved, scale, placed, *last),
    )


def shards(order, expression, genotypes, covariates, distance_bins, gene_folds, fold_weights):
    parts, ring = lax.axis_size("samp"), lax.axis_size("var")
    rows, width = expression.shape
    covs = covariates.shape[1]
    genes = width // parts
    deep = covs + 8
    dof = float(rows * parts - covs - 2)
    gt = genotypes.T
    variants = gt.shape[0]
    middle = ring // 2
    ids = jnp.stack([lax.axis_index("samp"), lax.axis_index("var")]).astype(jnp.int32)

    def exchange(x, d):
        return lax.ppermute(x, "samp", [(s, s ^ d) for s in range(parts)])

    forward = [(order[i], order[(i + 1) % ring]) for i in range(ring)]
    backward = [(b, a) for a, b in forward]

    def right(x):
        return lax.ppermute(x, "var", forward)

    def left(x):
        return lax.ppermute(x, "var", backward)

    stats = []
    lhs = solved = scale = None

    done = {}

    def starts(k):
        return [("came", 0) if k == 1 else ("got", 0) if k == 2 else ("sent", k - 1)]

    def turns(k):
        return [("got", k - 2)] if 1 < k < middle else []

    def ends(k):
        return [("got", k - 2)] if k == middle else []

    def after(*names):
        return [done[name] for name in names if name in done]

    block = (gt, gt)
    for k in range(middle + 1):
        if k > 0:
            block = gate(block, after(*turns(k)))
        if k < middle - 1:
            ahead = (right(block[0]), left(block[-1]))
        elif k == middle - 1:
            ahead = (right(block[0][: variants // 2]), left(block[-1][variants // 2 :]))
        if k == 0:
            lhs, send, other, mine = first_products(ids, expression, gt, covariates.T, parts)
        else:
            tokens = after(*starts(k))
            send, other, mine = next_products(lhs, block, parts, covs, tokens)
        came = exchange(send, 1)
        sent = add_cores(other, came, genes, deep, 1, after(*ends(k)))
        got = [[exchange(x, 2 * (i + 1)) for x in cut] for i, cut in enumerate(sent)]
        swapped = [*sent[0], *sum(got, [])]
        done["came", k], done["sent", k] = came, sent[0][0]
        done["got", k], done["rest", k] = got[-1][0], got[-1][-1]
        if k == 0:
            solved, norm = solve(mine, came, swapped, covs, dof)
            scale = widen(fold_weights, norm, distance_bins, gene_folds[None], ring * variants)
        if k < middle:
            stats.append(chunk_stat(solved, mine, came, swapped, covs, LANES if k == 0 else 0))
            block = ahead
    placed = place(ids, scale, stats, ring, tuple(order))
    return finish(ids, solved, scale, placed, (mine, came, *swapped), covs, ring, tuple(order))


def solution(mesh):
    return jax.shard_map(
        functools.partial(shards, ring_order(mesh)),
        mesh=mesh,
        in_specs=(
            P(("groups", "samp"), "var"),
            P(("groups", "samp"), "var"),
            P(("groups", "samp"), None),
            P("groups", ("var", "samp")),
            P(("groups", "var", "samp")),
            P(),
        ),
        out_specs=P(("groups", "var", "samp"), None),
        check_vma=False,
    )
```

```python
import functools
import math

import jax
import jax.numpy as jnp
from jax import lax
from jax.experimental import pallas as pl
from jax.experimental.pallas import tpu as pltpu
from jax.sharding import PartitionSpec as P

LANES = 128
EPS = 1e-06
COST = {'products': 10**8, 'add': 1, 'solve': 10**8, 'stat': 1, 'place': 1, 'finish': 1, 'gate': 10**10}
VMEM_LIMIT = 10 * 1024 * 1024

NT = (((1,), (1,)), ((), ()))
NN = (((1,), (0,)), ((), ()))
HIGHEST = lax.Precision.HIGHEST


def ring_order(mesh):
    members = list(mesh.devices[0, 0])
    places = [getattr(device, "coords", None) for device in members]
    if len(members) < 2 or any(place is None for place in places):
        return list(range(len(members)))
    axis = [i for i in range(len(places[0])) if places[0][i] != places[1][i]][0]
    columns = {}
    for index, place in enumerate(places):
        columns.setdefault(place[axis], []).append(index)
    order = []
    for step, key in enumerate(sorted(columns)):
        order += columns[key] if step % 2 == 0 else columns[key][::-1]
    return order


def call(kernel, out_shape, name, flops, operands, scratch=(), scalars=1, tokens=0):
    vmem = pl.BlockSpec(memory_space=pltpu.VMEM)
    smem = pl.BlockSpec(memory_space=pltpu.SMEM)
    rest = len(operands) - scalars - tokens
    return pl.pallas_call(
        kernel,
        out_shape=out_shape,
        in_specs=[smem] * scalars + [vmem] * rest + [pl.BlockSpec(memory_space=pl.ANY)] * tokens,
        out_specs=jax.tree.map(lambda _: vmem, out_shape),
        scratch_shapes=list(scratch),
        compiler_params=pltpu.CompilerParams(vmem_limit_bytes=VMEM_LIMIT),
        cost_estimate=pl.CostEstimate(flops=flops, bytes_accessed=0, transcendentals=0),
        name=name,
    )(*operands)


def gate_kernel(*refs):
    pass


def gate(blocks, tokens):
    vmem = pl.BlockSpec(memory_space=pltpu.VMEM)
    return pl.pallas_call(
        gate_kernel,
        out_shape=[jax.ShapeDtypeStruct(b.shape, b.dtype) for b in blocks],
        in_specs=[vmem] * len(blocks) + [pl.BlockSpec(memory_space=pl.ANY)] * len(tokens),
        out_specs=[vmem] * len(blocks),
        input_output_aliases={i: i for i in range(len(blocks))},
        compiler_params=pltpu.CompilerParams(vmem_limit_bytes=VMEM_LIMIT),
        cost_estimate=pl.CostEstimate(flops=COST["gate"], bytes_accessed=0, transcendentals=0),
        name="gate",
    )(*blocks, *tokens)


def first_kernel(parts, covs, ids_ref, e_ref, gt_ref, dt_ref, left_ref, send_ref, other_ref, mine_ref, wide):
    width = e_ref.shape[1]
    genes = width // parts
    sid = ids_ref[0]
    wide[...] = e_ref[...].T
    owners = [sid ^ 1 ^ d for d in range(2, parts, 2)] + [sid ^ 1]
    owners += [sid ^ d for d in range(2, parts, 2)] + [sid]
    for i, owner in enumerate(owners):
        start = pl.multiple_of(owner * genes, 16)
        left_ref[i * genes : (i + 1) * genes] = wide[pl.ds(start, genes), :]
    rows = dt_ref.shape[1]
    left_ref[width : width + covs] = dt_ref[...]
    first = lax.broadcasted_iota(jnp.int32, (16, rows), 0) == 0
    left_ref[width + covs :] = first.astype(jnp.float32).astype(jnp.bfloat16)
    design = left_ref[width:]
    right = jnp.concatenate([design, jnp.zeros((LANES - design.shape[0], rows), jnp.bfloat16)], axis=0)
    right = jnp.concatenate([right, gt_ref[...]], axis=0)
    split(parts, covs, genes, left_ref, right, send_ref, other_ref, mine_ref, True)


def next_kernel(parts, covs, blocks, left_ref, *rest):
    right = jnp.concatenate([ref[...] for ref in rest[:blocks]], axis=0)
    send_ref, other_ref, mine_ref = rest[-3:]
    genes = mine_ref.shape[0]
    split(parts, covs, genes, left_ref, right, send_ref, other_ref, mine_ref, False)


def split(parts, covs, genes, left_ref, right, send_ref, other_ref, mine_ref, squares):
    width = genes * parts
    span = genes * (parts // 2 - 1)
    deep = covs + 8

    prod = lax.dot_general(left_ref[...], right, NT, preferred_element_type=jnp.float32)
    outs = prod[:width]
    if squares:
        a = left_ref[:width].astype(jnp.float32)
        lane = lax.broadcasted_iota(jnp.int32, outs.shape, 1)
        outs = jnp.where(lane == covs + 1, jnp.sum(a * a, axis=1, keepdims=True), outs)
    send_ref[:span] = outs[:span]
    send_ref[span + deep :] = outs[span : span + genes]
    other_ref[:span] = outs[span + genes : 2 * span + genes]
    mine_ref[...] = outs[2 * span + genes :]
    square = right.astype(jnp.float32)
    square = square * square
    high = square.astype(jnp.bfloat16)
    low = (square - high.astype(jnp.float32)).astype(jnp.bfloat16)
    ones = jnp.ones((16, right.shape[1]), jnp.bfloat16)
    total = lax.dot_general(ones, high, NT, preferred_element_type=jnp.float32)
    total += lax.dot_general(ones, low, NT, preferred_element_type=jnp.float32)
    fits = prod[width : width + deep]
    row = lax.broadcasted_iota(jnp.int32, fits.shape, 0)
    fits = jnp.where(row == covs + 1, total[:1], fits)
    send_ref[span : span + deep] = fits
    other_ref[span:] = fits


def product_shapes(parts, covs, genes, columns):
    span = genes * (parts // 2 - 1)
    rows = (span + covs + 8 + genes, span + covs + 8, genes)
    return [jax.ShapeDtypeStruct((r, columns), jnp.float32) for r in rows]


def first_products(ids, e, gt, dt, parts):
    rows, width = e.shape
    covs = dt.shape[0]
    columns = LANES + gt.shape[0]
    left = jax.ShapeDtypeStruct((width + covs + 16, rows), jnp.bfloat16)
    return call(
        functools.partial(first_kernel, parts, covs),
        [left] + product_shapes(parts, covs, width // parts, columns),
        "first_products",
        COST["products"],
        (ids, e, gt, dt),
        scratch=[pltpu.VMEM((width, rows), jnp.bfloat16)],
    )


def next_products(left, blocks, parts, covs, tokens):
    rows = left.shape[1]
    width = left.shape[0] - covs - 16
    columns = sum(b.shape[0] for b in blocks)
    return call(
        functools.partial(next_kernel, parts, covs, len(blocks)),
        product_shapes(parts, covs, width // parts, columns),
        "next_products",
        COST["products"],
        (left, *blocks, *tokens),
        scalars=0,
        tokens=len(tokens),
    )


def packed_rows(tall, columns):
    return tall * (columns // LANES) + -(-tall // 16) * 8 if columns % LANES == LANES // 2 and columns > LANES else 0


def pack(block):
    tall, columns = block.shape
    fold = -(-tall // 16) * 8
    whole = columns // LANES
    rest = block[:, whole * LANES :]
    rest = jnp.concatenate([rest, jnp.zeros((2 * fold - tall, LANES // 2), rest.dtype)], axis=0)
    tiles = [block[:, i * LANES : (i + 1) * LANES] for i in range(whole)]
    return jnp.concatenate([*tiles, jnp.concatenate([rest[:fold], rest[fold:]], axis=1)], axis=0)


def unpack(block, tall):
    fold = -(-tall // 16) * 8
    whole = block.shape[0] // tall
    rest = block[whole * tall :]
    rest = jnp.concatenate([rest[:, : LANES // 2], rest[: tall - fold, LANES // 2 :]], axis=0)
    tiles = [block[i * tall : (i + 1) * tall] for i in range(whole)]
    return jnp.concatenate([*tiles, rest], axis=1)


def add_kernel(genes, deep, tokens, other_ref, came_ref, *rest):
    out_refs = rest[tokens:]
    cuts = len(out_refs) * genes // (other_ref.shape[0] - deep)
    span = other_ref.shape[0] - deep
    for i in range(span // genes):
        start = i * genes
        total = other_ref[start : start + genes] + came_ref[start : start + genes]
        fits = other_ref[span:] + came_ref[span : span + deep]
        total = jnp.concatenate([total, fits], axis=0)
        if out_refs[i * cuts].shape[0] > genes + deep:
            total = pack(total)
        row = 0
        for out_ref in out_refs[i * cuts : (i + 1) * cuts]:
            out_ref[...] = total[row : row + out_ref.shape[0]]
            row += out_ref.shape[0]


def add_cores(other, came, genes, deep, cuts, tokens):
    chips = (other.shape[0] - deep) // genes
    tall = genes + deep
    dense = packed_rows(tall, other.shape[1])
    if dense:
        heights, columns, cuts = [dense], LANES, 1
    else:
        heights, columns = [tall] if cuts == 1 else [tall // 16 * 8, tall - tall // 16 * 8], other.shape[1]
    shapes = [jax.ShapeDtypeStruct((h, columns), jnp.float32) for h in heights]
    out = call(
        functools.partial(add_kernel, genes, deep, len(tokens)),
        shapes * chips,
        "add_cores",
        COST["add"],
        (other, came, *tokens),
        scalars=0,
        tokens=len(tokens),
    )
    return [out[i * cuts : (i + 1) * cuts] for i in range(chips)]


def chunk_sums(genes, deep, mine_ref, came_ref, refs):
    tall = genes + deep
    blocks, rows = [], []
    for ref in refs:
        rows.append(unpack(ref[...], tall) if ref.shape[0] > tall else ref[...])
        if sum(r.shape[0] for r in rows) == tall:
            blocks.append(jnp.concatenate(rows, axis=0) if len(rows) > 1 else rows[0])
            rows = []
    corr = mine_ref[...] + came_ref[came_ref.shape[0] - genes :]
    fits = blocks[0][genes:]
    for block in blocks[1:]:
        corr = corr + block[:genes]
        fits = fits + block[genes:]
    return corr, fits


def solve_kernel(covs, dof, mine_ref, came_ref, *rest):
    refs, (solved_ref, norm_ref) = rest[:-2], rest[-2:]
    genes = mine_ref.shape[0]
    rank, deep = covs + 1, covs + 8
    corr, fits = chunk_sums(genes, deep, mine_ref, came_ref, refs)
    cross, gram = corr[:, :LANES], fits[:, :LANES]
    row = lax.broadcasted_iota(jnp.int32, gram.shape, 0)
    lane = lax.broadcasted_iota(jnp.int32, gram.shape, 1)
    inside = jnp.logical_and(row < rank, lane < rank)
    a = jnp.where(inside, gram, jnp.where(row == lane, 1.0, 0.0))
    for k in range(0, rank, 2):
        down0 = jnp.broadcast_to(a[:, k : k + 1], a.shape)
        down1 = jnp.broadcast_to(a[:, k + 1 : k + 2], a.shape)
        p00, p01, p11 = down0[k : k + 1], down1[k : k + 1], down1[k + 1 : k + 2]
        inv = 1.0 / (p00 * p11 - p01 * p01)
        q00, q01, q11 = p11 * inv, -p01 * inv, p00 * inv
        row0, row1 = a[k : k + 1], a[k + 1 : k + 2]
        first = q00 * row0 + q01 * row1
        second = q01 * row0 + q11 * row1
        swept = a - down0 * first - down1 * second
        swept = jnp.where(lane == k, down0 * q00 + down1 * q01, swept)
        swept = jnp.where(lane == k + 1, down0 * q01 + down1 * q11, swept)
        first = jnp.where(lane[:1] == k, -q00, jnp.where(lane[:1] == k + 1, -q01, first))
        second = jnp.where(lane[:1] == k, -q01, jnp.where(lane[:1] == k + 1, -q11, second))
        a = jnp.where(row == k, first, jnp.where(row == k + 1, second, swept))
    inverse = jnp.where(inside, -a, 0.0)
    lane = lax.broadcasted_iota(jnp.int32, cross.shape, 1)
    squares = jnp.sum(jnp.where(lane == rank, cross, 0.0), axis=1, keepdims=True)
    cross = jnp.where(lane < rank, cross, 0.0)
    beta = lax.dot_general(cross, inverse, NT, precision=HIGHEST, preferred_element_type=jnp.float32)
    norm = squares - jnp.sum(beta * cross[:, :deep], axis=1, keepdims=True)
    norm = jnp.maximum(norm, 1e-06 * squares) + EPS
    solved_ref[:genes] = beta
    solved_ref[genes:] = inverse[:, :deep]

    norm_ref[...] = jnp.broadcast_to(dof / norm, norm_ref.shape)


def solve(mine, came, swapped, covs, dof):
    genes = mine.shape[0]
    outs = [
        jax.ShapeDtypeStruct((genes + covs + 8, covs + 8), jnp.float32),
        jax.ShapeDtypeStruct((genes, LANES), jnp.float32),
    ]
    return call(
        functools.partial(solve_kernel, covs, dof),
        outs,
        "solve",
        COST["solve"],
        (mine, came, *swapped),
        scalars=0,
    )


def widen_kernel(weight_ref, norm_ref, bins_ref, folds_ref, scale_ref):
    bins, folds = bins_ref[...], folds_ref[...]
    tile = jnp.zeros(bins.shape, jnp.float32)
    for b in range(weight_ref.shape[1]):
        of_bin = jnp.zeros(folds.shape, jnp.float32)
        for f in range(weight_ref.shape[0]):
            of_bin = jnp.where(folds == f, weight_ref[f, b], of_bin)
        tile = jnp.where(bins == b, of_bin, tile)
    tile = tile.T * norm_ref[:, :1]
    genes, width = tile.shape[0], scale_ref.shape[1] // tile.shape[1]
    for t in range(0, tile.shape[1], 2):
        pair = [jnp.broadcast_to(tile[:, i : i + 1], (genes, width)) for i in (t, t + 1)]
        scale_ref[:, t * width : (t + 2) * width] = jnp.concatenate(pair, axis=1)


def widen(weights, norm, bins, folds, variants):
    return call(
        widen_kernel,
        jax.ShapeDtypeStruct((norm.shape[0], variants), jnp.float32),
        "widen",
        COST["place"],
        (weights, norm, bins, folds),
    )


def fitted_stat(covs, skip, solved_ref, mine_ref, came_ref, refs):
    genes = mine_ref.shape[0]
    corr, fits = chunk_sums(genes, covs + 8, mine_ref, came_ref, refs)
    corr, fits = corr[:, skip:], fits[:, skip:]
    row = lax.broadcasted_iota(jnp.int32, fits.shape, 0)
    squares = fits[covs + 1 : covs + 2]
    fits = jnp.where(row <= covs, fits, 0.0)
    both = lax.dot_general(solved_ref[...], fits, NN, precision=HIGHEST, preferred_element_type=jnp.float32)
    norm = squares - jnp.sum(both[genes:] * fits, axis=0, keepdims=True)
    norm = jnp.maximum(norm, 1e-06 * squares) + EPS
    corr = corr - both[:genes]
    return corr * corr * (1.0 / norm)


def stat_kernel(covs, skip, solved_ref, mine_ref, came_ref, *rest):
    rest[-1][...] = fitted_stat(covs, skip, solved_ref, mine_ref, came_ref, rest[:-1])


def chunk_stat(solved, mine, came, swapped, covs, skip):
    return call(
        functools.partial(stat_kernel, covs, skip),
        jax.ShapeDtypeStruct((mine.shape[0], mine.shape[1] - skip), jnp.float32),
        "chunk_stat",
        COST["stat"],
        (solved, mine, came, *swapped),
        scalars=0,
    )


def slot_of(index, here, ring, order):
    position = {block: i for i, block in enumerate(order)}
    mine = jnp.int32(0)
    for block in range(ring):
        mine = jnp.where(here == block, position[block], mine)
    return lax.rem(position[index] - mine + ring, ring)


def place_kernel(ring, order, ids_ref, scale_ref, *rest):
    stats, (out_ref, held) = rest[:-2], rest[-2:]
    variants = held.shape[2]
    held[ring // 2] = jnp.zeros_like(held[0])
    for k, stat in enumerate(stats):
        if k == 0:
            held[0] = stat[...]
        else:
            held[ring - k] = stat[:, :variants]
            held[k] = stat[:, variants:]
    group = LANES // math.gcd(variants, LANES)
    for j in range(0, ring, group):
        pieces = [held[slot_of(j + b, ids_ref[1], ring, order)] for b in range(group)]
        span = slice(j * variants, (j + group) * variants)
        out_ref[:, span] = jnp.concatenate(pieces, axis=1) * scale_ref[:, span]


def place(ids, scale, stats, ring, order):
    genes, total = scale.shape
    return call(
        functools.partial(place_kernel, ring, order),
        jax.ShapeDtypeStruct(scale.shape, jnp.float32),
        "place",
        COST["place"],
        (ids, scale, *stats),
        scratch=[pltpu.VMEM((ring, genes, total // ring), jnp.float32)],
    )


def finish_kernel(covs, ring, order, ids_ref, solved_ref, scale_ref, placed_ref, mine_ref, came_ref, *rest):
    out_ref, last, sems = rest[-3:]
    whole = pltpu.make_async_copy(placed_ref, out_ref, sems.at[0])
    whole.start()
    variants = mine_ref.shape[1]
    group = LANES // math.gcd(variants, LANES)
    width = group * variants
    stat = fitted_stat(covs, 0, solved_ref, mine_ref, came_ref, rest[:-3])
    index = jnp.int32(0)
    for block in range(ring):
        index = jnp.where(slot_of(block, ids_ref[1], ring, order) == ring // 2, block, index)
    span = pl.ds(pl.multiple_of(index // group * width, LANES), width)
    stat = jnp.concatenate([stat] * group, axis=1)
    lane = lax.broadcasted_iota(jnp.int32, stat.shape, 1)
    first = lax.rem(index, group) * variants
    inside = jnp.logical_and(lane >= first, lane < first + variants)
    last[...] = jnp.where(inside, stat * scale_ref[:, span], placed_ref[:, span])
    whole.wait()
    part = pltpu.make_async_copy(last, out_ref.at[:, span], sems.at[1])
    part.start()
    part.wait()


def finish(ids, solved, scale, placed, last, covs, ring, order):
    genes, total = scale.shape
    variants = total // ring
    width = LANES // math.gcd(variants, LANES) * variants
    vmem = pl.BlockSpec(memory_space=pltpu.VMEM)
    return pl.pallas_call(
        functools.partial(finish_kernel, covs, ring, order),
        out_shape=jax.ShapeDtypeStruct(scale.shape, jnp.float32),
        in_specs=[pl.BlockSpec(memory_space=pltpu.SMEM)] + [vmem] * (3 + len(last)),
        out_specs=pl.BlockSpec(memory_space=pl.ANY),
        scratch_shapes=[pltpu.VMEM((genes, width), jnp.float32), pltpu.SemaphoreType.DMA((2,))],
        compiler_params=pltpu.CompilerParams(vmem_limit_bytes=VMEM_LIMIT),
        cost_estimate=pl.CostEstimate(flops=COST["finish"], bytes_accessed=0, transcendentals=0),
        name="finish",
    )(ids, solved, scale, placed, *last)


def shards(order, expression, genotypes, covariates, distance_bins, gene_folds, fold_weights):
    parts, ring = lax.axis_size("samp"), lax.axis_size("var")
    rows, width = expression.shape
    covs = covariates.shape[1]
    genes = width // parts
    deep = covs + 8
    dof = float(rows * parts - covs - 2)
    gt = genotypes.T
    variants = gt.shape[0]
    middle = ring // 2
    ids = jnp.stack([lax.axis_index("samp"), lax.axis_index("var")]).astype(jnp.int32)

    def exchange(x, d):
        return lax.ppermute(x, "samp", [(s, s ^ d) for s in range(parts)])

    forward = [(order[i], order[(i + 1) % ring]) for i in range(ring)]
    backward = [(b, a) for a, b in forward]

    def right(x):
        return lax.ppermute(x, "var", forward)

    def left(x):
        return lax.ppermute(x, "var", backward)

    stats = []
    lhs = solved = scale = None

    done = {}

    def starts(k):
        return [("came", 0) if k == 1 else ("got", 0) if k == 2 else ("sent", k - 1)]

    def turns(k):
        return [("got", k - 2)] if 1 < k < middle else []

    def ends(k):
        return [("got", k - 2)] if k == middle else []

    def after(*names):
        return [done[name] for name in names if name in done]

    block = (gt, gt)
    for k in range(middle + 1):
        if k > 0:
            block = gate(block, after(*turns(k)))
        if k < middle - 1:
            ahead = (right(block[0]), left(block[-1]))
        elif k == middle - 1:
            ahead = (right(block[0][: variants // 2]), left(block[-1][variants // 2 :]))
        if k == 0:
            lhs, send, other, mine = first_products(ids, expression, gt, covariates.T, parts)
        else:
            tokens = after(*starts(k))
            send, other, mine = next_products(lhs, block, parts, covs, tokens)
        came = exchange(send, 1)
        sent = add_cores(other, came, genes, deep, 1, after(*ends(k)))
        got = [[exchange(x, 2 * (i + 1)) for x in cut] for i, cut in enumerate(sent)]
        swapped = [*sent[0], *sum(got, [])]
        done["came", k], done["sent", k] = came, sent[0][0]
        done["got", k], done["rest", k] = got[-1][0], got[-1][-1]
        if k == 0:
            solved, norm = solve(mine, came, swapped, covs, dof)
            scale = widen(fold_weights, norm, distance_bins, gene_folds[None], ring * variants)
        if k < middle:
            stats.append(chunk_stat(solved, mine, came, swapped, covs, LANES if k == 0 else 0))
            block = ahead
    placed = place(ids, scale, stats, ring, tuple(order))
    return finish(ids, solved, scale, placed, (mine, came, *swapped), covs, ring, tuple(order))


def solution(mesh):
    return jax.shard_map(
        functools.partial(shards, ring_order(mesh)),
        mesh=mesh,
        in_specs=(
            P(("groups", "samp"), "var"),
            P(("groups", "samp"), "var"),
            P(("groups", "samp"), None),
            P("groups", ("var", "samp")),
            P(("groups", "var", "samp")),
            P(),
        ),
        out_specs=P(("groups", "var", "samp"), None),
        check_vma=False,
    )
```

```python
import functools
import math

import jax
import jax.numpy as jnp
from jax import lax
from jax.experimental import pallas as pl
from jax.experimental.pallas import tpu as pltpu
from jax.sharding import PartitionSpec as P

LANES = 128
EPS = 1e-06
COST = {'products': 10**8, 'add': 1, 'solve': 10**8, 'stat': 1, 'place': 1, 'finish': 1, 'gate': 10**10}
VMEM_LIMIT = 10 * 1024 * 1024

NT = (((1,), (1,)), ((), ()))
NN = (((1,), (0,)), ((), ()))
HIGHEST = lax.Precision.HIGHEST


def ring_order(mesh):
    members = list(mesh.devices[0, 0])
    places = [getattr(device, "coords", None) for device in members]
    if len(members) < 2 or any(place is None for place in places):
        return list(range(len(members)))
    axis = [i for i in range(len(places[0])) if places[0][i] != places[1][i]][0]
    columns = {}
    for index, place in enumerate(places):
        columns.setdefault(place[axis], []).append(index)
    order = []
    for step, key in enumerate(sorted(columns)):
        order += columns[key] if step % 2 == 0 else columns[key][::-1]
    return order


def call(kernel, out_shape, name, flops, operands, scratch=(), scalars=1, tokens=0):
    vmem = pl.BlockSpec(memory_space=pltpu.VMEM)
    smem = pl.BlockSpec(memory_space=pltpu.SMEM)
    rest = len(operands) - scalars - tokens
    return pl.pallas_call(
        kernel,
        out_shape=out_shape,
        in_specs=[smem] * scalars + [vmem] * rest + [pl.BlockSpec(memory_space=pl.ANY)] * tokens,
        out_specs=jax.tree.map(lambda _: vmem, out_shape),
        scratch_shapes=list(scratch),
        compiler_params=pltpu.CompilerParams(vmem_limit_bytes=VMEM_LIMIT),
        cost_estimate=pl.CostEstimate(flops=flops, bytes_accessed=0, transcendentals=0),
        name=name,
    )(*operands)


def gate_kernel(*refs):
    pass


def gate(blocks, tokens):
    vmem = pl.BlockSpec(memory_space=pltpu.VMEM)
    return pl.pallas_call(
        gate_kernel,
        out_shape=[jax.ShapeDtypeStruct(b.shape, b.dtype) for b in blocks],
        in_specs=[vmem] * len(blocks) + [pl.BlockSpec(memory_space=pl.ANY)] * len(tokens),
        out_specs=[vmem] * len(blocks),
        input_output_aliases={i: i for i in range(len(blocks))},
        compiler_params=pltpu.CompilerParams(vmem_limit_bytes=VMEM_LIMIT),
        cost_estimate=pl.CostEstimate(flops=COST["gate"], bytes_accessed=0, transcendentals=0),
        name="gate",
    )(*blocks, *tokens)


def first_kernel(parts, covs, ids_ref, e_ref, gt_ref, dt_ref, left_ref, send_ref, other_ref, mine_ref, wide):
    width = e_ref.shape[1]
    genes = width // parts
    sid = ids_ref[0]
    wide[...] = e_ref[...].T
    owners = [sid ^ 1 ^ d for d in range(2, parts, 2)] + [sid ^ 1]
    owners += [sid ^ d for d in range(2, parts, 2)] + [sid]
    for i, owner in enumerate(owners):
        start = pl.multiple_of(owner * genes, 16)
        left_ref[i * genes : (i + 1) * genes] = wide[pl.ds(start, genes), :]
    rows = dt_ref.shape[1]
    left_ref[width : width + covs] = dt_ref[...]
    first = lax.broadcasted_iota(jnp.int32, (16, rows), 0) == 0
    left_ref[width + covs :] = first.astype(jnp.float32).astype(jnp.bfloat16)
    design = left_ref[width:]
    right = jnp.concatenate([design, jnp.zeros((LANES - design.shape[0], rows), jnp.bfloat16)], axis=0)
    right = jnp.concatenate([right, gt_ref[...]], axis=0)
    split(parts, covs, genes, left_ref, right, send_ref, other_ref, mine_ref, True)


def next_kernel(parts, covs, blocks, left_ref, *rest):
    right = jnp.concatenate([ref[...] for ref in rest[:blocks]], axis=0)
    send_ref, other_ref, mine_ref = rest[-3:]
    genes = mine_ref.shape[0]
    split(parts, covs, genes, left_ref, right, send_ref, other_ref, mine_ref, False)


def split(parts, covs, genes, left_ref, right, send_ref, other_ref, mine_ref, squares):
    width = genes * parts
    span = genes * (parts // 2 - 1)
    deep = covs + 8

    prod = lax.dot_general(left_ref[...], right, NT, preferred_element_type=jnp.float32)
    outs = prod[:width]
    if squares:
        a = left_ref[:width].astype(jnp.float32)
        lane = lax.broadcasted_iota(jnp.int32, outs.shape, 1)
        outs = jnp.where(lane == covs + 1, jnp.sum(a * a, axis=1, keepdims=True), outs)
    send_ref[:span] = outs[:span]
    send_ref[span + deep :] = outs[span : span + genes]
    other_ref[:span] = outs[span + genes : 2 * span + genes]
    mine_ref[...] = outs[2 * span + genes :]
    square = right.astype(jnp.float32)
    square = square * square
    high = square.astype(jnp.bfloat16)
    low = (square - high.astype(jnp.float32)).astype(jnp.bfloat16)
    ones = jnp.ones((16, right.shape[1]), jnp.bfloat16)
    total = lax.dot_general(ones, high, NT, preferred_element_type=jnp.float32)
    total += lax.dot_general(ones, low, NT, preferred_element_type=jnp.float32)
    fits = prod[width : width + deep]
    row = lax.broadcasted_iota(jnp.int32, fits.shape, 0)
    fits = jnp.where(row == covs + 1, total[:1], fits)
    send_ref[span : span + deep] = fits
    other_ref[span:] = fits


def product_shapes(parts, covs, genes, columns):
    span = genes * (parts // 2 - 1)
    rows = (span + covs + 8 + genes, span + covs + 8, genes)
    return [jax.ShapeDtypeStruct((r, columns), jnp.float32) for r in rows]


def first_products(ids, e, gt, dt, parts):
    rows, width = e.shape
    covs = dt.shape[0]
    columns = LANES + gt.shape[0]
    left = jax.ShapeDtypeStruct((width + covs + 16, rows), jnp.bfloat16)
    return call(
        functools.partial(first_kernel, parts, covs),
        [left] + product_shapes(parts, covs, width // parts, columns),
        "first_products",
        COST["products"],
        (ids, e, gt, dt),
        scratch=[pltpu.VMEM((width, rows), jnp.bfloat16)],
    )


def next_products(left, blocks, parts, covs, tokens):
    rows = left.shape[1]
    width = left.shape[0] - covs - 16
    columns = sum(b.shape[0] for b in blocks)
    return call(
        functools.partial(next_kernel, parts, covs, len(blocks)),
        product_shapes(parts, covs, width // parts, columns),
        "next_products",
        COST["products"],
        (left, *blocks, *tokens),
        scalars=0,
        tokens=len(tokens),
    )


def packed_rows(tall, columns):
    return tall * (columns // LANES) + -(-tall // 16) * 8 if columns % LANES == LANES // 2 and columns > LANES else 0


def pack(block):
    tall, columns = block.shape
    fold = -(-tall // 16) * 8
    whole = columns // LANES
    rest = block[:, whole * LANES :]
    rest = jnp.concatenate([rest, jnp.zeros((2 * fold - tall, LANES // 2), rest.dtype)], axis=0)
    tiles = [block[:, i * LANES : (i + 1) * LANES] for i in range(whole)]
    return jnp.concatenate([*tiles, jnp.concatenate([rest[:fold], rest[fold:]], axis=1)], axis=0)


def unpack(block, tall):
    fold = -(-tall // 16) * 8
    whole = block.shape[0] // tall
    rest = block[whole * tall :]
    rest = jnp.concatenate([rest[:, : LANES // 2], rest[: tall - fold, LANES // 2 :]], axis=0)
    tiles = [block[i * tall : (i + 1) * tall] for i in range(whole)]
    return jnp.concatenate([*tiles, rest], axis=1)


def add_kernel(genes, deep, tokens, other_ref, came_ref, *rest):
    out_refs = rest[tokens:]
    cuts = len(out_refs) * genes // (other_ref.shape[0] - deep)
    span = other_ref.shape[0] - deep
    for i in range(span // genes):
        start = i * genes
        total = other_ref[start : start + genes] + came_ref[start : start + genes]
        fits = other_ref[span:] + came_ref[span : span + deep]
        total = jnp.concatenate([total, fits], axis=0)
        if out_refs[i * cuts].shape[0] > genes + deep:
            total = pack(total)
        row = 0
        for out_ref in out_refs[i * cuts : (i + 1) * cuts]:
            out_ref[...] = total[row : row + out_ref.shape[0]]
            row += out_ref.shape[0]


def add_cores(other, came, genes, deep, cuts, tokens):
    chips = (other.shape[0] - deep) // genes
    tall = genes + deep
    dense = packed_rows(tall, other.shape[1])
    if dense:
        heights, columns, cuts = [dense], LANES, 1
    else:
        heights, columns = [tall] if cuts == 1 else [tall // 16 * 8, tall - tall // 16 * 8], other.shape[1]
    shapes = [jax.ShapeDtypeStruct((h, columns), jnp.float32) for h in heights]
    out = call(
        functools.partial(add_kernel, genes, deep, len(tokens)),
        shapes * chips,
        "add_cores",
        COST["add"],
        (other, came, *tokens),
        scalars=0,
        tokens=len(tokens),
    )
    return [out[i * cuts : (i + 1) * cuts] for i in range(chips)]


def chunk_sums(genes, deep, mine_ref, came_ref, refs):
    tall = genes + deep
    blocks, rows = [], []
    for ref in refs:
        rows.append(unpack(ref[...], tall) if ref.shape[0] > tall else ref[...])
        if sum(r.shape[0] for r in rows) == tall:
            blocks.append(jnp.concatenate(rows, axis=0) if len(rows) > 1 else rows[0])
            rows = []
    corr = mine_ref[...] + came_ref[came_ref.shape[0] - genes :]
    fits = blocks[0][genes:]
    for block in blocks[1:]:
        corr = corr + block[:genes]
        fits = fits + block[genes:]
    return corr, fits


def solve_kernel(covs, dof, mine_ref, came_ref, *rest):
    refs, (solved_ref, norm_ref) = rest[:-2], rest[-2:]
    genes = mine_ref.shape[0]
    rank, deep = covs + 1, covs + 8
    corr, fits = chunk_sums(genes, deep, mine_ref, came_ref, refs)
    cross, gram = corr[:, :LANES], fits[:, :LANES]
    row = lax.broadcasted_iota(jnp.int32, gram.shape, 0)
    lane = lax.broadcasted_iota(jnp.int32, gram.shape, 1)
    inside = jnp.logical_and(row < rank, lane < rank)
    a = jnp.where(inside, gram, jnp.where(row == lane, 1.0, 0.0))
    for k in range(0, rank, 2):
        down0 = jnp.broadcast_to(a[:, k : k + 1], a.shape)
        down1 = jnp.broadcast_to(a[:, k + 1 : k + 2], a.shape)
        p00, p01, p11 = down0[k : k + 1], down1[k : k + 1], down1[k + 1 : k + 2]
        inv = 1.0 / (p00 * p11 - p01 * p01)
        q00, q01, q11 = p11 * inv, -p01 * inv, p00 * inv
        row0, row1 = a[k : k + 1], a[k + 1 : k + 2]
        first = q00 * row0 + q01 * row1
        second = q01 * row0 + q11 * row1
        swept = a - down0 * first - down1 * second
        swept = jnp.where(lane == k, down0 * q00 + down1 * q01, swept)
        swept = jnp.where(lane == k + 1, down0 * q01 + down1 * q11, swept)
        first = jnp.where(lane[:1] == k, -q00, jnp.where(lane[:1] == k + 1, -q01, first))
        second = jnp.where(lane[:1] == k, -q01, jnp.where(lane[:1] == k + 1, -q11, second))
        a = jnp.where(row == k, first, jnp.where(row == k + 1, second, swept))
    inverse = jnp.where(inside, -a, 0.0)
    lane = lax.broadcasted_iota(jnp.int32, cross.shape, 1)
    squares = jnp.sum(jnp.where(lane == rank, cross, 0.0), axis=1, keepdims=True)
    cross = jnp.where(lane < rank, cross, 0.0)
    beta = lax.dot_general(cross, inverse, NT, precision=HIGHEST, preferred_element_type=jnp.float32)
    norm = squares - jnp.sum(beta * cross[:, :deep], axis=1, keepdims=True)
    norm = jnp.maximum(norm, 1e-06 * squares) + EPS
    solved_ref[:genes] = beta
    solved_ref[genes:] = inverse[:, :deep]

    norm_ref[...] = jnp.broadcast_to(dof / norm, norm_ref.shape)


def solve(mine, came, swapped, covs, dof):
    genes = mine.shape[0]
    outs = [
        jax.ShapeDtypeStruct((genes + covs + 8, covs + 8), jnp.float32),
        jax.ShapeDtypeStruct((genes, LANES), jnp.float32),
    ]
    return call(
        functools.partial(solve_kernel, covs, dof),
        outs,
        "solve",
        COST["solve"],
        (mine, came, *swapped),
        scalars=0,
    )


def widen_kernel(weight_ref, norm_ref, bins_ref, folds_ref, scale_ref):
    bins, folds = bins_ref[...], folds_ref[...]
    tile = jnp.zeros(bins.shape, jnp.float32)
    for b in range(weight_ref.shape[1]):
        of_bin = jnp.zeros(folds.shape, jnp.float32)
        for f in range(weight_ref.shape[0]):
            of_bin = jnp.where(folds == f, weight_ref[f, b], of_bin)
        tile = jnp.where(bins == b, of_bin, tile)
    tile = tile.T * norm_ref[:, :1]
    genes, width = tile.shape[0], scale_ref.shape[1] // tile.shape[1]
    for t in range(0, tile.shape[1], 2):
        pair = [jnp.broadcast_to(tile[:, i : i + 1], (genes, width)) for i in (t, t + 1)]
        scale_ref[:, t * width : (t + 2) * width] = jnp.concatenate(pair, axis=1)


def widen(weights, norm, bins, folds, variants):
    return call(
        widen_kernel,
        jax.ShapeDtypeStruct((norm.shape[0], variants), jnp.float32),
        "widen",
        COST["place"],
        (weights, norm, bins, folds),
    )


def fitted_stat(covs, skip, solved_ref, mine_ref, came_ref, refs):
    genes = mine_ref.shape[0]
    corr, fits = chunk_sums(genes, covs + 8, mine_ref, came_ref, refs)
    corr, fits = corr[:, skip:], fits[:, skip:]
    row = lax.broadcasted_iota(jnp.int32, fits.shape, 0)
    squares = fits[covs + 1 : covs + 2]
    fits = jnp.where(row <= covs, fits, 0.0)
    both = lax.dot_general(solved_ref[...], fits, NN, precision=HIGHEST, preferred_element_type=jnp.float32)
    norm = squares - jnp.sum(both[genes:] * fits, axis=0, keepdims=True)
    norm = jnp.maximum(norm, 1e-06 * squares) + EPS
    corr = corr - both[:genes]
    return corr * corr * (1.0 / norm)


def stat_kernel(covs, skip, solved_ref, mine_ref, came_ref, *rest):
    rest[-1][...] = fitted_stat(covs, skip, solved_ref, mine_ref, came_ref, rest[:-1])


def chunk_stat(solved, mine, came, swapped, covs, skip):
    return call(
        functools.partial(stat_kernel, covs, skip),
        jax.ShapeDtypeStruct((mine.shape[0], mine.shape[1] - skip), jnp.float32),
        "chunk_stat",
        COST["stat"],
        (solved, mine, came, *swapped),
        scalars=0,
    )


def lookup(key, table):
    value = jnp.int32(table[0])
    for i in range(1, len(table)):
        value = jnp.where(key == i, jnp.int32(table[i]), value)
    return value


def wrap(step, ring):
    step = jnp.where(step < 0, step + ring, step)
    return jnp.where(step >= ring, step - ring, step)


def place_kernel(ring, order, ids_ref, scale_ref, *rest):
    stats, (out_ref, held) = rest[:-2], rest[-2:]
    variants = held.shape[2]
    held[ring // 2] = jnp.zeros_like(held[0])
    for k, stat in enumerate(stats):
        if k == 0:
            held[0] = stat[...]
        else:
            held[ring - k] = stat[:, :variants]
            held[k] = stat[:, variants:]
    group = LANES // math.gcd(variants, LANES)
    position = [order.index(block) for block in range(ring)]
    mine = lookup(ids_ref[1], position)
    for j in range(0, ring, group):
        pieces = [held[wrap(position[j + b] - mine, ring)] for b in range(group)]
        span = slice(j * variants, (j + group) * variants)
        out_ref[:, span] = jnp.concatenate(pieces, axis=1) * scale_ref[:, span]


def place(ids, scale, stats, ring, order):
    genes, total = scale.shape
    return call(
        functools.partial(place_kernel, ring, order),
        jax.ShapeDtypeStruct(scale.shape, jnp.float32),
        "place",
        COST["place"],
        (ids, scale, *stats),
        scratch=[pltpu.VMEM((ring, genes, total // ring), jnp.float32)],
    )


def finish_kernel(covs, ring, order, ids_ref, solved_ref, scale_ref, placed_ref, mine_ref, came_ref, *rest):
    out_ref = rest[-1]
    variants = mine_ref.shape[1]
    group = LANES // math.gcd(variants, LANES)
    width = group * variants
    stat = fitted_stat(covs, 0, solved_ref, mine_ref, came_ref, rest[:-1])
    out_ref[...] = placed_ref[...]
    across = [order[(order.index(block) + ring // 2) % ring] for block in range(ring)]
    start = lookup(ids_ref[1], [block // group * width for block in across])
    first = lookup(ids_ref[1], [block % group * variants for block in across])
    span = pl.ds(pl.multiple_of(start, LANES), width)
    stat = jnp.concatenate([stat] * group, axis=1)
    lane = lax.broadcasted_iota(jnp.int32, stat.shape, 1)
    inside = jnp.logical_and(lane >= first, lane < first + variants)
    out_ref[:, span] = jnp.where(inside, stat * scale_ref[:, span], placed_ref[:, span])


def finish(ids, solved, scale, placed, last, covs, ring, order):
    return call(
        functools.partial(finish_kernel, covs, ring, order),
        jax.ShapeDtypeStruct(scale.shape, jnp.float32),
        "finish",
        COST["finish"],
        (ids, solved, scale, placed, *last),
    )


def shards(order, expression, genotypes, covariates, distance_bins, gene_folds, fold_weights):
    parts, ring = lax.axis_size("samp"), lax.axis_size("var")
    rows, width = expression.shape
    covs = covariates.shape[1]
    genes = width // parts
    deep = covs + 8
    dof = float(rows * parts - covs - 2)
    gt = genotypes.T
    variants = gt.shape[0]
    middle = ring // 2
    ids = jnp.stack([lax.axis_index("samp"), lax.axis_index("var")]).astype(jnp.int32)

    def exchange(x, d):
        return lax.ppermute(x, "samp", [(s, s ^ d) for s in range(parts)])

    forward = [(order[i], order[(i + 1) % ring]) for i in range(ring)]
    backward = [(b, a) for a, b in forward]

    def right(x):
        return lax.ppermute(x, "var", forward)

    def left(x):
        return lax.ppermute(x, "var", backward)

    stats = []
    lhs = solved = scale = None

    done = {}

    def starts(k):
        return [("came", 0) if k == 1 else ("got", 0) if k == 2 else ("sent", k - 1)]

    def turns(k):
        return [("got", k - 2)] if 1 < k < middle else []

    def ends(k):
        return [("got", k - 2)] if k == middle else []

    def after(*names):
        return [done[name] for name in names if name in done]

    block = (gt, gt)
    for k in range(middle + 1):
        if k > 0:
            block = gate(block, after(*turns(k)))
        if k < middle - 1:
            ahead = (right(block[0]), left(block[-1]))
        elif k == middle - 1:
            ahead = (right(block[0][: variants // 2]), left(block[-1][variants // 2 :]))
        if k == 0:
            lhs, send, other, mine = first_products(ids, expression, gt, covariates.T, parts)
        else:
            tokens = after(*starts(k))
            send, other, mine = next_products(lhs, block, parts, covs, tokens)
        came = exchange(send, 1)
        sent = add_cores(other, came, genes, deep, 1, after(*ends(k)))
        got = [[exchange(x, 2 * (i + 1)) for x in cut] for i, cut in enumerate(sent)]
        swapped = [*sent[0], *sum(got, [])]
        done["came", k], done["sent", k] = came, sent[0][0]
        done["got", k], done["rest", k] = got[-1][0], got[-1][-1]
        if k == 0:
            solved, norm = solve(mine, came, swapped, covs, dof)
            scale = widen(fold_weights, norm, distance_bins, gene_folds[None], ring * variants)
        if k < middle:
            stats.append(chunk_stat(solved, mine, came, swapped, covs, LANES if k == 0 else 0))
            block = ahead
    placed = place(ids, scale, stats, ring, tuple(order))
    return finish(ids, solved, scale, placed, (mine, came, *swapped), covs, ring, tuple(order))


def solution(mesh):
    return jax.shard_map(
        functools.partial(shards, ring_order(mesh)),
        mesh=mesh,
        in_specs=(
            P(("groups", "samp"), "var"),
            P(("groups", "samp"), "var"),
            P(("groups", "samp"), None),
            P("groups", ("var", "samp")),
            P(("groups", "var", "samp")),
            P(),
        ),
        out_specs=P(("groups", "var", "samp"), None),
        check_vma=False,
    )
```

```python
import functools
import math

import jax
import jax.numpy as jnp
from jax import lax
from jax.experimental import pallas as pl
from jax.experimental.pallas import tpu as pltpu
from jax.sharding import PartitionSpec as P

LANES = 128
EPS = 1e-06
COST = {'products': 10**8, 'add': 1, 'solve': 10**8, 'stat': 1, 'place': 1, 'finish': 1, 'gate': 10**10}
VMEM_LIMIT = 10 * 1024 * 1024

NT = (((1,), (1,)), ((), ()))
NN = (((1,), (0,)), ((), ()))
HIGHEST = lax.Precision.HIGHEST


def ring_order(mesh):
    members = list(mesh.devices[0, 0])
    places = [getattr(device, "coords", None) for device in members]
    if len(members) < 2 or any(place is None for place in places):
        return list(range(len(members)))
    axis = [i for i in range(len(places[0])) if places[0][i] != places[1][i]][0]
    columns = {}
    for index, place in enumerate(places):
        columns.setdefault(place[axis], []).append(index)
    order = []
    for step, key in enumerate(sorted(columns)):
        order += columns[key] if step % 2 == 0 else columns[key][::-1]
    return order


def call(kernel, out_shape, name, flops, operands, scratch=(), scalars=1, tokens=0):
    vmem = pl.BlockSpec(memory_space=pltpu.VMEM)
    smem = pl.BlockSpec(memory_space=pltpu.SMEM)
    rest = len(operands) - scalars - tokens
    return pl.pallas_call(
        kernel,
        out_shape=out_shape,
        in_specs=[smem] * scalars + [vmem] * rest + [pl.BlockSpec(memory_space=pl.ANY)] * tokens,
        out_specs=jax.tree.map(lambda _: vmem, out_shape),
        scratch_shapes=list(scratch),
        compiler_params=pltpu.CompilerParams(vmem_limit_bytes=VMEM_LIMIT),
        cost_estimate=pl.CostEstimate(flops=flops, bytes_accessed=0, transcendentals=0),
        name=name,
    )(*operands)


def gate_kernel(*refs):
    pass


def gate(blocks, tokens):
    vmem = pl.BlockSpec(memory_space=pltpu.VMEM)
    return pl.pallas_call(
        gate_kernel,
        out_shape=[jax.ShapeDtypeStruct(b.shape, b.dtype) for b in blocks],
        in_specs=[vmem] * len(blocks) + [pl.BlockSpec(memory_space=pl.ANY)] * len(tokens),
        out_specs=[vmem] * len(blocks),
        input_output_aliases={i: i for i in range(len(blocks))},
        compiler_params=pltpu.CompilerParams(vmem_limit_bytes=VMEM_LIMIT),
        cost_estimate=pl.CostEstimate(flops=COST["gate"], bytes_accessed=0, transcendentals=0),
        name="gate",
    )(*blocks, *tokens)


def first_kernel(parts, covs, ids_ref, e_ref, gt_ref, dt_ref, left_ref, send_ref, other_ref, mine_ref, wide):
    width = e_ref.shape[1]
    genes = width // parts
    sid = ids_ref[0]
    wide[...] = e_ref[...].T
    owners = [sid ^ 1 ^ d for d in range(2, parts, 2)] + [sid ^ 1]
    owners += [sid ^ d for d in range(2, parts, 2)] + [sid]
    for i, owner in enumerate(owners):
        start = pl.multiple_of(owner * genes, 16)
        left_ref[i * genes : (i + 1) * genes] = wide[pl.ds(start, genes), :]
    rows = dt_ref.shape[1]
    left_ref[width : width + covs] = dt_ref[...]
    first = lax.broadcasted_iota(jnp.int32, (16, rows), 0) == 0
    left_ref[width + covs :] = first.astype(jnp.float32).astype(jnp.bfloat16)
    design = left_ref[width:]
    right = jnp.concatenate([design, jnp.zeros((LANES - design.shape[0], rows), jnp.bfloat16)], axis=0)
    right = jnp.concatenate([right, gt_ref[...]], axis=0)
    split(parts, covs, genes, left_ref, right, send_ref, other_ref, mine_ref, True)


def next_kernel(parts, covs, blocks, left_ref, *rest):
    right = jnp.concatenate([ref[...] for ref in rest[:blocks]], axis=0)
    send_ref, other_ref, mine_ref = rest[-3:]
    genes = mine_ref.shape[0]
    split(parts, covs, genes, left_ref, right, send_ref, other_ref, mine_ref, False)


def split(parts, covs, genes, left_ref, right, send_ref, other_ref, mine_ref, squares):
    width = genes * parts
    span = genes * (parts // 2 - 1)
    deep = covs + 8

    prod = lax.dot_general(left_ref[...], right, NT, preferred_element_type=jnp.float32)
    outs = prod[:width]
    if squares:
        a = left_ref[:width].astype(jnp.float32)
        lane = lax.broadcasted_iota(jnp.int32, outs.shape, 1)
        outs = jnp.where(lane == covs + 1, jnp.sum(a * a, axis=1, keepdims=True), outs)
    send_ref[:span] = outs[:span]
    send_ref[span + deep :] = outs[span : span + genes]
    other_ref[:span] = outs[span + genes : 2 * span + genes]
    mine_ref[...] = outs[2 * span + genes :]
    square = right.astype(jnp.float32)
    square = square * square
    high = square.astype(jnp.bfloat16)
    low = (square - high.astype(jnp.float32)).astype(jnp.bfloat16)
    ones = jnp.ones((16, right.shape[1]), jnp.bfloat16)
    total = lax.dot_general(ones, high, NT, preferred_element_type=jnp.float32)
    total += lax.dot_general(ones, low, NT, preferred_element_type=jnp.float32)
    fits = prod[width : width + deep]
    row = lax.broadcasted_iota(jnp.int32, fits.shape, 0)
    fits = jnp.where(row == covs + 1, total[:1], fits)
    send_ref[span : span + deep] = fits
    other_ref[span:] = fits


def product_shapes(parts, covs, genes, columns):
    span = genes * (parts // 2 - 1)
    rows = (span + covs + 8 + genes, span + covs + 8, genes)
    return [jax.ShapeDtypeStruct((r, columns), jnp.float32) for r in rows]


def first_products(ids, e, gt, dt, parts):
    rows, width = e.shape
    covs = dt.shape[0]
    columns = LANES + gt.shape[0]
    left = jax.ShapeDtypeStruct((width + covs + 16, rows), jnp.bfloat16)
    return call(
        functools.partial(first_kernel, parts, covs),
        [left] + product_shapes(parts, covs, width // parts, columns),
        "first_products",
        COST["products"],
        (ids, e, gt, dt),
        scratch=[pltpu.VMEM((width, rows), jnp.bfloat16)],
    )


def next_products(left, blocks, parts, covs, tokens):
    rows = left.shape[1]
    width = left.shape[0] - covs - 16
    columns = sum(b.shape[0] for b in blocks)
    return call(
        functools.partial(next_kernel, parts, covs, len(blocks)),
        product_shapes(parts, covs, width // parts, columns),
        "next_products",
        COST["products"],
        (left, *blocks, *tokens),
        scalars=0,
        tokens=len(tokens),
    )


def packed_rows(tall, columns):
    return tall * (columns // LANES) + -(-tall // 16) * 8 if columns % LANES == LANES // 2 and columns > LANES else 0


def pack(block):
    tall, columns = block.shape
    fold = -(-tall // 16) * 8
    whole = columns // LANES
    rest = block[:, whole * LANES :]
    rest = jnp.concatenate([rest, jnp.zeros((2 * fold - tall, LANES // 2), rest.dtype)], axis=0)
    tiles = [block[:, i * LANES : (i + 1) * LANES] for i in range(whole)]
    return jnp.concatenate([*tiles, jnp.concatenate([rest[:fold], rest[fold:]], axis=1)], axis=0)


def unpack(block, tall):
    fold = -(-tall // 16) * 8
    whole = block.shape[0] // tall
    rest = block[whole * tall :]
    rest = jnp.concatenate([rest[:, : LANES // 2], rest[: tall - fold, LANES // 2 :]], axis=0)
    tiles = [block[i * tall : (i + 1) * tall] for i in range(whole)]
    return jnp.concatenate([*tiles, rest], axis=1)


def add_kernel(genes, deep, tokens, other_ref, came_ref, *rest):
    out_refs = rest[tokens:]
    cuts = len(out_refs) * genes // (other_ref.shape[0] - deep)
    span = other_ref.shape[0] - deep
    for i in range(span // genes):
        start = i * genes
        total = other_ref[start : start + genes] + came_ref[start : start + genes]
        fits = other_ref[span:] + came_ref[span : span + deep]
        total = jnp.concatenate([total, fits], axis=0)
        if out_refs[i * cuts].shape[0] > genes + deep:
            total = pack(total)
        row = 0
        for out_ref in out_refs[i * cuts : (i + 1) * cuts]:
            out_ref[...] = total[row : row + out_ref.shape[0]]
            row += out_ref.shape[0]


def add_cores(other, came, genes, deep, cuts, tokens):
    chips = (other.shape[0] - deep) // genes
    tall = genes + deep
    dense = packed_rows(tall, other.shape[1])
    if dense:
        heights, columns, cuts = [dense], LANES, 1
    else:
        heights, columns = [tall] if cuts == 1 else [tall // 16 * 8, tall - tall // 16 * 8], other.shape[1]
    shapes = [jax.ShapeDtypeStruct((h, columns), jnp.float32) for h in heights]
    out = call(
        functools.partial(add_kernel, genes, deep, len(tokens)),
        shapes * chips,
        "add_cores",
        COST["add"],
        (other, came, *tokens),
        scalars=0,
        tokens=len(tokens),
    )
    return [out[i * cuts : (i + 1) * cuts] for i in range(chips)]


def chunk_sums(genes, deep, mine_ref, came_ref, refs):
    tall = genes + deep
    blocks, rows = [], []
    for ref in refs:
        rows.append(unpack(ref[...], tall) if ref.shape[0] > tall else ref[...])
        if sum(r.shape[0] for r in rows) == tall:
            blocks.append(jnp.concatenate(rows, axis=0) if len(rows) > 1 else rows[0])
            rows = []
    corr = mine_ref[...] + came_ref[came_ref.shape[0] - genes :]
    fits = blocks[0][genes:]
    for block in blocks[1:]:
        corr = corr + block[:genes]
        fits = fits + block[genes:]
    return corr, fits


def solve_kernel(covs, dof, mine_ref, came_ref, *rest):
    refs, (solved_ref, norm_ref) = rest[:-2], rest[-2:]
    genes = mine_ref.shape[0]
    rank, deep = covs + 1, covs + 8
    corr, fits = chunk_sums(genes, deep, mine_ref, came_ref, refs)
    cross, gram = corr[:, :LANES], fits[:, :LANES]
    row = lax.broadcasted_iota(jnp.int32, gram.shape, 0)
    lane = lax.broadcasted_iota(jnp.int32, gram.shape, 1)
    inside = jnp.logical_and(row < rank, lane < rank)
    a = jnp.where(inside, gram, jnp.where(row == lane, 1.0, 0.0))
    for k in range(0, rank, 2):
        down0 = jnp.broadcast_to(a[:, k : k + 1], a.shape)
        down1 = jnp.broadcast_to(a[:, k + 1 : k + 2], a.shape)
        p00, p01, p11 = down0[k : k + 1], down1[k : k + 1], down1[k + 1 : k + 2]
        inv = 1.0 / (p00 * p11 - p01 * p01)
        q00, q01, q11 = p11 * inv, -p01 * inv, p00 * inv
        row0, row1 = a[k : k + 1], a[k + 1 : k + 2]
        first = q00 * row0 + q01 * row1
        second = q01 * row0 + q11 * row1
        swept = a - down0 * first - down1 * second
        swept = jnp.where(lane == k, down0 * q00 + down1 * q01, swept)
        swept = jnp.where(lane == k + 1, down0 * q01 + down1 * q11, swept)
        first = jnp.where(lane[:1] == k, -q00, jnp.where(lane[:1] == k + 1, -q01, first))
        second = jnp.where(lane[:1] == k, -q01, jnp.where(lane[:1] == k + 1, -q11, second))
        a = jnp.where(row == k, first, jnp.where(row == k + 1, second, swept))
    inverse = jnp.where(inside, -a, 0.0)
    lane = lax.broadcasted_iota(jnp.int32, cross.shape, 1)
    squares = jnp.sum(jnp.where(lane == rank, cross, 0.0), axis=1, keepdims=True)
    cross = jnp.where(lane < rank, cross, 0.0)
    beta = lax.dot_general(cross, inverse, NT, precision=HIGHEST, preferred_element_type=jnp.float32)
    norm = squares - jnp.sum(beta * cross[:, :deep], axis=1, keepdims=True)
    norm = jnp.maximum(norm, 1e-06 * squares) + EPS
    solved_ref[:genes] = beta
    solved_ref[genes:] = inverse[:, :deep]

    norm_ref[...] = jnp.broadcast_to(dof / norm, norm_ref.shape)


def solve(mine, came, swapped, covs, dof):
    genes = mine.shape[0]
    outs = [
        jax.ShapeDtypeStruct((genes + covs + 8, covs + 8), jnp.float32),
        jax.ShapeDtypeStruct((genes, LANES), jnp.float32),
    ]
    return call(
        functools.partial(solve_kernel, covs, dof),
        outs,
        "solve",
        COST["solve"],
        (mine, came, *swapped),
        scalars=0,
    )


def widen_kernel(weight_ref, norm_ref, bins_ref, folds_ref, scale_ref):
    bins, folds = bins_ref[...], folds_ref[...]
    tile = jnp.zeros(bins.shape, jnp.float32)
    for b in range(weight_ref.shape[1]):
        of_bin = jnp.zeros(folds.shape, jnp.float32)
        for f in range(weight_ref.shape[0]):
            of_bin = jnp.where(folds == f, weight_ref[f, b], of_bin)
        tile = jnp.where(bins == b, of_bin, tile)
    tile = tile.T * norm_ref[:, :1]
    genes, width = tile.shape[0], scale_ref.shape[1] // tile.shape[1]
    for t in range(0, tile.shape[1], 2):
        pair = [jnp.broadcast_to(tile[:, i : i + 1], (genes, width)) for i in (t, t + 1)]
        scale_ref[:, t * width : (t + 2) * width] = jnp.concatenate(pair, axis=1)


def widen(weights, norm, bins, folds, variants):
    return call(
        widen_kernel,
        jax.ShapeDtypeStruct((norm.shape[0], variants), jnp.float32),
        "widen",
        COST["place"],
        (weights, norm, bins, folds),
    )


def fitted_stat(covs, skip, solved_ref, mine_ref, came_ref, refs):
    genes = mine_ref.shape[0]
    corr, fits = chunk_sums(genes, covs + 8, mine_ref, came_ref, refs)
    corr, fits = corr[:, skip:], fits[:, skip:]
    row = lax.broadcasted_iota(jnp.int32, fits.shape, 0)
    squares = fits[covs + 1 : covs + 2]
    fits = jnp.where(row <= covs, fits, 0.0)
    both = lax.dot_general(solved_ref[...], fits, NN, precision=HIGHEST, preferred_element_type=jnp.float32)
    norm = squares - jnp.sum(both[genes:] * fits, axis=0, keepdims=True)
    norm = jnp.maximum(norm, 1e-06 * squares) + EPS
    corr = corr - both[:genes]
    return corr * corr * (1.0 / norm)


def stat_kernel(covs, skip, solved_ref, mine_ref, came_ref, *rest):
    rest[-1][...] = fitted_stat(covs, skip, solved_ref, mine_ref, came_ref, rest[:-1])


def chunk_stat(solved, mine, came, swapped, covs, skip):
    return call(
        functools.partial(stat_kernel, covs, skip),
        jax.ShapeDtypeStruct((mine.shape[0], mine.shape[1] - skip), jnp.float32),
        "chunk_stat",
        COST["stat"],
        (solved, mine, came, *swapped),
        scalars=0,
    )


def lookup(key, table):
    value = jnp.int32(table[0])
    for i in range(1, len(table)):
        value = jnp.where(key == i, jnp.int32(table[i]), value)
    return value


def wrap(step, ring):
    step = jnp.where(step < 0, step + ring, step)
    return jnp.where(step >= ring, step - ring, step)


def place_kernel(ring, order, ids_ref, scale_ref, *rest):
    stats, (out_ref, held) = rest[:-2], rest[-2:]
    variants = held.shape[2]
    held[ring // 2] = jnp.zeros_like(held[0])
    for k, stat in enumerate(stats):
        if k == 0:
            held[0] = stat[...]
        else:
            held[ring - k] = stat[:, :variants]
            held[k] = stat[:, variants:]
    group = LANES // math.gcd(variants, LANES)
    position = [order.index(block) for block in range(ring)]
    mine = lookup(ids_ref[1], position)
    for j in range(0, ring, group):
        pieces = [held[wrap(position[j + b] - mine, ring)] for b in range(group)]
        span = slice(j * variants, (j + group) * variants)
        out_ref[:, span] = jnp.concatenate(pieces, axis=1) * scale_ref[:, span]


def place(ids, scale, stats, ring, order):
    genes, total = scale.shape
    return call(
        functools.partial(place_kernel, ring, order),
        jax.ShapeDtypeStruct(scale.shape, jnp.float32),
        "place",
        COST["place"],
        (ids, scale, *stats),
        scratch=[pltpu.VMEM((ring, genes, total // ring), jnp.float32)],
    )


def finish_kernel(covs, ring, order, ids_ref, solved_ref, scale_ref, placed_ref, mine_ref, came_ref, *rest):
    out_ref, last, sems = rest[-3:]
    variants = mine_ref.shape[1]
    group = LANES // math.gcd(variants, LANES)
    width = group * variants
    across = [order[(order.index(block) + ring // 2) % ring] for block in range(ring)]
    start = lookup(ids_ref[1], [block // group * width for block in across])
    first = lookup(ids_ref[1], [block % group * variants for block in across])
    span = pl.ds(pl.multiple_of(start, LANES), width)
    there = pltpu.make_async_copy(placed_ref.at[:, span], last, sems.at[0])
    there.start()
    stat = fitted_stat(covs, 0, solved_ref, mine_ref, came_ref, rest[:-3])
    stat = jnp.concatenate([stat] * group, axis=1)
    lane = lax.broadcasted_iota(jnp.int32, stat.shape, 1)
    inside = jnp.logical_and(lane >= first, lane < first + variants)
    there.wait()
    last[...] = jnp.where(inside, stat * scale_ref[:, span], last[...])
    back = pltpu.make_async_copy(last, out_ref.at[:, span], sems.at[1])
    back.start()
    back.wait()


def finish(ids, solved, scale, placed, last, covs, ring, order):
    genes, total = scale.shape
    variants = total // ring
    width = LANES // math.gcd(variants, LANES) * variants
    vmem, anywhere = pl.BlockSpec(memory_space=pltpu.VMEM), pl.BlockSpec(memory_space=pl.ANY)
    return pl.pallas_call(
        functools.partial(finish_kernel, covs, ring, order),
        out_shape=jax.ShapeDtypeStruct(scale.shape, jnp.float32),
        in_specs=[pl.BlockSpec(memory_space=pltpu.SMEM), vmem, vmem, anywhere] + [vmem] * len(last),
        out_specs=anywhere,
        input_output_aliases={3: 0},
        scratch_shapes=[pltpu.VMEM((genes, width), jnp.float32), pltpu.SemaphoreType.DMA((2,))],
        compiler_params=pltpu.CompilerParams(vmem_limit_bytes=VMEM_LIMIT),
        cost_estimate=pl.CostEstimate(flops=COST["finish"], bytes_accessed=0, transcendentals=0),
        name="finish",
    )(ids, solved, scale, placed, *last)


def shards(order, expression, genotypes, covariates, distance_bins, gene_folds, fold_weights):
    parts, ring = lax.axis_size("samp"), lax.axis_size("var")
    rows, width = expression.shape
    covs = covariates.shape[1]
    genes = width // parts
    deep = covs + 8
    dof = float(rows * parts - covs - 2)
    gt = genotypes.T
    variants = gt.shape[0]
    middle = ring // 2
    ids = jnp.stack([lax.axis_index("samp"), lax.axis_index("var")]).astype(jnp.int32)

    def exchange(x, d):
        return lax.ppermute(x, "samp", [(s, s ^ d) for s in range(parts)])

    forward = [(order[i], order[(i + 1) % ring]) for i in range(ring)]
    backward = [(b, a) for a, b in forward]

    def right(x):
        return lax.ppermute(x, "var", forward)

    def left(x):
        return lax.ppermute(x, "var", backward)

    stats = []
    lhs = solved = scale = None

    done = {}

    def starts(k):
        return [("came", 0) if k == 1 else ("got", 0) if k == 2 else ("sent", k - 1)]

    def turns(k):
        return [("got", k - 2)] if 1 < k < middle else []

    def ends(k):
        return [("got", k - 2)] if k == middle else []

    def after(*names):
        return [done[name] for name in names if name in done]

    block = (gt, gt)
    for k in range(middle + 1):
        if k > 0:
            block = gate(block, after(*turns(k)))
        if k < middle - 1:
            ahead = (right(block[0]), left(block[-1]))
        elif k == middle - 1:
            ahead = (right(block[0][: variants // 2]), left(block[-1][variants // 2 :]))
        if k == 0:
            lhs, send, other, mine = first_products(ids, expression, gt, covariates.T, parts)
        else:
            tokens = after(*starts(k))
            send, other, mine = next_products(lhs, block, parts, covs, tokens)
        came = exchange(send, 1)
        sent = add_cores(other, came, genes, deep, 1, after(*ends(k)))
        got = [[exchange(x, 2 * (i + 1)) for x in cut] for i, cut in enumerate(sent)]
        swapped = [*sent[0], *sum(got, [])]
        done["came", k], done["sent", k] = came, sent[0][0]
        done["got", k], done["rest", k] = got[-1][0], got[-1][-1]
        if k == 0:
            solved, norm = solve(mine, came, swapped, covs, dof)
            scale = widen(fold_weights, norm, distance_bins, gene_folds[None], ring * variants)
        if k < middle:
            stats.append(chunk_stat(solved, mine, came, swapped, covs, LANES if k == 0 else 0))
            block = ahead
    placed = place(ids, scale, stats, ring, tuple(order))
    return finish(ids, solved, scale, placed, (mine, came, *swapped), covs, ring, tuple(order))


def solution(mesh):
    return jax.shard_map(
        functools.partial(shards, ring_order(mesh)),
        mesh=mesh,
        in_specs=(
            P(("groups", "samp"), "var"),
            P(("groups", "samp"), "var"),
            P(("groups", "samp"), None),
            P("groups", ("var", "samp")),
            P(("groups", "var", "samp")),
            P(),
        ),
        out_specs=P(("groups", "var", "samp"), None),
        check_vma=False,
    )
```
